32 devices in a mesh: batch: 16 (over z, x, core), mp: 2 (over y).
Axes of the slice: x: 2, y: 2, z: 4, core: 2. Of those that a mesh axis runs over, the one named last changes fastest.
Arguments:
- hidden_in: bfloat16 [18432, 768], P('batch'), may hold values from -6 to 6
- cotangent: bfloat16 [18432, 768], P('batch'), may hold values from -6 to 6
- valid: int32 [64], P('batch'), may hold values from 0 to 1, as said below
- answers: int32 [64, 2], P('batch'), may hold values from 0 to 287, as said below
- query_embed: float32 [8, 128], replicated, may hold values from -1 to 1
- w_qkv: bfloat16 [3, 768, 768], P(None, None, 'mp'), may hold values from -0.21875 to 0.21875
- b_qv: float32 [2, 768], P(None, 'mp'), may hold values from -3 to 3
- w_out: bfloat16 [768, 768], P('mp'), may hold values from -0.875 to 0.875
- b_out: float32 [768], replicated, may hold values from -2 to 2
- gain_attn: float32 [768], replicated, may hold values from 0.5 to 1.5
- shift_attn: float32 [768], replicated, may hold values from -2 to 2
- w_in: bfloat16 [768, 3072], P(None, 'mp'), may hold values from -0.21875 to 0.21875
- b_in: float32 [3072], P('mp'), may hold values from -3 to 3
- w_down: bfloat16 [3072, 768], P('mp'), may hold values from -0.109375 to 0.109375
- b_down: float32 [768], replicated, may hold values from -2 to 2
- gain_ffn: float32 [768], replicated, may hold values from 0.5 to 1.5
- shift_ffn: float32 [768], replicated, may hold values from -2 to 2
- w_ret: float32 [768, 128], replicated, may hold values from -0.21875 to 0.21875
- w_span: float32 [768, 2], replicated, may hold values from -0.21875 to 0.21875
Outputs:
- mll: float32 [8], replicated
- layer_out: bfloat16 [18432, 768], P('batch')
- grad_in: float32 [18432, 768], P('batch')
- grad_w_qkv: float32 [3, 768, 768], P(None, 'batch', 'mp')
- grad_b_qv: float32 [2, 768], P(None, ('mp', 'batch'))
- grad_w_out: float32 [768, 768], P('mp', 'batch')
- grad_b_out: float32 [768], P('batch')
- grad_gain_attn: float32 [768], P('batch')
- grad_shift_attn: float32 [768], P('batch')
- grad_w_in: float32 [768, 3072], P('batch', 'mp')
- grad_b_in: float32 [3072], P(('mp', 'batch'))
- grad_w_down: float32 [3072, 768], P('mp', 'batch')
- grad_b_down: float32 [768], P('batch')
- grad_gain_ffn: float32 [768], P('batch')
- grad_shift_ffn: float32 [768], P('batch')
- grad_w_ret: float32 [768, 128], P('batch')
- grad_w_span: float32 [768, 2], P('batch')
The draws below stay inside these ranges and needn't reach their ends.
Inputs may be any that keep to these rules, and one draw needn't show every extreme that they name: `valid`: each query's 8 entries hold 4 to 8 ones; some query has exactly 4 and some has 8. `answers`: in each slot start <= end <= start + 8; some slot starts at 0 and some ends at 287.
All inputs are finite; a program needn't handle non-finite values.
Results may differ from the reference program's by a relative error of at most 0.013.
The reference program's roundings to bfloat16 on the way count: a program that leaves them out, or rounds other values in their place, can miss the bound.
Values sent between devices are 32-bit elements; how exact they have to be, the bound alone decides.
No kernel may reach another device: no remote copies, remote signals or barrier semaphores. Data moves between devices by JAX's collectives and lax.ppermute only.
A program may use at most 192 MiB of HBM per device.

```python
import jax
import jax.numpy as jnp
from jax import lax

D = 768
HEADS = 12
HEAD_DIM = 64
FF = 3072
RET = 128
SEQ = 288
SLOTS = 8
QUERIES = 8
SLOTS_ALL = 64
TOKENS = 18432


def draw_valid(key, part):
    count_key, order_key = jax.random.split(jax.random.fold_in(key, 11))
    counts = jax.random.randint(count_key, (QUERIES,), 4, SLOTS + 1)
    counts = counts.at[0].set(4).at[QUERIES - 1].set(SLOTS)
    order_keys = jax.random.split(order_key, QUERIES)
    ranks = jax.vmap(lambda k: jax.random.permutation(k, SLOTS))(order_keys)
    return (ranks < counts[:, None]).astype(jnp.int32).reshape(SLOTS_ALL)


def draw_answers(key, part):
    start_key, width_key = jax.random.split(jax.random.fold_in(key, 23))
    start = jax.random.randint(start_key, (SLOTS_ALL,), 0, SEQ)
    width = jax.random.randint(width_key, (SLOTS_ALL,), 0, 9)
    end = jnp.minimum(start + width, SEQ - 1)
    start = start.at[0].set(0)
    end = end.at[0].set(jnp.minimum(width[0], SEQ - 1))
    end = end.at[1].set(SEQ - 1)
    start = start.at[1].set(jnp.maximum(SEQ - 1 - width[1], 0))
    return jnp.stack([start, end], -1).astype(jnp.int32)


def strengthened(result, stream_key, source, target, parts, factor):
    def block_of(position):
        return (jnp.arange(result.shape[position]) // (result.shape[position] // parts)).reshape((-1,) + (1,) * (result.ndim - 1 - position))

    near = jax.random.permutation(stream_key, parts)[block_of(target)]
    other_side = (block_of(target) + parts // 2) % parts
    return jnp.where((block_of(source) == near) | (block_of(source) == other_side), factor * result, result)


def shard_levels(own_key, extent, pieces, low, top_value):
    def one(position, shards_of):
        draws = jax.random.uniform(jax.random.fold_in(jax.random.fold_in(own_key, 6), position), (shards_of,), jnp.float32, low / len(pieces), top_value / len(pieces))
        return jnp.repeat(jnp.exp(draws), extent[position] // shards_of).reshape((-1,) + (1,) * (len(extent) - position - 1))

    factor_of = one(*pieces[0])
    for cut in pieces[1:]:
        factor_of = factor_of * one(*cut)
    return factor_of


def centred(stream_key, shape, deviation, bound, cuts=(), dtype=jnp.bfloat16):
    values = deviation * jax.random.normal(stream_key, shape, jnp.float32)
    if cuts:
        values = values * shard_levels(stream_key, shape, cuts, -0.22, 0.18)
    return jnp.clip(values, -bound, bound).astype(dtype)


def heavy_noise(stream_key, shape, deviation, limit, cuts, heavy, held_as=jnp.bfloat16):
    result = deviation * jax.random.normal(stream_key, shape, jnp.float32)
    if cuts:
        result = result * shard_levels(stream_key, shape, cuts, -0.22, 0.18)
    return jnp.clip(strengthened(result, jax.random.fold_in(stream_key, 3), *heavy), -limit, limit).astype(held_as)


def setup_inputs(seed: int = 0) -> dict:
    arg_keys = jax.random.split(jax.random.key(seed), 20)
    return {
        "hidden_in": heavy_noise(arg_keys[0], (TOKENS, D), 1.0, 6.0, ((0, 16),), (0, 1, 16, 2.0)),
        "cotangent": heavy_noise(arg_keys[1], (TOKENS, D), 1.0, 6.0, ((0, 16),), (0, 1, 16, 2.0)),
        "valid": draw_valid(jax.random.fold_in(arg_keys[19], 71), 0),
        "answers": draw_answers(jax.random.fold_in(arg_keys[19], 71), 0),
        "query_embed": centred(arg_keys[4], (QUERIES, RET), 0.15, 1.0, (), jnp.float32),
        "w_qkv": centred(arg_keys[5], (3, D, D), D ** -0.5, 0.21875, ((2, 2),)),
        "b_qv": centred(arg_keys[6], (2, D), 0.5, 3.0, ((1, 2),), jnp.float32),
        "w_out": centred(arg_keys[7], (D, D), (D // 16) ** -0.5, 0.875, ((0, 2),)),
        "b_out": centred(arg_keys[8], (D,), 0.3, 2.0, (), jnp.float32),
        "gain_attn": jnp.clip(1.0 + 0.1 * jax.random.normal(arg_keys[9], (D,), jnp.float32), 0.5, 1.5),
        "shift_attn": centred(arg_keys[10], (D,), 0.3, 2.0, (), jnp.float32),
        "w_in": centred(arg_keys[11], (D, FF), D ** -0.5, 0.21875, ((1, 2),)),
        "b_in": centred(arg_keys[12], (FF,), 0.5, 3.0, ((0, 2),), jnp.float32),
        "w_down": centred(arg_keys[13], (FF, D), FF ** -0.5, 0.109375, ((0, 2),)),
        "b_down": centred(arg_keys[14], (D,), 0.3, 2.0, (), jnp.float32),
        "gain_ffn": jnp.clip(1.0 + 0.1 * jax.random.normal(arg_keys[15], (D,), jnp.float32), 0.5, 1.5),
        "shift_ffn": centred(arg_keys[16], (D,), 0.3, 2.0, (), jnp.float32),
        "w_ret": centred(arg_keys[17], (D, RET), D ** -0.5, 0.21875, (), jnp.float32),
        "w_span": centred(arg_keys[18], (D, 2), D ** -0.5, 0.21875, (), jnp.float32),
    }


@jax.custom_vjp
def low(v):
    return lax.optimization_barrier(v.astype(jnp.bfloat16)).astype(jnp.float32)

@jax.custom_vjp
def low_back(v):
    return v

def low_keep(v):
    return (low(v), None)

def low_pass(kept, grad):
    return (grad,)

def back_keep(v):
    return (v, None)

def back_low(kept, grad):
    return (low(grad),)
low.defvjp(low_keep, low_pass)
low_back.defvjp(back_keep, back_low)
eps = 1e-05
floor_value = -1e+30

def mult(a, b):
    return jnp.dot(a, b, precision=lax.Precision.HIGHEST, preferred_element_type=jnp.float32)

def layer_norm(v, gain, shift):
    centre = v - lax.optimization_barrier(jnp.mean(v, -1, keepdims=True))
    return centre * lax.rsqrt(lax.optimization_barrier(jnp.mean(centre * centre, -1, keepdims=True)) + eps) * gain + shift

def query_layer(x_block, v_block, a_block, q_vec, params):
    w_qkv, b_qv, w_out, b_out, gain_attn, shift_attn, w_in, b_in, w_down, b_down, gain_ffn, shift_ffn, w_ret, w_span = params
    hi = lax.Precision.HIGHEST
    query = low(low_back(mult(x_block, w_qkv[0]) + b_qv[0]))
    keys = low(low_back(mult(x_block, w_qkv[1])))
    values = low(low_back(mult(x_block, w_qkv[2]) + b_qv[1]))
    shape4 = (SLOTS, SEQ, HEADS, HEAD_DIM)
    raw = jnp.einsum('bqhd,bkhd->bhqk', query.reshape(shape4), keys.reshape(shape4), precision=hi)
    scores = low_back(raw) * HEAD_DIM ** (-0.5)
    probs = low(jax.nn.softmax(scores, axis=-1))
    context = jnp.einsum('bhqk,bkhd->bqhd', probs, values.reshape(shape4), precision=hi)
    context = low(low_back(context.reshape(SLOTS * SEQ, D)))
    mixed = x_block + low_back(mult(context, w_out)) + b_out
    first = layer_norm(mixed, gain_attn, shift_attn)
    inner = low_back(mult(low(first), w_in) + b_in)
    act = low(jax.nn.gelu(inner, approximate=False))
    second = layer_norm(first + low_back(mult(act, w_down)) + b_down, gain_ffn, shift_ffn)
    lead = second.reshape(SLOTS, SEQ, D)[:, 0, :]
    retrieval = lax.optimization_barrier(jnp.sum(mult(lead, w_ret) * q_vec[None, :], -1))
    logits = mult(second, w_span).reshape(SLOTS, SEQ, 2)
    log_probs = jax.nn.log_softmax(logits, axis=1)
    marks = (jnp.arange(SEQ)[None, :, None] == a_block[:, None, :]).astype(jnp.float32)
    span = lax.optimization_barrier(jnp.sum(log_probs * marks, axis=(1, 2)))
    live = v_block > 0
    joint = jnp.where(live, retrieval + span, floor_value)
    prior = jnp.where(live, retrieval, floor_value)
    mll = jax.scipy.special.logsumexp(joint) - jax.scipy.special.logsumexp(prior)
    return (second, mll)

def reference(hidden_in, cotangent, valid, answers, query_embed, w_qkv, b_qv, w_out, b_out, gain_attn, shift_attn, w_in, b_in, w_down, b_down, gain_ffn, shift_ffn, w_ret, w_span):
    params = tuple((p.astype(jnp.float32) for p in (w_qkv, b_qv, w_out, b_out, gain_attn, shift_attn, w_in, b_in, w_down, b_down, gain_ffn, shift_ffn, w_ret, w_span)))
    inputs = hidden_in.astype(jnp.float32).reshape(QUERIES, SLOTS * SEQ, D)
    blocks_valid = valid.reshape(QUERIES, SLOTS)
    blocks_answers = answers.reshape(QUERIES, SLOTS, 2)
    q_table = query_embed.astype(jnp.float32)

    def whole(inputs, params):

        def one(block):
            return query_layer(block[0], block[1], block[2], block[3], params)
        return lax.map(jax.checkpoint(one), (inputs, blocks_valid, blocks_answers, q_table))
    (second, mll), pull = jax.vjp(whole, inputs, params)
    upstream = (cotangent.astype(jnp.float32).reshape(QUERIES, SLOTS * SEQ, D), -jnp.ones((QUERIES,), jnp.float32))
    grad_in, grads = pull(upstream)
    return (mll, second.reshape(TOKENS, D).astype(jnp.bfloat16), grad_in.reshape(TOKENS, D), grads[0], grads[1], grads[2], grads[3], grads[4], grads[5], grads[6], grads[7], grads[8], grads[9], grads[10], grads[11], grads[12], grads[13])
```

```python
import functools

import jax
import jax.numpy as jnp
from jax import lax
from jax.experimental import pallas as pl
from jax.experimental.pallas import tpu as pltpu
from jax.sharding import PartitionSpec as P

HEAD_DIM = 64
SEQ = 288
SLOTS = 8
BLOCKS = 16
CORE, X, Z0, Z1 = 1, 2, 4, 8
EPS = 1e-05
FLOOR = -1e30
F32 = jnp.float32
BF16 = jnp.bfloat16
HIGHEST = lax.Precision.HIGHEST


def across(v, mask):
    n = lax.axis_size("batch")
    return lax.ppermute(v, "batch", [(i, i ^ mask) for i in range(n)])


def over_y(v):
    return lax.ppermute(v, "mp", [(0, 1), (1, 0)])


def bit_mask(bit):
    return bit * (lax.axis_size("batch") // BLOCKS)


def assemble_kernel(order, me_ref, *refs):
    out_ref = refs[-1]
    rows = out_ref.shape[0] // 8
    piece = 0
    for ref in refs[:-1]:
        for k in range(ref.shape[0] // rows):
            start = pl.multiple_of((order[piece] ^ me_ref[0]) * rows, rows)
            out_ref[pl.ds(start, rows), :] = ref[pl.ds(k * rows, rows), :].astype(BF16)
            piece += 1


def assemble(parts, order, me):
    rows = sum(p.shape[0] for p in parts)
    return pl.pallas_call(
        functools.partial(assemble_kernel, order),
        out_shape=jax.ShapeDtypeStruct((rows, parts[0].shape[1]), BF16),
        in_specs=[pl.BlockSpec(memory_space=pltpu.SMEM)]
        + [pl.BlockSpec(memory_space=pltpu.VMEM)] * len(parts),
        out_specs=pl.BlockSpec(memory_space=pltpu.VMEM),
        compiler_params=pltpu.CompilerParams(vmem_limit_bytes=50 * 2**20),
    )((me & 7).reshape(1), *parts)


def other_half(w, bits, me):
    rows = w.shape[0] // 8
    mine = lax.dynamic_slice_in_dim(w, (me & 7) * rows, rows, 0).astype(F32)
    parts = [over_y(mine)]
    order = [0]
    for bit in bits:
        held = parts[0] if len(parts) == 1 else jnp.concatenate(parts)
        parts = [held, across(held, bit_mask(bit))]
        order = order + [r | bit for r in order]
    return assemble(parts, tuple(order), me)


def place_kernel(y_ref, mine_ref, theirs_ref, out_ref):
    rows = mine_ref.shape[0]
    at = pl.multiple_of(y_ref[0] * rows, rows)
    out_ref[pl.ds(at, rows), :] = mine_ref[...].astype(out_ref.dtype)
    at = pl.multiple_of((1 - y_ref[0]) * rows, rows)
    out_ref[pl.ds(at, rows), :] = theirs_ref[...].astype(out_ref.dtype)


def place(mine, theirs, y, dtype):
    rows, width = mine.shape
    return pl.pallas_call(
        place_kernel,
        out_shape=jax.ShapeDtypeStruct((2 * rows, width), dtype),
        in_specs=[pl.BlockSpec(memory_space=pltpu.SMEM)]
        + [pl.BlockSpec(memory_space=pltpu.VMEM)] * 2,
        out_specs=pl.BlockSpec(memory_space=pltpu.VMEM),
        compiler_params=pltpu.CompilerParams(vmem_limit_bytes=50 * 2**20),
    )(y.reshape(1), mine, theirs)


def row_order(bits):
    order = []
    for p in range(BLOCKS):
        r = 0
        for k, bit in enumerate(bits):
            if (p >> (len(bits) - 1 - k)) & 1:
                r |= bit
        order.append(r)
    return order


def relative_rows(a, bits, me):
    width = a.shape[1]
    t = a.T.reshape(BLOCKS, width // BLOCKS, a.shape[0])
    index = jnp.array(row_order(bits), jnp.int32) ^ me
    return jnp.take(t, index, axis=0).reshape(width, a.shape[0])


def reduce_scatter(own, other, steps):
    for step in steps:
        if step == "y":
            own, other = own + over_y(other), None
        else:
            half = own.shape[0] // 2
            mask = bit_mask(step)
            own = own[:half] + across(own[half:], mask)
            if other is not None:
                other = other[:half] + across(other[half:], mask)
    rest = lax.axis_size("batch") // BLOCKS
    if rest > 1:
        groups = [[g * rest + k for k in range(rest)] for g in range(BLOCKS)]
        own = lax.psum_scatter(
            own, "batch", scatter_dimension=0, axis_index_groups=groups, tiled=True
        )
    return own


def total(v, y_part):
    own, other = y_part
    n = v.shape[0]
    both = jnp.concatenate([v, own]) + over_y(jnp.concatenate([v, other]))
    mask = 1
    while mask < lax.axis_size("batch"):
        both = both + across(both, mask)
        mask *= 2
    return both[:n], both[n:]


def layer_norm(v, gain, shift):
    centre = v - jnp.mean(v, -1, keepdims=True)
    inverse = lax.rsqrt(jnp.mean(centre * centre, -1, keepdims=True) + EPS)
    normed = centre * inverse
    return (normed * gain + shift, normed, inverse)


def norm_back(grad, normed, inverse, gain):
    grad_gain = jnp.sum(grad * normed, 0)
    grad_shift = jnp.sum(grad, 0)
    scaled = grad * gain
    grad_input = inverse * (
        scaled
        - jnp.mean(scaled, -1, keepdims=True)
        - normed * jnp.mean(scaled * normed, -1, keepdims=True)
    )
    return (grad_input, grad_gain, grad_shift)


def attention(x, w, b, w_out):
    rows = x.shape[0]
    slots = rows // SEQ
    local = w.shape[2]
    shape4 = (slots, SEQ, local // HEAD_DIM, HEAD_DIM)
    proj = jnp.einsum("rd,cde->cre", x, w, preferred_element_type=F32)
    q = (proj[0] + b[0]).astype(BF16)
    k = proj[1].astype(BF16)
    v = (proj[2] + b[1]).astype(BF16)
    scores = jnp.einsum(
        "bqhd,bkhd->bhqk", q.reshape(shape4), k.reshape(shape4), preferred_element_type=F32
    ) * HEAD_DIM ** (-0.5)
    lse = jax.nn.logsumexp(scores, axis=-1, keepdims=True)
    probs = jnp.exp(scores - lse).astype(BF16)
    context = jnp.einsum(
        "bhqk,bkhd->bqhd", probs, v.reshape(shape4), preferred_element_type=F32
    )
    context = context.reshape(rows, local).astype(BF16)
    return q, k, v, lse, context, jnp.dot(context, w_out, preferred_element_type=F32)


def attention_back(x, w, q, k, v, lse, d_context, x_rel):
    rows = x.shape[0]
    slots = rows // SEQ
    local = w.shape[2]
    shape4 = (slots, SEQ, local // HEAD_DIM, HEAD_DIM)
    q4, k4, v4, dc4 = (a.reshape(shape4) for a in (q, k, v, d_context))
    scale = HEAD_DIM ** (-0.5)
    scores = jnp.einsum("bqhd,bkhd->bhqk", q4, k4, preferred_element_type=F32) * scale
    probs = jnp.exp(scores - lse)
    d_v = jnp.einsum("bhqk,bqhd->bkhd", probs.astype(BF16), dc4, preferred_element_type=F32)
    d_probs = jnp.einsum("bqhd,bkhd->bhqk", dc4, v4, preferred_element_type=F32)
    centre = jnp.sum(d_probs * probs, -1, keepdims=True)
    d_scores = (probs * (d_probs - centre) * scale).astype(BF16)
    d_q = jnp.einsum("bhqk,bkhd->bqhd", d_scores, k4, preferred_element_type=F32)
    d_k = jnp.einsum("bhqk,bqhd->bkhd", d_scores, q4, preferred_element_type=F32)
    d_q, d_k, d_v = (a.reshape(rows, local).astype(BF16) for a in (d_q, d_k, d_v))
    sums = jnp.concatenate([jnp.sum(d_q.astype(F32), 0), jnp.sum(d_v.astype(F32), 0)])
    grads = [jnp.dot(x_rel, d, preferred_element_type=F32) for d in (d_q, d_k, d_v)]
    part = sum(
        jnp.dot(d, w[c].T, preferred_element_type=F32) for c, d in enumerate((d_q, d_k, d_v))
    )
    return sums, jnp.concatenate(grads, 1), part


def merge(a, b):
    peak = jnp.maximum(a[0], b[0])
    return peak, a[1] * jnp.exp(a[0] - peak) + b[1] * jnp.exp(b[0] - peak)


def on_device(
    hidden_in,
    cotangent,
    valid,
    answers,
    query_embed,
    w_qkv,
    b_qv,
    w_out,
    b_out,
    gain_attn,
    shift_attn,
    w_in,
    b_in,
    w_down,
    b_down,
    gain_ffn,
    shift_ffn,
    w_ret,
    w_span,
):
    here = lax.axis_index("batch")
    y = lax.axis_index("mp")
    me = here // (lax.axis_size("batch") // BLOCKS)
    width = hidden_in.shape[1]
    rows = hidden_in.shape[0] // 2
    slots = rows // SEQ
    slots_here = 2 * slots
    per_query = SLOTS // slots_here
    n_queries = query_embed.shape[0]

    cols = w_qkv.shape[2]
    w_qkv2 = other_half(w_qkv.reshape(-1, cols), (Z0, X, CORE), me).reshape(w_qkv.shape)
    w_out2 = other_half(w_out, (X, Z0, CORE), me)
    w_in2 = other_half(w_in, (Z0, X, CORE), me)
    w_down2 = other_half(w_down, (X, Z0, CORE), me)
    biases = over_y(jnp.concatenate([b_qv.reshape(-1), b_in]))
    b_qv2 = biases[: b_qv.size].reshape(b_qv.shape)
    b_in2 = biases[b_qv.size :]

    x = lax.dynamic_slice_in_dim(hidden_in, y * rows, rows, 0)
    cot = lax.dynamic_slice_in_dim(cotangent, y * rows, rows, 0)
    live = lax.dynamic_slice_in_dim(valid, y * slots, slots, 0) > 0
    marked = lax.dynamic_slice_in_dim(answers, y * slots, slots, 0)

    q1, k1, v1, lse1, ctx1, part1 = attention(x, w_qkv, b_qv, w_out)
    q2, k2, v2, lse2, ctx2, part2 = attention(x, w_qkv2, b_qv2, w_out2)
    mixed = x.astype(F32) + (part1 + part2) + b_out
    first, normed_a, inverse_a = layer_norm(mixed, gain_attn, shift_attn)
    first_low = first.astype(BF16)

    def up(w, b):
        inner = jnp.dot(first_low, w, preferred_element_type=F32) + b
        return inner, jax.nn.gelu(inner, approximate=False).astype(BF16)

    inner1, act1 = up(w_in, b_in)
    inner2, act2 = up(w_in2, b_in2)
    ffn = jnp.dot(act1, w_down, preferred_element_type=F32) + jnp.dot(
        act2, w_down2, preferred_element_type=F32
    )
    second, normed_f, inverse_f = layer_norm(first + ffn + b_down, gain_ffn, shift_ffn)
    layer_out = place(second, over_y(second), y, BF16)

    query = here // per_query
    q_row = lax.dynamic_slice_in_dim(query_embed, query, 1, 0)
    lead = second.reshape(slots, SEQ, width)[:, 0, :]
    embed = jnp.dot(lead, w_ret, precision=HIGHEST)
    retrieval = jnp.sum(embed * q_row, -1)
    logits = jnp.dot(second, w_span, precision=HIGHEST).reshape(slots, SEQ, 2)
    log_probs = jax.nn.log_softmax(logits, axis=1)
    marks = (jnp.arange(SEQ)[None, :, None] == marked[:, None, :]).astype(F32)
    span = jnp.sum(log_probs * marks, axis=(1, 2))
    table = jnp.where(live, jnp.stack([retrieval + span, retrieval]), FLOOR)
    peak = jnp.max(table, 1)
    sums = jnp.sum(jnp.where(live, jnp.exp(table - peak[:, None]), 0.0), 1)
    stats = jnp.stack([peak, sums])
    stats = jnp.stack(merge(stats, over_y(stats)))
    mask = 1
    while mask < per_query:
        stats = jnp.stack(merge(stats, across(stats, mask)))
        mask *= 2
    lse = stats[0] + jnp.log(stats[1])
    mll_mine = jnp.where(
        (jnp.arange(n_queries) == query) & (y == 0) & (here % per_query == 0), lse[0] - lse[1], 0.0
    )
    post = jnp.where(live, jnp.exp(retrieval + span - lse[0]), 0.0)
    prior = jnp.where(live, jnp.exp(retrieval - lse[1]), 0.0)
    d_retrieval = prior - post
    d_logits = (-post)[:, None, None] * (marks - jnp.exp(log_probs))
    d_logits = d_logits.reshape(rows, 2)
    d_embed = d_retrieval[:, None] * q_row
    d_second = cot.astype(F32) + jnp.dot(d_logits, w_span.T, precision=HIGHEST)
    d_second = (
        d_second.reshape(slots, SEQ, width)
        .at[:, 0, :]
        .add(jnp.dot(d_embed, w_ret.T, precision=HIGHEST))
        .reshape(rows, width)
    )
    g_span = jnp.dot(second.T, d_logits, precision=HIGHEST)
    lead_rel = relative_rows(lead, (CORE, X, Z0, Z1), me)
    g_ret = jnp.dot(lead_rel, d_embed, precision=HIGHEST)

    d_sum, g_gain_ffn, g_shift_ffn = norm_back(d_second, normed_f, inverse_f, gain_ffn)
    g_b_down = jnp.sum(d_sum, 0)
    d_ffn = d_sum.astype(BF16)
    down_steps = (CORE, "y", X, Z0, Z1)
    d_ffn_rel = relative_rows(d_ffn, (CORE, X, Z0, Z1), me)
    g_w_down = reduce_scatter(
        jnp.dot(d_ffn_rel, act1, preferred_element_type=F32),
        jnp.dot(d_ffn_rel, act2, preferred_element_type=F32),
        down_steps,
    )

    def down_back(inner, w):
        d_act = jnp.dot(d_ffn, w.T, preferred_element_type=F32)
        return jax.vjp(lambda v: jax.nn.gelu(v, approximate=False), inner)[1](d_act)[0].astype(BF16)

    d_inner1 = down_back(inner1, w_down)
    d_inner2 = down_back(inner2, w_down2)
    g_b_in = (jnp.sum(d_inner1.astype(F32), 0), jnp.sum(d_inner2.astype(F32), 0))
    first_rel = relative_rows(first_low, (CORE, X, Z0, Z1), me)
    g_w_in = reduce_scatter(
        jnp.concatenate([jnp.dot(first_rel, d_inner1, preferred_element_type=F32), g_ret], 1),
        jnp.concatenate([jnp.dot(first_rel, d_inner2, preferred_element_type=F32), g_ret], 1),
        (CORE, X, Z0, Z1, "y"),
    )
    d_first = d_sum + (
        jnp.dot(d_inner1, w_in.T, preferred_element_type=F32)
        + jnp.dot(d_inner2, w_in2.T, preferred_element_type=F32)
    )

    d_mixed, g_gain_attn, g_shift_attn = norm_back(d_first, normed_a, inverse_a, gain_attn)
    g_b_out = jnp.sum(d_mixed, 0)
    d_att = d_mixed.astype(BF16)
    late = (CORE, Z0, X, Z1)
    d_att_rel = relative_rows(d_att, late, me)
    x_rel = relative_rows(x, late, me)
    g_w_out = reduce_scatter(
        jnp.dot(d_att_rel, ctx1, preferred_element_type=F32),
        jnp.dot(d_att_rel, ctx2, preferred_element_type=F32),
        late + ("y",),
    )
    d_ctx1 = jnp.dot(d_att, w_out.T, preferred_element_type=F32).astype(BF16)
    d_ctx2 = jnp.dot(d_att, w_out2.T, preferred_element_type=F32).astype(BF16)
    s1, g1, in1 = attention_back(x, w_qkv, q1, k1, v1, lse1, d_ctx1, x_rel)
    s2, g2, in2 = attention_back(x, w_qkv2, q2, k2, v2, lse2, d_ctx2, x_rel)
    g_w_qkv = reduce_scatter(g1, g2, late + ("y",))
    g_in = d_mixed + (in1 + in2)
    grad_in = place(g_in, over_y(g_in), y, F32)

    common = [g_b_out, g_gain_attn, g_shift_attn, g_b_down, g_gain_ffn, g_shift_ffn]
    common = jnp.concatenate(common + [g_span[:, 0], g_span[:, 1], mll_mine])
    common, own = total(
        common, (jnp.concatenate([s1, g_b_in[0]]), jnp.concatenate([s2, g_b_in[1]]))
    )
    few = width // lax.axis_size("batch")
    vectors = [
        lax.dynamic_slice_in_dim(common, k * width + here * few, few, 0) for k in range(8)
    ]
    mll = common[8 * width :]
    few_q = cols // lax.axis_size("batch")
    few_i = b_in.shape[0] // lax.axis_size("batch")
    g_b_qv = jnp.stack(
        [lax.dynamic_slice_in_dim(own, k * cols + here * few_q, few_q, 0) for k in range(2)]
    )
    g_b_in = lax.dynamic_slice_in_dim(own, 2 * cols + here * few_i, few_i, 0)
    half = w_in.shape[1]
    return (
        mll,
        layer_out,
        grad_in,
        jnp.stack([g_w_qkv[:, c * cols : (c + 1) * cols] for c in range(3)]),
        g_b_qv,
        g_w_out.T,
        vectors[0],
        vectors[1],
        vectors[2],
        g_w_in[:, :half],
        g_b_in,
        g_w_down.T,
        vectors[3],
        vectors[4],
        vectors[5],
        g_w_in[:, half:],
        jnp.stack([vectors[6], vectors[7]], 1),
    )


def solution(mesh):
    return jax.shard_map(
        on_device,
        mesh=mesh,
        in_specs=(
            P("batch", None),
            P("batch", None),
            P("batch"),
            P("batch", None),
            P(),
            P(None, None, "mp"),
            P(None, "mp"),
            P("mp", None),
            P(),
            P(),
            P(),
            P(None, "mp"),
            P("mp"),
            P("mp", None),
            P(),
            P(),
            P(),
            P(),
            P(),
        ),
        out_specs=(
            P(),
            P("batch", None),
            P("batch", None),
            P(None, "batch", "mp"),
            P(None, ("mp", "batch")),
            P("mp", "batch"),
            P("batch"),
            P("batch"),
            P("batch"),
            P("batch", "mp"),
            P(("mp", "batch")),
            P("mp", "batch"),
            P("batch"),
            P("batch"),
            P("batch"),
            P("batch", None),
            P("batch", None),
        ),
        check_vma=False,
    )
```

```python
import functools

import jax
import jax.numpy as jnp
from jax import lax
from jax.experimental import pallas as pl
from jax.experimental.pallas import tpu as pltpu
from jax.sharding import PartitionSpec as P

HEAD_DIM = 64
PAIR = 2 * HEAD_DIM
SEQ = 288
SLOTS = 8
BLOCKS = 16
CORE, X, Z0, Z1 = 1, 2, 4, 8
EPS = 1e-05
FLOOR = -1e30
F32 = jnp.float32
BF16 = jnp.bfloat16
HIGHEST = lax.Precision.HIGHEST
LIMIT = 16
X_FIRST = (CORE, X, Z0, Z1)
Z_FIRST = (CORE, Z0, X, Z1)
SCALE = HEAD_DIM ** (-0.5)
HALF, OTHER, ALL = 0, 1, 2

VMEM = pl.BlockSpec(memory_space=pltpu.VMEM)
SMEM = pl.BlockSpec(memory_space=pltpu.SMEM)


def across(v, mask):
    n = lax.axis_size("batch")
    return lax.ppermute(v, "batch", [(i, i ^ mask) for i in range(n)])


def over_y(v):
    return lax.ppermute(v, "mp", [(0, 1), (1, 0)])


def bit_mask(bit):
    return bit * (lax.axis_size("batch") // BLOCKS)


def shape(dims, dtype=F32):
    return jax.ShapeDtypeStruct(dims, dtype)


def cost(flops, moved, exps=0):
    return pl.CostEstimate(flops=int(flops), bytes_accessed=int(moved), transcendentals=int(exps))


class Line:
    def __init__(self, pos):
        self.pos = pos
        self.last = []
        self.token = pos

    def after(self, *arrays):
        self.last = self.last + list(arrays)
        self.token = arrays[-1]

    def here(self, array):
        return lax.optimization_barrier((array, self.token))[0]

    def run(self, kernel, outs, args, specs=None, scratch=(), work=(0, 0, 0)):
        n, extra = len(args), self.last
        params = pltpu.CompilerParams(vmem_limit_bytes=LIMIT * 2**20)

        def body(pos, *refs):
            kernel(pos, *refs[:n], *refs[n + len(extra) :])

        unread = [pl.BlockSpec(memory_space=pl.ANY)] * len(extra)
        if specs is None:
            small = [SMEM if a.dtype == jnp.int32 else VMEM for a in args]
            how = {
                "in_specs": [SMEM] + small + unread,
                "out_specs": (VMEM,) * len(outs),
                "scratch_shapes": list(scratch),
            }
        else:
            how = {
                "grid_spec": pltpu.PrefetchScalarGridSpec(
                    num_scalar_prefetch=1,
                    grid=(1,),
                    in_specs=[whole(a) if spec is None else spec for a, spec in zip(args, specs)]
                    + unread,
                    out_specs=tuple(whole(o) for o in outs),
                    scratch_shapes=list(scratch),
                )
            }
        results = pl.pallas_call(
            body,
            out_shape=tuple(outs),
            compiler_params=params,
            cost_estimate=cost(1e11, 1e8),
            **how,
        )(self.pos, *args, *extra)
        self.last = [min(results, key=lambda r: r.size)]
        self.token = self.last[0]
        return results


def whole(a):
    return pl.BlockSpec(a.shape, lambda *_: (0,) * len(a.shape))


def dot(a, b, precision=None):
    return jnp.dot(a, b, precision=precision, preferred_element_type=F32)


def dot_nt(a, b, precision=None):
    return lax.dot_general(
        a, b, (((1,), (1,)), ((), ())), precision=precision, preferred_element_type=F32
    )


def dot_tn(a, b):
    return lax.dot_general(a, b, (((0,), (0,)), ((), ())), preferred_element_type=F32)


def pack_attn_kernel(pos, qkv_ref, out_ref, bqv_ref, bin_ref, a_ref):
    n, cols = qkv_ref.shape
    m = out_ref.shape[0]
    a_ref[:n, :] = qkv_ref[...].astype(F32)
    a_ref[n : n + m, :] = out_ref[:, :cols].astype(F32)
    a_ref[n + m : n + 2 * m, :] = out_ref[:, cols:].astype(F32)
    at = n + 2 * m
    a_ref[at : at + 8, :] = jnp.zeros((8, cols), F32)
    a_ref[at : at + 2, :] = bqv_ref[...]
    for k in range(bin_ref.shape[1] // cols):
        a_ref[at + 2 + k : at + 3 + k, :] = bin_ref[:, k * cols : (k + 1) * cols]


def eighth_of(w, place):
    return pl.BlockSpec((w.shape[0] // 8, w.shape[1]), lambda i, pos: (pos[place], 0))


def pack_attn(line, qkv, w_out, b_qv, b_in, place):
    rows = qkv.shape[0] // 8 + w_out.shape[0] // 4 + 8
    specs = [eighth_of(qkv, place), eighth_of(w_out, place), None, None]
    outs = [shape((rows, qkv.shape[1]))]
    return line.run(pack_attn_kernel, outs, (qkv, w_out, b_qv, b_in), specs)[0]


def pack_in_kernel(pos, in_ref, b_ref):
    r, wide = in_ref.shape[0], b_ref.shape[1]
    b_ref[:r, :] = in_ref[:, :wide].astype(F32)
    b_ref[r:, :] = in_ref[:, wide:].astype(F32)


def pack_in(line, w, place):
    outs = [shape((w.shape[0] // 4, w.shape[1] // 2))]
    return line.run(pack_in_kernel, outs, (w,), [eighth_of(w, place)])[0]


def pack_down_kernel(pos, down_ref, c_ref):
    c_ref[...] = down_ref[...].astype(F32)


def pack_down(line, w, place):
    outs = [shape((w.shape[0] // 8, w.shape[1]))]
    return line.run(pack_down_kernel, outs, (w,), [eighth_of(w, place)])[0]


def unpack_attn_kernel(order, pos, *refs):
    qkv_ref, out_ref, bqv_ref, bin_ref = refs[-4:]
    n, m = qkv_ref.shape[0] // 8, out_ref.shape[0] // 8
    cols = qkv_ref.shape[1]
    for r, ref in zip(order, refs[:-4]):
        place = r ^ pos[2]
        to = pl.ds(pl.multiple_of(place * n, 16), n)
        qkv_ref[to, :] = ref[:n, :].astype(BF16)
        to = pl.ds(pl.multiple_of(place * m, 16), m)
        out_ref[to, :cols] = ref[n : n + m, :].astype(BF16)
        out_ref[to, cols:] = ref[n + m : n + 2 * m, :].astype(BF16)
    first = refs[0]
    at = n + 2 * m
    bqv_ref[...] = first[at : at + 2, :]
    for k in range(bin_ref.shape[1] // cols):
        bin_ref[:, k * cols : (k + 1) * cols] = first[at + 2 + k : at + 3 + k, :]


def unpack_in_kernel(order, pos, *refs):
    in_ref = refs[-1]
    n = in_ref.shape[0] // 8
    wide = in_ref.shape[1] // 2
    for r, ref in zip(order, refs[:-1]):
        to = pl.ds(pl.multiple_of((r ^ pos[2]) * n, 16), n)
        in_ref[to, :wide] = ref[:n, :].astype(BF16)
        in_ref[to, wide:] = ref[n:, :].astype(BF16)


def unpack_down_kernel(order, pos, *refs):
    down_ref = refs[-1]
    m = down_ref.shape[0] // 8
    for r, ref in zip(order, refs[:-1]):
        to = pl.ds(pl.multiple_of((r ^ pos[2]) * m, 16), m)
        down_ref[to, :] = ref[...].astype(BF16)


def with_core(parts, order):
    return parts + [across(p, bit_mask(CORE)) for p in parts], order + [r | CORE for r in order]


def place_kernel(pos, mine_ref, theirs_ref, out_ref):
    rows = mine_ref.shape[0]
    at = pl.multiple_of(pos[0] * rows, rows)
    out_ref[pl.ds(at, rows), :] = mine_ref[...].astype(out_ref.dtype)
    at = pl.multiple_of((1 - pos[0]) * rows, rows)
    out_ref[pl.ds(at, rows), :] = theirs_ref[...].astype(out_ref.dtype)


def place(line, mine, theirs, dtype):
    rows, width = mine.shape
    return line.run(place_kernel, [shape((2 * rows, width), dtype)], (mine, theirs))[0]


def row_order(bits):
    order = []
    for p in range(BLOCKS):
        r = 0
        for k, bit in enumerate(bits):
            if (p >> (len(bits) - 1 - k)) & 1:
                r |= bit
        order.append(r)
    return order


def store_relative(a, me, scratch, *places):
    scratch[...] = a.T
    for bits, out_ref in places:
        n = out_ref.shape[0] // BLOCKS
        for p, r in enumerate(row_order(bits)):
            at = pl.multiple_of((r ^ me) * n, 16)
            out_ref[p * n : (p + 1) * n, :] = scratch[pl.ds(at, n), :]


def own_rows(pos, ref):
    rows = ref.shape[0] // 2
    return ref[pl.ds(pl.multiple_of(pos[0] * rows, 16), rows), :]


def summed(terms):
    result = terms[0]
    for t in terms[1:]:
        result = result + t
    return result


class Arrival:
    def __init__(self, line, array):
        self.line, self.array, self.waited = line, array, False

    def get(self):
        if not self.waited:
            self.array, self.waited = self.line.here(self.array), True
        return self.array


class Chunk:
    def __init__(self, line, keep, send):
        self.terms = [keep]
        self.n, self.cols = keep.shape[1], keep.shape[2]
        self.heads = keep.shape[0]
        self.pending = (Arrival(line, across(send, bit_mask(CORE))), 0)

    def take(self):
        if self.pending:
            arrival, at = self.pending
            self.terms = self.terms + [arrival.get()[:, :, at : at + self.cols]]
            self.pending = None

    def give(self, what):
        self.take()
        if what == HALF:
            half = self.n // 2
            piece = summed([t[: self.heads, half : self.n] for t in self.terms])
            self.n = half
        elif what == OTHER:
            piece = summed([t[1:2, : self.n] for t in self.terms])
            self.heads = 1
        else:
            piece = summed([t[:1, : self.n] for t in self.terms])
        return piece

    def result(self, *more):
        return summed([t[0, : self.n] for t in [*self.terms, *more]])


def exchange(line, move, what, *chunks):
    pieces = [c.give(what) for c in chunks]
    sent = pieces[0] if len(pieces) == 1 else jnp.concatenate(pieces, 2)
    line.after(sent)
    arrival = Arrival(line, move(sent))
    at = 0
    for c in chunks:
        c.pending = (arrival, at)
        at += c.cols
    return arrival


def over(bit):
    return lambda v: across(v, bit_mask(bit))


def groups_of(rest):
    return [[g * rest + k for k in range(rest)] for g in range(BLOCKS)]


def last_rows(v):
    rest = lax.axis_size("batch") // BLOCKS
    if rest == 1:
        return v
    groups = groups_of(rest)
    return lax.psum_scatter(v, "batch", scatter_dimension=0, axis_index_groups=groups, tiled=True)


def norm(v):
    centre = v - jnp.mean(v, -1, keepdims=True)
    inverse = lax.rsqrt(jnp.mean(centre * centre, -1, keepdims=True) + EPS)
    return centre * inverse, inverse


def norm_back(grad, normed, inverse, gain):
    scaled = grad * gain
    return inverse * (
        scaled
        - jnp.mean(scaled, -1, keepdims=True)
        - normed * jnp.mean(scaled * normed, -1, keepdims=True)
    )


def column_sum(v):
    return jnp.sum(v, 0, keepdims=True)


def head_masks():
    lane = lax.broadcasted_iota(jnp.int32, (1, PAIR), 1)
    first = jnp.where(lane < HEAD_DIM, 1.0, 0.0)
    return lane < HEAD_DIM, (first.astype(BF16), (1.0 - first).astype(BF16))


def attend(x, w_ref, b_ref, wo_ref, q_ref, k_ref, v_ref, ctx_ref):
    q_ref[...] = (dot(x, w_ref[0]) + b_ref[0:1, :]).astype(BF16)
    k_ref[...] = dot(x, w_ref[1]).astype(BF16)
    v_ref[...] = (dot(x, w_ref[2]) + b_ref[1:2, :]).astype(BF16)
    is_first, masks = head_masks()
    for s in range(q_ref.shape[0] // SEQ):
        at = slice(s * SEQ, (s + 1) * SEQ)
        for p in range(q_ref.shape[1] // PAIR):
            lanes = slice(p * PAIR, (p + 1) * PAIR)
            q, k, v = q_ref[at, lanes] * SCALE, k_ref[at, lanes], v_ref[at, lanes]
            results = []
            for mask in masks:
                scores = dot_nt(q * mask, k)
                e = jnp.exp(scores - jnp.max(scores, -1, keepdims=True))
                probs = (e * (1.0 / jnp.sum(e, -1, keepdims=True))).astype(BF16)
                results.append(dot(probs, v))
            ctx_ref[at, lanes] = jnp.where(is_first, *results).astype(BF16)
    return dot(ctx_ref[...], wo_ref[...])


def attend_own_kernel(
    pos, x_ref, w_ref, b_ref, wo_ref, q_ref, k_ref, v_ref, ctx_ref, part_ref, rel1_ref, rel2_ref, scratch
):
    x = own_rows(pos, x_ref)
    store_relative(x, pos[1], scratch, (X_FIRST, rel1_ref), (Z_FIRST, rel2_ref))
    part_ref[...] = attend(x, w_ref, b_ref, wo_ref, q_ref, k_ref, v_ref, ctx_ref)


def attend_other_kernel(
    pos,
    x_ref,
    w_ref,
    b_ref,
    wo_ref,
    part_ref,
    bias_ref,
    gain_ref,
    shift_ref,
    down_ref,
    q_ref,
    k_ref,
    v_ref,
    ctx_ref,
    mixed_ref,
    base_ref,
    low_ref,
    rel1_ref,
    rel2_ref,
    scratch,
):
    x = own_rows(pos, x_ref)
    part = attend(x, w_ref, b_ref, wo_ref, q_ref, k_ref, v_ref, ctx_ref)
    mixed = x.astype(F32) + (part_ref[...] + part) + bias_ref[...]
    mixed_ref[...] = mixed
    first = norm(mixed)[0] * gain_ref[...] + shift_ref[...]
    base_ref[...] = first + down_ref[...]
    low = first.astype(BF16)
    low_ref[...] = low
    store_relative(low, pos[1], scratch, (X_FIRST, rel1_ref), (Z_FIRST, rel2_ref))


def lift(low, w_in_ref, b_ref, act_ref, slope_ref, block):
    for i in range(act_ref.shape[1] // block):
        at = slice(i * block, (i + 1) * block)
        inner = dot(low, w_in_ref[:, at]) + b_ref[:, at]
        cdf = 0.5 + 0.5 * lax.erf(inner * 0.5**0.5)
        density = jnp.exp(-0.5 * inner * inner) * 0.3989422804014327
        act_ref[:, at] = (inner * cdf).astype(BF16)
        slope_ref[:, at] = cdf + inner * density


def up_kernel(block, pos, low_ref, w_in_ref, b_ref, w_down_ref, before_ref, act_ref, slope_ref, sum_ref):
    lift(low_ref[...], w_in_ref, b_ref, act_ref, slope_ref, block)
    sum_ref[...] = before_ref[...] + dot(act_ref[...], w_down_ref[...])


def up_in_kernel(block, pos, low_ref, w_in_ref, b_ref, act_ref, slope_ref):
    lift(low_ref[...], w_in_ref, b_ref, act_ref, slope_ref, block)


def up_down_kernel(pos, act_ref, w_down_ref, before_ref, sum_ref):
    sum_ref[...] = before_ref[...] + dot(act_ref[...], w_down_ref[...])


def loss_kernel(
    pos,
    pre_ref,
    answers,
    valid,
    gain_f,
    shift_f,
    span_ref,
    ret_ref,
    query_ref,
    second_ref,
    marks_ref,
    stats_ref,
):
    second = norm(pre_ref[...])[0] * gain_f[...] + shift_f[...]
    second_ref[...] = second
    q_row = query_ref[pl.ds(pos[3], 1), :]
    row = lax.broadcasted_iota(jnp.int32, (SEQ, 1), 0)
    line = lax.broadcasted_iota(jnp.int32, (8, 128), 0)
    lane = lax.broadcasted_iota(jnp.int32, (8, 128), 1)
    stats = jnp.full((8, 128), FLOOR, F32)
    slots = second.shape[0] // SEQ
    for s in range(slots):
        slot = pos[0] * slots + s
        mine = second[s * SEQ : (s + 1) * SEQ, :]
        span = jnp.zeros((1, 1), F32)
        for c in range(2):
            logits = jnp.sum(mine * span_ref[c : c + 1, :], -1, keepdims=True)
            shifted = logits - jnp.max(logits, 0, keepdims=True)
            log_probs = shifted - jnp.log(jnp.sum(jnp.exp(shifted), 0, keepdims=True))
            mark = jnp.where(row == answers[slot, c], 1.0, 0.0)
            span = span + jnp.sum(log_probs * mark, 0, keepdims=True)
            marks_ref[s * SEQ : (s + 1) * SEQ, c : c + 1] = mark - jnp.exp(log_probs)
        embed = dot(mine[:8, :], ret_ref[...], HIGHEST)[0:1, :]
        retrieval = jnp.sum(embed * q_row, -1, keepdims=True)
        live = valid[slot] > 0
        joint = jnp.where(live, retrieval + span, FLOOR)
        prior = jnp.where(live, retrieval, FLOOR)
        stats = jnp.where((line == s) & (lane == 0), joint, stats)
        stats = jnp.where((line == s) & (lane == 1), prior, stats)
    stats_ref[...] = stats


def loss_back_kernel(n_stats, pos, cot_ref, *refs):
    stats_refs = refs[:n_stats]
    (
        second_ref,
        pre_ref,
        marks_ref,
        gain_f,
        span_ref,
        ret_ref,
        query_ref,
        sum_ref,
        low_ref,
        rel1_ref,
        rel2_ref,
        sent_ref,
        ret_out,
        small_ref,
        mll_ref,
        scratch,
        leads,
    ) = refs[n_stats:]
    all_stats = [ref[...] for ref in stats_refs]
    peak = jnp.max(functools.reduce(jnp.maximum, all_stats), 0, keepdims=True)
    total = jnp.sum(summed([jnp.exp(t - peak) for t in all_stats]), 0, keepdims=True)
    lse = peak + jnp.log(total)
    weight = jnp.exp(all_stats[0] - lse)
    q_row = query_ref[pl.ds(pos[3], 1), :]
    lead_grad = dot_nt(jnp.broadcast_to(q_row, (8, q_row.shape[1])), ret_ref[...], HIGHEST)
    top = lax.broadcasted_iota(jnp.int32, (8, 1), 0) == 0
    rows = cot_ref.shape[0] // 2
    slots = rows // SEQ
    small_ref[...] = jnp.zeros(small_ref.shape, F32)
    embeds = []
    for s in range(slots):
        at = slice(s * SEQ, (s + 1) * SEQ)
        post = weight[s : s + 1, 0:1]
        prior = weight[s : s + 1, 1:2]
        second = second_ref[at, :]
        sent_ref[at, :] = second
        start = pl.multiple_of(pos[0] * rows + s * SEQ, 16)
        grad = cot_ref[pl.ds(start, SEQ), :].astype(F32)
        for c in range(2):
            d_logits = -post * marks_ref[at, c : c + 1]
            grad = grad + d_logits * span_ref[c : c + 1, :]
            small_ref[3 + c : 4 + c, :] += column_sum(second * d_logits)
        sum_ref[at, :] = grad
        sum_ref[s * SEQ : s * SEQ + 8, :] += jnp.where(top, (prior - post) * lead_grad, 0.0)
        small_ref[5 + s : 6 + s, :] = second[0:1, :]
        embeds.append((prior - post) * q_row)
    leads[...] = small_ref[...].T
    n = ret_out.shape[0] // BLOCKS
    for p, r in enumerate(row_order(X_FIRST)):
        block = leads[pl.ds(pl.multiple_of((r ^ pos[1]) * n, 8), n), :]
        ret_out[p * n : (p + 1) * n, :] = summed(
            [block[:, 5 + s : 6 + s] * embed for s, embed in enumerate(embeds)]
        )
    grad = sum_ref[...]
    normed, inverse = norm(pre_ref[...])
    small_ref[0:1, :] = column_sum(grad * normed)
    small_ref[1:2, :] = column_sum(grad)
    d_sum = norm_back(grad, normed, inverse, gain_f[...])
    small_ref[2:3, :] = column_sum(d_sum)
    sum_ref[...] = d_sum
    low = d_sum.astype(BF16)
    low_ref[...] = low
    store_relative(low, pos[1], scratch, (X_FIRST, rel1_ref), (Z_FIRST, rel2_ref))
    lane = lax.broadcasted_iota(jnp.int32, mll_ref.shape, 1)
    mll = lse[:, 0:1] - lse[:, 1:2]
    mll_ref[...] = jnp.where(lane == pos[4], mll, 0.0)


def halves(left_ref, right, keep_ref, send_ref, index):
    half = left_ref.shape[0] // 2
    keep_ref[index] = dot(left_ref[:half, :], right)
    send_ref[index] = dot(left_ref[half:, :], right)


def product_kernel(start, block, pos, left_ref, own_ref, other_ref, *refs):
    *more, keep_ref, send_ref = refs
    at = slice(start, start + block)
    half = keep_ref.shape[1]
    for h, ref in enumerate((own_ref, other_ref)):
        halves(left_ref, ref[:, at], keep_ref, send_ref, (h, slice(None), slice(0, block)))
        for extra in more:
            keep_ref[h, :, block:] = extra[:half, :]
            send_ref[h, :, block:] = extra[half:, :]


def product(line, left, own, other, start, block, *more):
    width = left.shape[0]
    outs = [shape((2, width // 2, block + sum(m.shape[1] for m in more)))] * 2
    kernel = functools.partial(product_kernel, start, block)
    return line.run(kernel, outs, (left, own, other, *more))


def down_back_kernel(
    block, pos, low_ref, rel_ref, wd_ref, wi_ref, slope_ref, before_ref, keep_ref, send_ref, sum_ref, bias_ref, d_ref
):
    low = low_ref[...]
    for i in range(d_ref.shape[1] // block):
        at = slice(i * block, (i + 1) * block)
        d_inner = (dot_nt(low, wd_ref[at, :]) * slope_ref[:, at]).astype(BF16)
        d_ref[:, at] = d_inner
        bias_ref[:, at] = column_sum(d_inner.astype(F32))
        halves(rel_ref, d_inner, keep_ref, send_ref, (0, slice(None), at))
    sum_ref[...] = before_ref[...] + dot_nt(d_ref[...], wi_ref[...])


def down_back(line, low, rel, w_down, w_in, slope, before, block):
    rows, width = low.shape
    hidden = w_in.shape[1]
    return line.run(
        functools.partial(down_back_kernel, block),
        [
            shape((1, width // 2, hidden)),
            shape((1, width // 2, hidden)),
            shape((rows, width)),
            shape((1, hidden)),
        ],
        (low, rel, w_down, w_in, slope, before),
        scratch=[pltpu.VMEM((rows, hidden), BF16)],
    )


def mixed_back_kernel(
    pos, part_ref, mixed_ref, gain_ref, mix_ref, low_ref, rel1_ref, rel2_ref, small_ref, scratch
):
    grad = part_ref[...]
    normed, inverse = norm(mixed_ref[...])
    small_ref[...] = jnp.zeros(small_ref.shape, F32)
    small_ref[1:2, :] = column_sum(grad * normed)
    small_ref[2:3, :] = column_sum(grad)
    d_mixed = norm_back(grad, normed, inverse, gain_ref[...])
    small_ref[0:1, :] = column_sum(d_mixed)
    mix_ref[...] = d_mixed
    low = d_mixed.astype(BF16)
    low_ref[...] = low
    store_relative(low, pos[1], scratch, (X_FIRST, rel1_ref), (Z_FIRST, rel2_ref))


def attend_back_kernel(
    bits,
    pos,
    q_ref,
    k_ref,
    v_ref,
    ctx_ref,
    low_ref,
    low_rel_ref,
    rel_ref,
    w_ref,
    wo_ref,
    before_ref,
    a_ref,
    f_ref,
    bin_ref,
    mll_ref,
    keep_ref,
    send_ref,
    sum_ref,
    d_ref,
    dc_ref,
    blocks,
):
    is_first, masks = head_masks()
    cols = q_ref.shape[1]
    dc_ref[...] = dot_nt(low_ref[...], wo_ref[...]).astype(BF16)
    for s in range(q_ref.shape[0] // SEQ):
        at = slice(s * SEQ, (s + 1) * SEQ)
        for p in range(cols // PAIR):
            lanes = slice(p * PAIR, (p + 1) * PAIR)
            q, k, v, dc = (r[at, lanes] for r in (q_ref, k_ref, v_ref, dc_ref))
            q_low, k_low = q * SCALE, k * SCALE
            d_q, d_k, d_v = [], [], []
            for mask in masks:
                scores = dot_nt(k_low * mask, q)
                e = jnp.exp(scores - jnp.max(scores, 0, keepdims=True))
                probs = e * (1.0 / jnp.sum(e, 0, keepdims=True))
                d_probs = dot_nt(v * mask, dc)
                centre = jnp.sum(d_probs * probs, 0, keepdims=True)
                d_scores = (probs * (d_probs - centre)).astype(BF16)
                d_v.append(dot(probs.astype(BF16), dc))
                d_k.append(dot(d_scores, q_low))
                d_q.append(dot_tn(d_scores, k_low))
            for c, d in enumerate((d_q, d_k, d_v)):
                to = slice(c * cols + p * PAIR, c * cols + (p + 1) * PAIR)
                d_ref[at, to] = jnp.where(is_first, *d).astype(BF16)
    d = d_ref[...]
    halves(rel_ref, d, keep_ref, send_ref, (0, slice(None), slice(0, 3 * cols)))
    halves(low_rel_ref, ctx_ref[...], keep_ref, send_ref, (0, slice(None), slice(3 * cols, 4 * cols)))
    bias_q = column_sum(d[:, :cols].astype(F32))
    bias_v = column_sum(d[:, 2 * cols :].astype(F32))
    vectors = jnp.concatenate([a_ref[0:3, :], f_ref[2:3, :], f_ref[0:2, :], f_ref[3:5, :]])
    blocks[...] = jnp.zeros(blocks.shape, F32)
    n = rel_ref.shape[0] // BLOCKS
    few_q, few_i = cols // BLOCKS, bin_ref.shape[1] // BLOCKS
    for b in range(BLOCKS):
        blocks[b, 0:8, :n] = vectors[:, b * n : (b + 1) * n]
        blocks[b, 8:9, :few_i] = bin_ref[:, b * few_i : (b + 1) * few_i]
        blocks[b, 9:10, :] = mll_ref[...]
        blocks[b, 10:11, :few_q] = bias_q[:, b * few_q : (b + 1) * few_q]
        blocks[b, 11:12, :few_q] = bias_v[:, b * few_q : (b + 1) * few_q]
    half = keep_ref.shape[1]
    order = row_order(bits)
    for ref, first in ((keep_ref, 0), (send_ref, BLOCKS // 2)):
        ref[0, :, 4 * cols :] = jnp.zeros((half, 128), F32)
        for p in range(BLOCKS // 2):
            ref[0, p * n : p * n + 16, 4 * cols :] = blocks[order[first + p] ^ pos[1]]
    sum_ref[...] = (
        before_ref[...]
        + dot_nt(d[:, :cols], w_ref[0])
        + dot_nt(d[:, cols : 2 * cols], w_ref[1])
        + dot_nt(d[:, 2 * cols :], w_ref[2])
    )


def attend_back(line, bits, q, k, v, ctx, low, low_rel, rel, w, w_out, before, *small):
    rows, cols = q.shape
    width = before.shape[1]
    sent = shape((1, width // 2, 4 * cols + 128))
    scratch = [
        pltpu.VMEM((rows, 3 * cols), BF16),
        pltpu.VMEM((rows, cols), BF16),
        pltpu.VMEM((BLOCKS, 16, 128), F32),
    ]
    args = (q, k, v, ctx, low, low_rel, rel, w, w_out, before, *small)
    kernel = functools.partial(attend_back_kernel, bits)
    return line.run(kernel, [sent, sent, shape((rows, width))], args, scratch=scratch)


def on_device(
    hidden_in,
    cotangent,
    valid,
    answers,
    query_embed,
    w_qkv,
    b_qv,
    w_out,
    b_out,
    gain_attn,
    shift_attn,
    w_in,
    b_in,
    w_down,
    b_down,
    gain_ffn,
    shift_ffn,
    w_ret,
    w_span,
):
    here = lax.axis_index("batch")
    y = lax.axis_index("mp")
    devices = lax.axis_size("batch")
    me = here // (devices // BLOCKS)
    width = hidden_in.shape[1]
    rows = hidden_in.shape[0] // 2
    slots = rows // SEQ
    per_query = SLOTS // (2 * slots)
    n_queries = query_embed.shape[0]
    cols = w_qkv.shape[2]
    hidden = w_in.shape[1]
    query = here // per_query
    told = jnp.where((y == 0) & (here % per_query == 0), query, -1)
    pos = jnp.stack([y, me, me & 7, query, told, here, (me & 7) ^ (X | Z0)]).astype(jnp.int32)
    line = Line(pos)
    block = hidden // 3

    def row(v):
        return v.reshape(1, -1)

    rel = shape((width, rows), BF16)
    low_shape = shape((rows, width), BF16)
    full = shape((rows, width))
    turn = [pltpu.VMEM((width, rows), BF16)]

    qkv_flat = w_qkv.reshape(-1, cols)
    b_in_row = row(b_in)
    heads = [shape((rows, cols), BF16)] * 4
    a0 = over_y(pack_attn(line, qkv_flat, w_out, b_qv, b_in_row, 2))
    ad = over_y(pack_attn(line, qkv_flat, w_out, b_qv, b_in_row, 6))
    q1, k1, v1, ctx1, part, x_rel1, x_rel2 = line.run(
        attend_own_kernel, heads + [full, rel, rel], (hidden_in, w_qkv, b_qv, w_out), scratch=turn
    )
    f0 = over_y(pack_in(line, w_in, 2))
    a0 = line.here(a0)
    ax, az = across(a0, bit_mask(X)), across(a0, bit_mask(Z0))
    g0 = over_y(pack_down(line, w_down, 2))
    ad = line.here(ad)
    parts, order = with_core([a0, ax, az, ad], [0, X, Z0, X | Z0])
    qkv2, w_out2, b_qv2, b_in2 = line.run(
        functools.partial(unpack_attn_kernel, order),
        [shape(qkv_flat.shape, BF16), shape(w_out.shape, BF16), shape(b_qv.shape), shape((1, hidden))],
        parts,
    )
    w_qkv2 = qkv2.reshape(w_qkv.shape)
    q2, k2, v2, ctx2, mixed, base, first_low, first_rel1, first_rel2 = line.run(
        attend_other_kernel,
        heads + [full, full, low_shape, rel, rel],
        (
            hidden_in,
            w_qkv2,
            b_qv2,
            w_out2,
            part,
            row(b_out),
            row(gain_attn),
            row(shift_attn),
            row(b_down),
        ),
        scratch=turn,
    )
    fd = over_y(pack_in(line, w_in, 6))
    f0 = line.here(f0)
    fx, fz = across(f0, bit_mask(X)), across(f0, bit_mask(Z0))
    act_shapes = [shape((rows, hidden), BF16), shape((rows, hidden))]
    act1, slope1, pre = line.run(
        functools.partial(up_kernel, block),
        act_shapes + [full],
        (first_low, w_in, b_in_row, w_down, base),
    )
    gd = over_y(pack_down(line, w_down, 6))
    g0 = line.here(g0)
    gx, gz = across(g0, bit_mask(X)), across(g0, bit_mask(Z0))
    parts, order = with_core([f0, fx, fz, fd], [0, X, Z0, X | Z0])
    (w_in2,) = line.run(
        functools.partial(unpack_in_kernel, order), [shape(w_in.shape, BF16)], parts
    )
    act2, slope2 = line.run(
        functools.partial(up_in_kernel, block), act_shapes, (first_low, w_in2, b_in2)
    )
    parts, order = with_core([g0, gx, gz, gd], [0, X, Z0, X | Z0])
    (w_down2,) = line.run(
        functools.partial(unpack_down_kernel, order), [shape(w_down.shape, BF16)], parts
    )
    (pre,) = line.run(up_down_kernel, [full], (act2, w_down2, pre))
    span_rows = w_span.T
    second, marks, stats = line.run(
        loss_kernel,
        [full, shape((rows, 2)), shape((8, 128))],
        (pre, answers, valid, row(gain_ffn), row(shift_ffn), span_rows, w_ret, query_embed),
    )

    all_stats = [stats, over_y(stats)]
    mask = 1
    while mask < per_query:
        all_stats = all_stats + [across(t, mask) for t in all_stats]
        mask *= 2
    d_sum, d_ffn, d_ffn_rel1, d_ffn_rel2, sent, ret_rel, small_f, mll_row = line.run(
        functools.partial(loss_back_kernel, len(all_stats)),
        [
            full,
            low_shape,
            rel,
            rel,
            full,
            shape((width, w_ret.shape[1])),
            shape((8, width)),
            shape((1, 128)),
        ],
        (cotangent, *all_stats, second, pre, marks, row(gain_ffn), span_rows, w_ret, query_embed),
        scratch=turn + [pltpu.VMEM((width, 8), F32)],
    )
    second_theirs = over_y(sent)

    half = hidden // 2
    d1 = Chunk(line, *product(line, d_ffn_rel1, act1, act2, 0, half, ret_rel))
    d2 = Chunk(line, *product(line, d_ffn_rel2, act1, act2, half, half))
    keep, send, part, b_in_o = down_back(line, d_ffn, first_rel2, w_down2, w_in2, slope2, d_sum, block)
    i2 = Chunk(line, keep, send)
    exchange(line, over(X), HALF, d1)
    exchange(line, over(Z0), HALF, d2)
    keep, send, part, b_in_s = down_back(line, d_ffn, first_rel1, w_down, w_in, slope1, part, block)
    i1 = Chunk(line, keep, send)
    exchange(line, over(Z0), HALF, i2)

    d_mixed, d_att, d_att_rel1, d_att_rel2, small_a = line.run(
        mixed_back_kernel,
        [full, low_shape, rel, rel, shape((8, width))],
        (part, mixed, row(gain_attn)),
        scratch=turn,
    )
    exchange(line, over(X), HALF, i1)
    keep, send, part = attend_back(
        line,
        X_FIRST,
        *(q2, k2, v2, ctx2, d_att, d_att_rel1, x_rel1, w_qkv2, w_out2, d_mixed),
        *(small_a, small_f, b_in_o, mll_row),
    )
    q_other = Chunk(line, keep, send)
    keep, send, g_in = attend_back(
        line,
        Z_FIRST,
        *(q1, k1, v1, ctx1, d_att, d_att_rel2, x_rel2, w_qkv, w_out, part),
        *(small_a, small_f, b_in_s, mll_row),
    )
    q_own = Chunk(line, keep, send)
    layer_out = place(line, second, line.here(second_theirs), BF16)
    exchange(line, over_y, OTHER, d1, d2)
    exchange(line, over(X), HALF, q_other)
    exchange(line, over(Z0), HALF, q_own)
    grad_theirs = over_y(line.here(g_in))
    exchange(line, over(Z0), HALF, d1, i1)
    exchange(line, over(X), HALF, d2, i2)
    exchange(line, over(Z0), HALF, q_other)
    exchange(line, over(X), HALF, q_own)
    exchange(line, over(Z1), HALF, d1, d2, i1, i2)
    exchange(line, over(Z1), HALF, q_own, q_other)
    d1.take()
    d2.take()
    i1.take()
    i2_theirs = exchange(line, over_y, ALL, i2)
    g_in1 = i1.result(i2_theirs.get())
    g_down1, g_down2 = d1.result(), d2.result()
    q_own.take()
    q_theirs = exchange(line, over_y, ALL, q_other)
    line.last = []
    grad_in = place(line, g_in, line.here(grad_theirs), F32)
    g_q = q_own.result(q_theirs.get())

    rest = devices // BLOCKS
    misc = g_q[:, 4 * cols :]
    if rest > 1:
        misc = lax.psum(misc, "batch", axis_index_groups=groups_of(rest))

    def mine(line_number, total):
        few = total // devices
        values = misc[line_number, : total // BLOCKS]
        return values if rest == 1 else lax.dynamic_slice_in_dim(values, here % rest * few, few, 0)

    vectors = [mine(k, width) for k in range(8)]
    g_qkv = last_rows(g_q[:, : 3 * cols])
    g_down = jnp.concatenate([last_rows(g_down1[:, :half]).T, last_rows(g_down2).T])
    return (
        misc[9, :n_queries],
        layer_out,
        grad_in,
        jnp.stack([g_qkv[:, c * cols : (c + 1) * cols] for c in range(3)]),
        jnp.stack([mine(10, cols), mine(11, cols)]),
        last_rows(g_q[:, 3 * cols : 4 * cols]).T,
        vectors[0],
        vectors[1],
        vectors[2],
        last_rows(g_in1),
        mine(8, hidden),
        g_down,
        vectors[3],
        vectors[4],
        vectors[5],
        last_rows(g_down1[:, half:]),
        jnp.stack(vectors[6:8], 1),
    )


def solution(mesh):
    return jax.shard_map(
        on_device,
        mesh=mesh,
        in_specs=(
            P("batch", None),
            P("batch", None),
            P("batch"),
            P("batch", None),
            P(),
            P(None, None, "mp"),
            P(None, "mp"),
            P("mp", None),
            P(),
            P(),
            P(),
            P(None, "mp"),
            P("mp"),
            P("mp", None),
            P(),
            P(),
            P(),
            P(),
            P(),
        ),
        out_specs=(
            P(),
            P("batch", None),
            P("batch", None),
            P(None, "batch", "mp"),
            P(None, ("mp", "batch")),
            P("mp", "batch"),
            P("batch"),
            P("batch"),
            P("batch"),
            P("batch", "mp"),
            P(("mp", "batch")),
            P("mp", "batch"),
            P("batch"),
            P("batch"),
            P("batch"),
            P("batch", None),
            P("batch", None),
        ),
        check_vma=False,
    )
```

```python
import functools

import jax
import jax.numpy as jnp
from jax import lax
from jax.experimental import pallas as pl
from jax.experimental.pallas import tpu as pltpu
from jax.sharding import PartitionSpec as P

HEAD_DIM = 64
PAIR = 2 * HEAD_DIM
SEQ = 288
SLOTS = 8
BLOCKS = 16
CORE, X, Z0, Z1 = 1, 2, 4, 8
EPS = 1e-05
FLOOR = -1e30
F32 = jnp.float32
BF16 = jnp.bfloat16
HIGHEST = lax.Precision.HIGHEST
LIMIT = 16
X_FIRST = (CORE, X, Z0, Z1)
Z_FIRST = (CORE, Z0, X, Z1)
SCALE = HEAD_DIM ** (-0.5)
HALF, OTHER, ALL = 0, 1, 2

VMEM = pl.BlockSpec(memory_space=pltpu.VMEM)
SMEM = pl.BlockSpec(memory_space=pltpu.SMEM)


def across(v, mask):
    n = lax.axis_size("batch")
    return lax.ppermute(v, "batch", [(i, i ^ mask) for i in range(n)])


def over_y(v):
    return lax.ppermute(v, "mp", [(0, 1), (1, 0)])


def bit_mask(bit):
    return bit * (lax.axis_size("batch") // BLOCKS)


def shape(dims, dtype=F32):
    return jax.ShapeDtypeStruct(dims, dtype)


def cost(flops, moved, exps=0):
    return pl.CostEstimate(flops=int(flops), bytes_accessed=int(moved), transcendentals=int(exps))


class Line:
    def __init__(self, pos):
        self.pos = pos
        self.last = []
        self.token = pos

    def after(self, *arrays):
        self.last = self.last + list(arrays)
        self.token = arrays[-1]

    def post(self):
        def kernel(pos, out_ref):
            out_ref[...] = jnp.zeros(out_ref.shape, F32)

        self.run(kernel, [jax.ShapeDtypeStruct((8, 128), F32)], (), flops=1e12)

    def here(self, array):
        return lax.optimization_barrier((array, self.token))[0]

    def run(self, kernel, outs, args, specs=None, scratch=(), flops=0):
        n, extra = len(args), self.last
        params = pltpu.CompilerParams(vmem_limit_bytes=LIMIT * 2**20)

        def body(pos, *refs):
            kernel(pos, *refs[:n], *refs[n + len(extra) :])

        unread = [pl.BlockSpec(memory_space=pl.ANY)] * len(extra)
        if specs is None:
            small = [SMEM if a.dtype == jnp.int32 else VMEM for a in args]
            how = {
                "in_specs": [SMEM] + small + unread,
                "out_specs": (VMEM,) * len(outs),
                "scratch_shapes": list(scratch),
            }
        else:
            how = {
                "grid_spec": pltpu.PrefetchScalarGridSpec(
                    num_scalar_prefetch=1,
                    grid=(1,),
                    in_specs=[whole(a) if spec is None else spec for a, spec in zip(args, specs)]
                    + unread,
                    out_specs=tuple(whole(o) for o in outs),
                    scratch_shapes=list(scratch),
                )
            }
        results = pl.pallas_call(
            body,
            out_shape=tuple(outs),
            compiler_params=params,
            cost_estimate=cost(1e11, 1e8),
            **how,
        )(self.pos, *args, *extra)
        self.last = [min(results, key=lambda r: r.size)]
        self.token = self.last[0]
        return results


def whole(a):
    return pl.BlockSpec(a.shape, lambda *_: (0,) * len(a.shape))


def dot(a, b, precision=None):
    return jnp.dot(a, b, precision=precision, preferred_element_type=F32)


def dot_nt(a, b, precision=None):
    return lax.dot_general(
        a, b, (((1,), (1,)), ((), ())), precision=precision, preferred_element_type=F32
    )


def dot_tn(a, b):
    return lax.dot_general(a, b, (((0,), (0,)), ((), ())), preferred_element_type=F32)


def pack_attn_kernel(pos, qkv_ref, out_ref, bqv_ref, bin_ref, a_ref):
    n, cols = qkv_ref.shape
    m = out_ref.shape[0]
    a_ref[:n, :] = qkv_ref[...].astype(F32)
    a_ref[n : n + m, :] = out_ref[:, :cols].astype(F32)
    a_ref[n + m : n + 2 * m, :] = out_ref[:, cols:].astype(F32)
    at = n + 2 * m
    a_ref[at : at + 8, :] = jnp.zeros((8, cols), F32)
    a_ref[at : at + 2, :] = bqv_ref[...]
    for k in range(bin_ref.shape[1] // cols):
        a_ref[at + 2 + k : at + 3 + k, :] = bin_ref[:, k * cols : (k + 1) * cols]


def eighth_of(w, place):
    return pl.BlockSpec((w.shape[0] // 8, w.shape[1]), lambda i, pos: (pos[place], 0))


def pack_attn(line, qkv, w_out, b_qv, b_in, place):
    rows = qkv.shape[0] // 8 + w_out.shape[0] // 4 + 8
    specs = [eighth_of(qkv, place), eighth_of(w_out, place), None, None]
    outs = [shape((rows, qkv.shape[1]))]
    return line.run(pack_attn_kernel, outs, (qkv, w_out, b_qv, b_in), specs)[0]


def pack_in_kernel(pos, in_ref, b_ref):
    r, wide = in_ref.shape[0], b_ref.shape[1]
    b_ref[:r, :] = in_ref[:, :wide].astype(F32)
    b_ref[r:, :] = in_ref[:, wide:].astype(F32)


def pack_in(line, w, place):
    outs = [shape((w.shape[0] // 4, w.shape[1] // 2))]
    return line.run(pack_in_kernel, outs, (w,), [eighth_of(w, place)])[0]


def pack_down_kernel(pos, down_ref, c_ref):
    c_ref[...] = down_ref[...].astype(F32)


def pack_down(line, w, place):
    outs = [shape((w.shape[0] // 8, w.shape[1]))]
    return line.run(pack_down_kernel, outs, (w,), [eighth_of(w, place)])[0]


def unpack_attn_kernel(order, pos, *refs):
    qkv_ref, out_ref, bqv_ref, bin_ref = refs[-4:]
    n, m = qkv_ref.shape[0] // 8, out_ref.shape[0] // 8
    cols = qkv_ref.shape[1]
    for r, ref, at in pieces(order, refs[:-4], n + 2 * m + 8):
        place = r ^ pos[2]
        to = pl.ds(pl.multiple_of(place * n, 16), n)
        qkv_ref[to, :] = ref[at : at + n, :].astype(BF16)
        to = pl.ds(pl.multiple_of(place * m, 16), m)
        out_ref[to, :cols] = ref[at + n : at + n + m, :].astype(BF16)
        out_ref[to, cols:] = ref[at + n + m : at + n + 2 * m, :].astype(BF16)
    first = refs[0]
    at = n + 2 * m
    bqv_ref[...] = first[at : at + 2, :]
    for k in range(bin_ref.shape[1] // cols):
        bin_ref[:, k * cols : (k + 1) * cols] = first[at + 2 + k : at + 3 + k, :]


def unpack_in_kernel(order, pos, *refs):
    in_ref = refs[-1]
    n = in_ref.shape[0] // 8
    wide = in_ref.shape[1] // 2
    for r, ref, at in pieces(order, refs[:-1], 2 * n):
        to = pl.ds(pl.multiple_of((r ^ pos[2]) * n, 16), n)
        in_ref[to, :wide] = ref[at : at + n, :].astype(BF16)
        in_ref[to, wide:] = ref[at + n : at + 2 * n, :].astype(BF16)


def unpack_down_kernel(order, pos, *refs):
    down_ref = refs[-1]
    m = down_ref.shape[0] // 8
    for r, ref, at in pieces(order, refs[:-1], m):
        to = pl.ds(pl.multiple_of((r ^ pos[2]) * m, 16), m)
        down_ref[to, :] = ref[at : at + m, :].astype(BF16)


class Pieces:
    def __init__(self, line):
        self.line = line
        self.parts, self.order = [], []

    def add(self, arrays, order):
        arrays = [self.line.here(a) for a in arrays]
        both = arrays[0] if len(arrays) == 1 else jnp.concatenate(arrays)
        self.line.after(both)
        self.parts = self.parts + [both, across(both, bit_mask(CORE))]
        self.order = self.order + order + [r | CORE for r in order]


def pieces(order, refs, rows):
    at = 0
    for ref in refs:
        for k in range(ref.shape[0] // rows):
            yield order[at], ref, k * rows
            at += 1


def place_kernel(pos, mine_ref, theirs_ref, out_ref):
    rows = mine_ref.shape[0]
    at = pl.multiple_of(pos[0] * rows, rows)
    out_ref[pl.ds(at, rows), :] = mine_ref[...].astype(out_ref.dtype)
    at = pl.multiple_of((1 - pos[0]) * rows, rows)
    out_ref[pl.ds(at, rows), :] = theirs_ref[...].astype(out_ref.dtype)


def place(line, mine, theirs, dtype):
    rows, width = mine.shape
    return line.run(place_kernel, [shape((2 * rows, width), dtype)], (mine, theirs))[0]


def row_order(bits):
    order = []
    for p in range(BLOCKS):
        r = 0
        for k, bit in enumerate(bits):
            if (p >> (len(bits) - 1 - k)) & 1:
                r |= bit
        order.append(r)
    return order


def store_relative(a, me, scratch, *places):
    scratch[...] = a.T
    for bits, out_ref in places:
        n = out_ref.shape[0] // BLOCKS
        for p, r in enumerate(row_order(bits)):
            at = pl.multiple_of((r ^ me) * n, 16)
            out_ref[p * n : (p + 1) * n, :] = scratch[pl.ds(at, n), :]


def own_rows(pos, ref):
    rows = ref.shape[0] // 2
    return ref[pl.ds(pl.multiple_of(pos[0] * rows, 16), rows), :]


def summed(terms):
    result = terms[0]
    for t in terms[1:]:
        result = result + t
    return result


class Arrival:
    def __init__(self, line, array):
        self.line, self.array, self.waited = line, array, False

    def get(self):
        if not self.waited:
            self.array, self.waited = self.line.here(self.array), True
        return self.array


class Chunk:
    def __init__(self, line, keep, send):
        self.terms = [keep]
        self.n, self.cols = keep.shape[1], keep.shape[2]
        self.heads = keep.shape[0]
        self.pending = (Arrival(line, across(send, bit_mask(CORE))), 0)

    def take(self):
        if self.pending:
            arrival, at = self.pending
            self.terms = self.terms + [arrival.get()[:, :, at : at + self.cols]]
            self.pending = None

    def give(self, what):
        self.take()
        if what == HALF:
            half = self.n // 2
            piece = summed([t[: self.heads, half : self.n] for t in self.terms])
            self.n = half
        elif what == OTHER:
            piece = summed([t[1:2, : self.n] for t in self.terms])
            self.heads = 1
        else:
            piece = summed([t[:1, : self.n] for t in self.terms])
        return piece

    def result(self, *more):
        return summed([t[0, : self.n] for t in [*self.terms, *more]])


def exchange(line, move, what, *chunks):
    pieces = [c.give(what) for c in chunks]
    sent = pieces[0] if len(pieces) == 1 else jnp.concatenate(pieces, 2)
    line.after(sent)
    arrival = Arrival(line, move(sent))
    at = 0
    for c in chunks:
        c.pending = (arrival, at)
        at += c.cols
    return arrival


def over(bit):
    return lambda v: across(v, bit_mask(bit))


def groups_of(rest):
    return [[g * rest + k for k in range(rest)] for g in range(BLOCKS)]


def last_rows(v):
    rest = lax.axis_size("batch") // BLOCKS
    if rest == 1:
        return v
    groups = groups_of(rest)
    return lax.psum_scatter(v, "batch", scatter_dimension=0, axis_index_groups=groups, tiled=True)


def norm(v):
    centre = v - jnp.mean(v, -1, keepdims=True)
    inverse = lax.rsqrt(jnp.mean(centre * centre, -1, keepdims=True) + EPS)
    return centre * inverse, inverse


def norm_back(grad, normed, inverse, gain):
    scaled = grad * gain
    return inverse * (
        scaled
        - jnp.mean(scaled, -1, keepdims=True)
        - normed * jnp.mean(scaled * normed, -1, keepdims=True)
    )


def column_sum(v):
    return jnp.sum(v, 0, keepdims=True)


def head_masks():
    lane = lax.broadcasted_iota(jnp.int32, (1, PAIR), 1)
    first = jnp.where(lane < HEAD_DIM, 1.0, 0.0)
    return lane < HEAD_DIM, (first.astype(BF16), (1.0 - first).astype(BF16))


def attend(x, w_ref, b_ref, wo_ref, q_ref, k_ref, v_ref, ctx_ref):
    q_ref[...] = (dot(x, w_ref[0]) + b_ref[0:1, :]).astype(BF16)
    k_ref[...] = dot(x, w_ref[1]).astype(BF16)
    v_ref[...] = (dot(x, w_ref[2]) + b_ref[1:2, :]).astype(BF16)
    is_first, masks = head_masks()
    for s in range(q_ref.shape[0] // SEQ):
        at = slice(s * SEQ, (s + 1) * SEQ)
        for p in range(q_ref.shape[1] // PAIR):
            lanes = slice(p * PAIR, (p + 1) * PAIR)
            q, k, v = q_ref[at, lanes] * SCALE, k_ref[at, lanes], v_ref[at, lanes]
            results = []
            for mask in masks:
                scores = dot_nt(q * mask, k)
                e = jnp.exp(scores - jnp.max(scores, -1, keepdims=True))
                probs = (e * (1.0 / jnp.sum(e, -1, keepdims=True))).astype(BF16)
                results.append(dot(probs, v))
            ctx_ref[at, lanes] = jnp.where(is_first, *results).astype(BF16)
    return dot(ctx_ref[...], wo_ref[...])


def attend_own_kernel(
    pos, x_ref, w_ref, b_ref, wo_ref, q_ref, k_ref, v_ref, ctx_ref, part_ref, rel_ref, scratch
):
    x = own_rows(pos, x_ref)
    store_relative(x, pos[1], scratch, (X_FIRST, rel_ref))
    part_ref[...] = attend(x, w_ref, b_ref, wo_ref, q_ref, k_ref, v_ref, ctx_ref)


def attend_other_kernel(
    pos,
    x_ref,
    w_ref,
    b_ref,
    wo_ref,
    part_ref,
    bias_ref,
    gain_ref,
    shift_ref,
    down_ref,
    q_ref,
    k_ref,
    v_ref,
    ctx_ref,
    mixed_ref,
    base_ref,
    low_ref,
    rel1_ref,
    rel2_ref,
    scratch,
):
    x = own_rows(pos, x_ref)
    part = attend(x, w_ref, b_ref, wo_ref, q_ref, k_ref, v_ref, ctx_ref)
    mixed = x.astype(F32) + (part_ref[...] + part) + bias_ref[...]
    mixed_ref[...] = mixed
    first = norm(mixed)[0] * gain_ref[...] + shift_ref[...]
    base_ref[...] = first + down_ref[...]
    low = first.astype(BF16)
    low_ref[...] = low
    store_relative(low, pos[1], scratch, (X_FIRST, rel1_ref), (Z_FIRST, rel2_ref))


def lift(low, w_in_ref, b_ref, act_ref, slope_ref, block):
    for i in range(act_ref.shape[1] // block):
        at = slice(i * block, (i + 1) * block)
        inner = dot(low, w_in_ref[:, at]) + b_ref[:, at]
        cdf = 0.5 + 0.5 * lax.erf(inner * 0.5**0.5)
        density = jnp.exp(-0.5 * inner * inner) * 0.3989422804014327
        act_ref[:, at] = (inner * cdf).astype(BF16)
        slope_ref[:, at] = cdf + inner * density


def up_kernel(block, pos, low_ref, w_in_ref, b_ref, w_down_ref, before_ref, act_ref, slope_ref, sum_ref):
    lift(low_ref[...], w_in_ref, b_ref, act_ref, slope_ref, block)
    sum_ref[...] = before_ref[...] + dot(act_ref[...], w_down_ref[...])


def up_in_kernel(block, pos, low_ref, w_in_ref, b_ref, act_ref, slope_ref):
    lift(low_ref[...], w_in_ref, b_ref, act_ref, slope_ref, block)


def up_down_kernel(pos, act_ref, w_down_ref, before_ref, sum_ref):
    sum_ref[...] = before_ref[...] + dot(act_ref[...], w_down_ref[...])


def loss_kernel(
    pos,
    pre_ref,
    answers,
    valid,
    gain_f,
    shift_f,
    span_ref,
    ret_ref,
    query_ref,
    second_ref,
    marks_ref,
    stats_ref,
):
    second = norm(pre_ref[...])[0] * gain_f[...] + shift_f[...]
    second_ref[...] = second
    q_row = query_ref[pl.ds(pos[3], 1), :]
    row = lax.broadcasted_iota(jnp.int32, (SEQ, 1), 0)
    line = lax.broadcasted_iota(jnp.int32, (8, 128), 0)
    lane = lax.broadcasted_iota(jnp.int32, (8, 128), 1)
    stats = jnp.full((8, 128), FLOOR, F32)
    slots = second.shape[0] // SEQ
    for s in range(slots):
        slot = pos[0] * slots + s
        mine = second[s * SEQ : (s + 1) * SEQ, :]
        span = jnp.zeros((1, 1), F32)
        for c in range(2):
            logits = jnp.sum(mine * span_ref[c : c + 1, :], -1, keepdims=True)
            shifted = logits - jnp.max(logits, 0, keepdims=True)
            log_probs = shifted - jnp.log(jnp.sum(jnp.exp(shifted), 0, keepdims=True))
            mark = jnp.where(row == answers[slot, c], 1.0, 0.0)
            span = span + jnp.sum(log_probs * mark, 0, keepdims=True)
            marks_ref[s * SEQ : (s + 1) * SEQ, c : c + 1] = mark - jnp.exp(log_probs)
        embed = dot(mine[:8, :], ret_ref[...], HIGHEST)[0:1, :]
        retrieval = jnp.sum(embed * q_row, -1, keepdims=True)
        live = valid[slot] > 0
        joint = jnp.where(live, retrieval + span, FLOOR)
        prior = jnp.where(live, retrieval, FLOOR)
        stats = jnp.where((line == s) & (lane == 0), joint, stats)
        stats = jnp.where((line == s) & (lane == 1), prior, stats)
    stats_ref[...] = stats


def loss_back_kernel(n_stats, pos, cot_ref, *refs):
    stats_refs = refs[:n_stats]
    (
        second_ref,
        pre_ref,
        marks_ref,
        gain_f,
        span_ref,
        ret_ref,
        query_ref,
        sum_ref,
        low_ref,
        rel_ref,
        sent_ref,
        ret_out,
        small_ref,
        mll_ref,
        scratch,
        leads,
    ) = refs[n_stats:]
    all_stats = [ref[...] for ref in stats_refs]
    peak = jnp.max(functools.reduce(jnp.maximum, all_stats), 0, keepdims=True)
    total = jnp.sum(summed([jnp.exp(t - peak) for t in all_stats]), 0, keepdims=True)
    lse = peak + jnp.log(total)
    weight = jnp.exp(all_stats[0] - lse)
    q_row = query_ref[pl.ds(pos[3], 1), :]
    lead_grad = dot_nt(jnp.broadcast_to(q_row, (8, q_row.shape[1])), ret_ref[...], HIGHEST)
    top = lax.broadcasted_iota(jnp.int32, (8, 1), 0) == 0
    rows = cot_ref.shape[0] // 2
    slots = rows // SEQ
    small_ref[...] = jnp.zeros(small_ref.shape, F32)
    embeds = []
    for s in range(slots):
        at = slice(s * SEQ, (s + 1) * SEQ)
        post = weight[s : s + 1, 0:1]
        prior = weight[s : s + 1, 1:2]
        second = second_ref[at, :]
        sent_ref[at, :] = second
        start = pl.multiple_of(pos[0] * rows + s * SEQ, 16)
        grad = cot_ref[pl.ds(start, SEQ), :].astype(F32)
        for c in range(2):
            d_logits = -post * marks_ref[at, c : c + 1]
            grad = grad + d_logits * span_ref[c : c + 1, :]
            small_ref[3 + c : 4 + c, :] += column_sum(second * d_logits)
        sum_ref[at, :] = grad
        sum_ref[s * SEQ : s * SEQ + 8, :] += jnp.where(top, (prior - post) * lead_grad, 0.0)
        small_ref[5 + s : 6 + s, :] = second[0:1, :]
        embeds.append((prior - post) * q_row)
    leads[...] = small_ref[...].T
    n = ret_out.shape[0] // BLOCKS
    for p, r in enumerate(row_order(Z_FIRST)):
        block = leads[pl.ds(pl.multiple_of((r ^ pos[1]) * n, 8), n), :]
        ret_out[p * n : (p + 1) * n, :] = summed(
            [block[:, 5 + s : 6 + s] * embed for s, embed in enumerate(embeds)]
        )
    grad = sum_ref[...]
    normed, inverse = norm(pre_ref[...])
    small_ref[0:1, :] = column_sum(grad * normed)
    small_ref[1:2, :] = column_sum(grad)
    d_sum = norm_back(grad, normed, inverse, gain_f[...])
    small_ref[2:3, :] = column_sum(d_sum)
    sum_ref[...] = d_sum
    low = d_sum.astype(BF16)
    low_ref[...] = low
    store_relative(low, pos[1], scratch, (Z_FIRST, rel_ref))
    lane = lax.broadcasted_iota(jnp.int32, mll_ref.shape, 1)
    mll = lse[:, 0:1] - lse[:, 1:2]
    mll_ref[...] = jnp.where(lane == pos[4], mll, 0.0)


def halves(left_ref, right, keep_ref, send_ref, index):
    half = left_ref.shape[0] // 2
    keep_ref[index] = dot(left_ref[:half, :], right)
    send_ref[index] = dot(left_ref[half:, :], right)


def product_kernel(start, block, pos, left_ref, own_ref, other_ref, *refs):
    *more, keep_ref, send_ref = refs
    at = slice(start, start + block)
    half = keep_ref.shape[1]
    for h, ref in enumerate((own_ref, other_ref)):
        halves(left_ref, ref[:, at], keep_ref, send_ref, (h, slice(None), slice(0, block)))
        for extra in more:
            keep_ref[h, :, block:] = extra[:half, :]
            send_ref[h, :, block:] = extra[half:, :]


def product(line, left, own, other, start, block, *more):
    width = left.shape[0]
    outs = [shape((2, width // 2, block + sum(m.shape[1] for m in more)))] * 2
    kernel = functools.partial(product_kernel, start, block)
    return line.run(kernel, outs, (left, own, other, *more))


def down_back_kernel(
    start,
    block,
    pos,
    low_ref,
    rel_ref,
    wd1_ref,
    wd2_ref,
    wi1_ref,
    wi2_ref,
    slope1_ref,
    slope2_ref,
    before_ref,
    keep_ref,
    send_ref,
    sum_ref,
    bias_ref,
    d_ref,
):
    low = low_ref[...]
    total = before_ref[...]
    count = keep_ref.shape[2]
    for h, (wd_ref, wi_ref, slope_ref) in enumerate(
        ((wd1_ref, wi1_ref, slope1_ref), (wd2_ref, wi2_ref, slope2_ref))
    ):
        for i in range(count // block):
            to = slice(i * block, (i + 1) * block)
            at = slice(start + i * block, start + (i + 1) * block)
            d_inner = (dot_nt(low, wd_ref[at, :]) * slope_ref[:, at]).astype(BF16)
            d_ref[:, to] = d_inner
            bias_ref[h : h + 1, to] = column_sum(d_inner.astype(F32))
            halves(rel_ref, d_inner, keep_ref, send_ref, (h, slice(None), to))
        total = total + dot_nt(d_ref[...], wi_ref[:, start : start + count])
    sum_ref[...] = total


def down_back(line, start, count, low, rel, w_down, w_in, slope, before):
    rows, width = low.shape
    block = count // 2
    return line.run(
        functools.partial(down_back_kernel, start, block),
        [
            shape((2, width // 2, count)),
            shape((2, width // 2, count)),
            shape((rows, width)),
            shape((2, count)),
        ],
        (low, rel, *w_down, *w_in, *slope, before),
        scratch=[pltpu.VMEM((rows, count), BF16)],
    )


def mixed_back_kernel(
    pos, part_ref, mixed_ref, gain_ref, mix_ref, low_ref, rel_ref, small_ref, scratch
):
    grad = part_ref[...]
    normed, inverse = norm(mixed_ref[...])
    small_ref[...] = jnp.zeros(small_ref.shape, F32)
    small_ref[1:2, :] = column_sum(grad * normed)
    small_ref[2:3, :] = column_sum(grad)
    d_mixed = norm_back(grad, normed, inverse, gain_ref[...])
    small_ref[0:1, :] = column_sum(d_mixed)
    mix_ref[...] = d_mixed
    low = d_mixed.astype(BF16)
    low_ref[...] = low
    store_relative(low, pos[1], scratch, (X_FIRST, rel_ref))


def head_back(pos, lanes, at, q_ref, k_ref, v_ref, dc, store):
    is_first, masks = head_masks()
    q, k, v = (r[at, lanes] for r in (q_ref, k_ref, v_ref))
    q_low, k_low = q * SCALE, k * SCALE
    d_q, d_k, d_v = [], [], []
    for mask in masks:
        scores = dot_nt(k_low * mask, q)
        e = jnp.exp(scores - jnp.max(scores, 0, keepdims=True))
        probs = e * (1.0 / jnp.sum(e, 0, keepdims=True))
        d_probs = dot_nt(v * mask, dc)
        centre = jnp.sum(d_probs * probs, 0, keepdims=True)
        d_scores = (probs * (d_probs - centre)).astype(BF16)
        d_v.append(dot(probs.astype(BF16), dc))
        d_k.append(dot(d_scores, q_low))
        d_q.append(dot_tn(d_scores, k_low))
    for c, d in enumerate((d_q, d_k, d_v)):
        store(c, jnp.where(is_first, *d).astype(BF16))


def attend_back_kernel(pairs, more, pos, *refs):
    heads = (refs[0:6], refs[6:12])
    low_ref, low_rel_ref, rel_ref, before_ref = refs[12:16]
    keep_ref, send_ref, sum_ref, bias_ref, d_ref, dc_ref = refs[16 + more : 22 + more]
    start, count = pairs[0] * PAIR, len(pairs) * PAIR
    ours = slice(start, start + count)
    total = before_ref[...]
    for h, (q_ref, k_ref, v_ref, ctx_ref, w_ref, wo_ref) in enumerate(heads):
        dc_ref[...] = dot_nt(low_ref[...], wo_ref[ours, :]).astype(BF16)
        for s in range(q_ref.shape[0] // SEQ):
            at = slice(s * SEQ, (s + 1) * SEQ)
            for p in range(len(pairs)):
                lanes = slice(start + p * PAIR, start + (p + 1) * PAIR)

                def store(c, d, at=at, p=p):
                    d_ref[at, c * count + p * PAIR : c * count + (p + 1) * PAIR] = d

                dc = dc_ref[at, p * PAIR : (p + 1) * PAIR]
                head_back(pos, lanes, at, q_ref, k_ref, v_ref, dc, store)
        d = d_ref[...]
        bias_ref[h : h + 1, :count] = column_sum(d[:, :count].astype(F32))
        bias_ref[h : h + 1, count:] = column_sum(d[:, 2 * count :].astype(F32))
        halves(rel_ref, d, keep_ref, send_ref, (h, slice(None), slice(0, 3 * count)))
        context = ctx_ref[:, ours]
        halves(low_rel_ref, context, keep_ref, send_ref, (h, slice(None), slice(3 * count, 4 * count)))
        for c in range(3):
            total = total + dot_nt(d[:, c * count : (c + 1) * count], w_ref[c][:, ours])
    sum_ref[...] = total


def attend_back_last_kernel(bits, pairs, pos, *refs):
    more = 6
    attend_back_kernel(pairs, more, pos, *refs)
    a_ref, f_ref, bin1_ref, bin2_ref, mll_ref, before_ref = refs[16 : 16 + more]
    keep_ref, send_ref, _, bias_ref = refs[16 + more : 20 + more]
    blocks = refs[-1]
    last, count = len(pairs) * PAIR, before_ref.shape[1] // 2
    vectors = jnp.concatenate([a_ref[0:3, :], f_ref[2:3, :], f_ref[0:2, :], f_ref[3:5, :]])
    n = vectors.shape[1] // BLOCKS
    half = keep_ref.shape[1]
    order = row_order(bits)
    blocks[...] = jnp.zeros(blocks.shape, F32)
    for h in range(2):
        b_in = jnp.concatenate([bin1_ref[h : h + 1, :], bin2_ref[h : h + 1, :]], 1)
        b_q = jnp.concatenate([before_ref[h : h + 1, :count], bias_ref[h : h + 1, :last]], 1)
        b_v = jnp.concatenate([before_ref[h : h + 1, count:], bias_ref[h : h + 1, last:]], 1)
        for b in range(BLOCKS):
            blocks[b, 0:8, :n] = vectors[:, b * n : (b + 1) * n]
            blocks[b, 9:10, :] = mll_ref[...]
            for k, v in ((8, b_in), (10, b_q), (11, b_v)):
                few = v.shape[1] // BLOCKS
                blocks[b, k : k + 1, :few] = v[:, b * few : (b + 1) * few]
        for ref, first in ((keep_ref, 0), (send_ref, BLOCKS // 2)):
            ref[h, :, 4 * last :] = jnp.zeros((half, 128), F32)
            for p in range(BLOCKS // 2):
                ref[h, p * n : p * n + 16, 4 * last :] = blocks[order[first + p] ^ pos[1]]


def attend_back(line, kernel, count, extra, heads, shared, small=(), scratch=()):
    rows, width = shared[-1].shape
    sent = shape((2, width // 2, 4 * count + extra))
    scratch = [pltpu.VMEM((rows, 3 * count), BF16), pltpu.VMEM((rows, count), BF16), *scratch]
    outs = [sent, sent, shape((rows, width)), shape((2, 2 * count))]
    return line.run(kernel, outs, (*heads, *shared, *small), scratch=scratch)


def on_device(
    hidden_in,
    cotangent,
    valid,
    answers,
    query_embed,
    w_qkv,
    b_qv,
    w_out,
    b_out,
    gain_attn,
    shift_attn,
    w_in,
    b_in,
    w_down,
    b_down,
    gain_ffn,
    shift_ffn,
    w_ret,
    w_span,
):
    here = lax.axis_index("batch")
    y = lax.axis_index("mp")
    devices = lax.axis_size("batch")
    me = here // (devices // BLOCKS)
    width = hidden_in.shape[1]
    rows = hidden_in.shape[0] // 2
    slots = rows // SEQ
    per_query = SLOTS // (2 * slots)
    n_queries = query_embed.shape[0]
    cols = w_qkv.shape[2]
    hidden = w_in.shape[1]
    query = here // per_query
    told = jnp.where((y == 0) & (here % per_query == 0), query, -1)
    pos = jnp.stack([y, me, me & 7, query, told, here, (me & 7) ^ (X | Z0)]).astype(jnp.int32)
    line = Line(pos)
    block = hidden // 3

    def row(v):
        return v.reshape(1, -1)

    rel = shape((width, rows), BF16)
    low_shape = shape((rows, width), BF16)
    full = shape((rows, width))
    turn = [pltpu.VMEM((width, rows), BF16)]

    qkv_flat = w_qkv.reshape(-1, cols)
    b_in_row = row(b_in)
    heads = [shape((rows, cols), BF16)] * 4
    a0 = over_y(pack_attn(line, qkv_flat, w_out, b_qv, b_in_row, 2))
    ad = over_y(pack_attn(line, qkv_flat, w_out, b_qv, b_in_row, 6))
    q1, k1, v1, ctx1, part, x_rel1 = line.run(
        attend_own_kernel, heads + [full, rel], (hidden_in, w_qkv, b_qv, w_out), scratch=turn
    )
    f0 = over_y(pack_in(line, w_in, 2))
    line.post()
    a0 = line.here(a0)
    ax, az = across(a0, bit_mask(X)), across(a0, bit_mask(Z0))
    g0 = over_y(pack_down(line, w_down, 2))
    fd = over_y(pack_in(line, w_in, 6))
    gd = over_y(pack_down(line, w_down, 6))
    a = Pieces(line)
    a.add([a0, ad], [0, X | Z0])
    a.add([ax, az], [X, Z0])
    line.post()
    qkv2, w_out2, b_qv2, b_in2 = line.run(
        functools.partial(unpack_attn_kernel, a.order),
        [shape(qkv_flat.shape, BF16), shape(w_out.shape, BF16), shape(b_qv.shape), shape((1, hidden))],
        a.parts,
    )
    w_qkv2 = qkv2.reshape(w_qkv.shape)
    f0 = line.here(f0)
    fx, fz = across(f0, bit_mask(X)), across(f0, bit_mask(Z0))
    line.after(f0)
    line.post()
    q2, k2, v2, ctx2, mixed, base, first_low, first_rel1, first_rel2 = line.run(
        attend_other_kernel,
        heads + [full, full, low_shape, rel, rel],
        (
            hidden_in,
            w_qkv2,
            b_qv2,
            w_out2,
            part,
            row(b_out),
            row(gain_attn),
            row(shift_attn),
            row(b_down),
        ),
        scratch=turn,
    )
    act_shapes = [shape((rows, hidden), BF16), shape((rows, hidden))]
    act1, slope1, pre = line.run(
        functools.partial(up_kernel, block),
        act_shapes + [full],
        (first_low, w_in, b_in_row, w_down, base),
    )
    g0 = line.here(g0)
    line.after(g0)
    gx, gz = across(g0, bit_mask(X)), across(g0, bit_mask(Z0))
    f = Pieces(line)
    f.add([f0, fx, fz], [0, X, Z0])
    f.add([fd], [X | Z0])
    line.post()
    (w_in2,) = line.run(
        functools.partial(unpack_in_kernel, f.order), [shape(w_in.shape, BF16)], f.parts
    )
    act2, slope2 = line.run(
        functools.partial(up_in_kernel, block), act_shapes, (first_low, w_in2, b_in2)
    )
    g = Pieces(line)
    g.add([g0, gx], [0, X])
    g.add([gz, gd], [Z0, X | Z0])
    line.post()
    (w_down2,) = line.run(
        functools.partial(unpack_down_kernel, g.order), [shape(w_down.shape, BF16)], g.parts
    )
    (pre,) = line.run(up_down_kernel, [full], (act2, w_down2, pre))
    span_rows = w_span.T
    second, marks, stats = line.run(
        loss_kernel,
        [full, shape((rows, 2)), shape((8, 128))],
        (pre, answers, valid, row(gain_ffn), row(shift_ffn), span_rows, w_ret, query_embed),
    )

    all_stats = [stats, over_y(stats)]
    mask = 1
    while mask < per_query:
        all_stats = all_stats + [across(t, mask) for t in all_stats]
        mask *= 2
    d_sum, d_ffn, d_ffn_rel2, sent, ret_rel, small_f, mll_row = line.run(
        functools.partial(loss_back_kernel, len(all_stats)),
        [
            full,
            low_shape,
            rel,
            full,
            shape((width, w_ret.shape[1])),
            shape((8, width)),
            shape((1, 128)),
        ],
        (cotangent, *all_stats, second, pre, marks, row(gain_ffn), span_rows, w_ret, query_embed),
        scratch=turn + [pltpu.VMEM((width, 8), F32)],
    )
    second_theirs = over_y(sent)
    line.post()

    half = hidden // 2
    d1 = Chunk(line, *product(line, d_ffn_rel2, act1, act2, 0, half, ret_rel))
    d2 = Chunk(line, *product(line, d_ffn_rel2, act1, act2, half, half))
    both = (w_down, w_down2), (w_in, w_in2), (slope1, slope2)
    keep, send, part, b_in1 = down_back(line, 0, half, d_ffn, first_rel1, *both, d_sum)
    i1 = Chunk(line, keep, send)
    exchange(line, over(Z0), HALF, d1)
    line.post()
    keep, send, part, b_in2 = down_back(line, half, half, d_ffn, first_rel2, *both, part)
    i2 = Chunk(line, keep, send)
    exchange(line, over_y, OTHER, d2)
    exchange(line, over(X), HALF, i1)

    d_mixed, d_att, d_att_rel, small_a = line.run(
        mixed_back_kernel,
        [full, low_shape, rel, shape((8, width))],
        (part, mixed, row(gain_attn)),
        scratch=turn,
    )
    exchange(line, over(Z0), HALF, i2)
    two_heads = (q1, k1, v1, ctx1, w_qkv, w_out, q2, k2, v2, ctx2, w_qkv2, w_out2)
    pairs = tuple(range(cols // PAIR))
    keep, send, part, bias = attend_back(
        line,
        functools.partial(attend_back_kernel, pairs[:-1], 0),
        cols - PAIR,
        0,
        two_heads,
        (d_att, d_att_rel, x_rel1, d_mixed),
    )
    q1 = Chunk(line, keep, send)
    second_theirs = line.here(second_theirs)
    line.after(second_theirs)
    keep, send, g_in, _ = attend_back(
        line,
        functools.partial(attend_back_last_kernel, X_FIRST, pairs[-1:]),
        PAIR,
        128,
        two_heads,
        (d_att, d_att_rel, x_rel1, part),
        (small_a, small_f, b_in1, b_in2, mll_row, bias),
        [pltpu.VMEM((BLOCKS, 16, 128), F32)],
    )
    q2 = Chunk(line, keep, send)
    exchange(line, over_y, OTHER, q1)
    exchange(line, over(X), HALF, d1)
    exchange(line, over(Z0), HALF, i1)
    line.post()
    exchange(line, over(Z0), HALF, d2)
    exchange(line, over(X), HALF, q2)
    exchange(line, over(Z1), HALF, d1)
    exchange(line, over(X), HALF, i2)
    exchange(line, over_y, OTHER, i1)
    exchange(line, over_y, OTHER, q2)
    exchange(line, over(X), HALF, q1)
    layer_out = place(line, second, second_theirs, BF16)
    exchange(line, over(X), HALF, d2)
    exchange(line, over(Z1), HALF, i1)
    exchange(line, over_y, OTHER, d1)
    exchange(line, over_y, OTHER, i2)
    exchange(line, over(Z0), HALF, q2)
    grad_theirs = over_y(line.here(g_in))
    exchange(line, over(Z0), HALF, q1)
    exchange(line, over(Z1), HALF, i2)
    exchange(line, over(Z1), HALF, q2)
    exchange(line, over(Z1), HALF, d2)
    exchange(line, over(Z1), HALF, q1)
    for chunk in (i1, d1, d2, i2):
        chunk.take()
    g_in1 = jnp.concatenate([i1.result(), i2.result()], 1)
    g_down1, g_down2 = d1.result(), d2.result()
    line.last = []
    q2.take()
    q1.take()
    g_q, g_q2 = q1.result(), q2.result()
    grad_in = place(line, g_in, line.here(grad_theirs), F32)

    rest = devices // BLOCKS
    misc = g_q2[:, 4 * PAIR :]
    if rest > 1:
        misc = lax.psum(misc, "batch", axis_index_groups=groups_of(rest))

    def mine(line_number, total):
        few = total // devices
        values = misc[line_number, : total // BLOCKS]
        return values if rest == 1 else lax.dynamic_slice_in_dim(values, here % rest * few, few, 0)

    vectors = [mine(k, width) for k in range(8)]
    n = cols - PAIR

    def joined(c):
        parts = [g_q[:, c * n : (c + 1) * n], g_q2[:, c * PAIR : (c + 1) * PAIR]]
        return last_rows(jnp.concatenate(parts, 1))

    g_down = jnp.concatenate([last_rows(g_down1[:, :half]).T, last_rows(g_down2).T])
    return (
        misc[9, :n_queries],
        layer_out,
        grad_in,
        jnp.stack([joined(c) for c in range(3)]),
        jnp.stack([mine(10, cols), mine(11, cols)]),
        joined(3).T,
        vectors[0],
        vectors[1],
        vectors[2],
        last_rows(g_in1),
        mine(8, hidden),
        g_down,
        vectors[3],
        vectors[4],
        vectors[5],
        last_rows(g_down1[:, half:]),
        jnp.stack(vectors[6:8], 1),
    )


def solution(mesh):
    return jax.shard_map(
        on_device,
        mesh=mesh,
        in_specs=(
            P("batch", None),
            P("batch", None),
            P("batch"),
            P("batch", None),
            P(),
            P(None, None, "mp"),
            P(None, "mp"),
            P("mp", None),
            P(),
            P(),
            P(),
            P(None, "mp"),
            P("mp"),
            P("mp", None),
            P(),
            P(),
            P(),
            P(),
            P(),
        ),
        out_specs=(
            P(),
            P("batch", None),
            P("batch", None),
            P(None, "batch", "mp"),
            P(None, ("mp", "batch")),
            P("mp", "batch"),
            P("batch"),
            P("batch"),
            P("batch"),
            P("batch", "mp"),
            P(("mp", "batch")),
            P("mp", "batch"),
            P("batch"),
            P("batch"),
            P("batch"),
            P("batch", None),
            P("batch", None),
        ),
        check_vma=False,
    )
```

```python
import functools

import jax
import jax.numpy as jnp
from jax import lax
from jax.experimental import pallas as pl
from jax.experimental.pallas import tpu as pltpu
from jax.sharding import PartitionSpec as P

HEAD_DIM = 64
PAIR = 2 * HEAD_DIM
SEQ = 288
SLOTS = 8
BLOCKS = 16
CORE, X, Z0, Z1 = 1, 2, 4, 8
EPS = 1e-05
FLOOR = -1e30
F32 = jnp.float32
BF16 = jnp.bfloat16
HIGHEST = lax.Precision.HIGHEST
LIMIT = 16
X_FIRST = (CORE, X, Z0, Z1)
Z_FIRST = (CORE, Z0, X, Z1)
Y = 0
ROUTES = {
    "d1": (X, Y, Z0, Z1),
    "d2": (Z0, X, Y, Z1),
    "i1": (Y, Z0, X, Z1),
    "i2": (Z0, Y, X, Z1),
    "q1": (X, Z0, Z1, Y),
    "q2": (Y, X, Z0, Z1),
}
PLAN = (
    "l", "D1", "cd1", "D2", "cd2", "I1", "d1", "d2", "ci1", "post",
    "I2", "ci2", "i1", "M", "i2", "Q1", "cq1", "d2", "d1", "L",
    "Q2", "cq2", "q1", "i1", "d2", "post", "q2", "i2", "d1", "d2",
    "i1", "d1", "q1", "g", "post", "q2", "i1", "place", "i2", "q1",
    "q2", "i2", "q2", "q1", "G",
)


def rows_of(chunk):
    route = ROUTES[chunk]
    return X_FIRST if route.index(X) < route.index(Z0) else Z_FIRST


def orders_of(*chunks):
    return tuple(sorted({rows_of(c) for c in chunks}))

SCALE = HEAD_DIM ** (-0.5)
HALF, OTHER, ALL = 0, 1, 2

VMEM = pl.BlockSpec(memory_space=pltpu.VMEM)
SMEM = pl.BlockSpec(memory_space=pltpu.SMEM)


def across(v, mask):
    n = lax.axis_size("batch")
    return lax.ppermute(v, "batch", [(i, i ^ mask) for i in range(n)])


def over_y(v):
    return lax.ppermute(v, "mp", [(0, 1), (1, 0)])


def bit_mask(bit):
    return bit * (lax.axis_size("batch") // BLOCKS)


def shape(dims, dtype=F32):
    return jax.ShapeDtypeStruct(dims, dtype)


def cost(flops, moved, exps=0):
    return pl.CostEstimate(flops=int(flops), bytes_accessed=int(moved), transcendentals=int(exps))


class Line:
    def __init__(self, pos):
        self.pos = pos
        self.last = []
        self.token = pos

    def after(self, *arrays):
        self.last = self.last + list(arrays)
        self.token = arrays[-1]

    def post(self):
        def kernel(pos, out_ref):
            out_ref[...] = jnp.zeros(out_ref.shape, F32)

        self.run(kernel, [jax.ShapeDtypeStruct((8, 128), F32)], (), flops=1e12)

    def here(self, array):
        return lax.optimization_barrier((array, self.token))[0]

    def run(self, kernel, outs, args, specs=None, scratch=(), flops=0):
        n, extra = len(args), self.last
        params = pltpu.CompilerParams(vmem_limit_bytes=LIMIT * 2**20)

        def body(pos, *refs):
            kernel(pos, *refs[:n], *refs[n + len(extra) :])

        unread = [pl.BlockSpec(memory_space=pl.ANY)] * len(extra)
        if specs is None:
            small = [SMEM if a.dtype == jnp.int32 else VMEM for a in args]
            how = {
                "in_specs": [SMEM] + small + unread,
                "out_specs": (VMEM,) * len(outs),
                "scratch_shapes": list(scratch),
            }
        else:
            how = {
                "grid_spec": pltpu.PrefetchScalarGridSpec(
                    num_scalar_prefetch=1,
                    grid=(1,),
                    in_specs=[whole(a) if spec is None else spec for a, spec in zip(args, specs)]
                    + unread,
                    out_specs=tuple(whole(o) for o in outs),
                    scratch_shapes=list(scratch),
                )
            }
        results = pl.pallas_call(
            body,
            out_shape=tuple(outs),
            compiler_params=params,
            cost_estimate=cost(1e11, 1e8),
            **how,
        )(self.pos, *args, *extra)
        self.last = [min(results, key=lambda r: r.size)]
        self.token = self.last[0]
        return results


def whole(a):
    return pl.BlockSpec(a.shape, lambda *_: (0,) * len(a.shape))


def dot(a, b, precision=None):
    return jnp.dot(a, b, precision=precision, preferred_element_type=F32)


def dot_nt(a, b, precision=None):
    return lax.dot_general(
        a, b, (((1,), (1,)), ((), ())), precision=precision, preferred_element_type=F32
    )


def dot_tn(a, b):
    return lax.dot_general(a, b, (((0,), (0,)), ((), ())), preferred_element_type=F32)


def pack_attn_kernel(pos, qkv_ref, out_ref, bqv_ref, bin_ref, a_ref):
    n, cols = qkv_ref.shape
    m = out_ref.shape[0]
    a_ref[:n, :] = qkv_ref[...].astype(F32)
    a_ref[n : n + m, :] = out_ref[:, :cols].astype(F32)
    a_ref[n + m : n + 2 * m, :] = out_ref[:, cols:].astype(F32)
    at = n + 2 * m
    a_ref[at : at + 8, :] = jnp.zeros((8, cols), F32)
    a_ref[at : at + 2, :] = bqv_ref[...]
    for k in range(bin_ref.shape[1] // cols):
        a_ref[at + 2 + k : at + 3 + k, :] = bin_ref[:, k * cols : (k + 1) * cols]


def eighth_of(w, place):
    return pl.BlockSpec((w.shape[0] // 8, w.shape[1]), lambda i, pos: (pos[place], 0))


def pack_attn(line, qkv, w_out, b_qv, b_in, place):
    rows = qkv.shape[0] // 8 + w_out.shape[0] // 4 + 8
    specs = [eighth_of(qkv, place), eighth_of(w_out, place), None, None]
    outs = [shape((rows, qkv.shape[1]))]
    return line.run(pack_attn_kernel, outs, (qkv, w_out, b_qv, b_in), specs)[0]


def pack_in_kernel(pos, in_ref, b_ref):
    r, wide = in_ref.shape[0], b_ref.shape[1]
    b_ref[:r, :] = in_ref[:, :wide].astype(F32)
    b_ref[r:, :] = in_ref[:, wide:].astype(F32)


def pack_in(line, w, place):
    outs = [shape((w.shape[0] // 4, w.shape[1] // 2))]
    return line.run(pack_in_kernel, outs, (w,), [eighth_of(w, place)])[0]


def pack_down_kernel(pos, down_ref, c_ref):
    c_ref[...] = down_ref[...].astype(F32)


def pack_down(line, w, place):
    outs = [shape((w.shape[0] // 8, w.shape[1]))]
    return line.run(pack_down_kernel, outs, (w,), [eighth_of(w, place)])[0]


def unpack_attn_kernel(order, pos, *refs):
    qkv_ref, out_ref, bqv_ref, bin_ref = refs[-4:]
    n, m = qkv_ref.shape[0] // 8, out_ref.shape[0] // 8
    cols = qkv_ref.shape[1]
    for r, ref, at in pieces(order, refs[:-4], n + 2 * m + 8):
        place = r ^ pos[2]
        to = pl.ds(pl.multiple_of(place * n, 16), n)
        qkv_ref[to, :] = ref[at : at + n, :].astype(BF16)
        to = pl.ds(pl.multiple_of(place * m, 16), m)
        out_ref[to, :cols] = ref[at + n : at + n + m, :].astype(BF16)
        out_ref[to, cols:] = ref[at + n + m : at + n + 2 * m, :].astype(BF16)
    first = refs[0]
    at = n + 2 * m
    bqv_ref[...] = first[at : at + 2, :]
    for k in range(bin_ref.shape[1] // cols):
        bin_ref[:, k * cols : (k + 1) * cols] = first[at + 2 + k : at + 3 + k, :]


def unpack_in_kernel(order, pos, *refs):
    in_ref = refs[-1]
    n = in_ref.shape[0] // 8
    wide = in_ref.shape[1] // 2
    for r, ref, at in pieces(order, refs[:-1], 2 * n):
        to = pl.ds(pl.multiple_of((r ^ pos[2]) * n, 16), n)
        in_ref[to, :wide] = ref[at : at + n, :].astype(BF16)
        in_ref[to, wide:] = ref[at + n : at + 2 * n, :].astype(BF16)


def unpack_down_kernel(order, pos, *refs):
    down_ref = refs[-1]
    m = down_ref.shape[0] // 8
    for r, ref, at in pieces(order, refs[:-1], m):
        to = pl.ds(pl.multiple_of((r ^ pos[2]) * m, 16), m)
        down_ref[to, :] = ref[at : at + m, :].astype(BF16)


class Pieces:
    def __init__(self, line):
        self.line = line
        self.parts, self.order = [], []

    def add(self, arrays, order):
        arrays = [self.line.here(a) for a in arrays]
        both = arrays[0] if len(arrays) == 1 else jnp.concatenate(arrays)
        self.line.after(both)
        self.parts = self.parts + [both, across(both, bit_mask(CORE))]
        self.order = self.order + order + [r | CORE for r in order]


def pieces(order, refs, rows):
    at = 0
    for ref in refs:
        for k in range(ref.shape[0] // rows):
            yield order[at], ref, k * rows
            at += 1


def place_kernel(pos, mine_ref, theirs_ref, out_ref):
    rows = mine_ref.shape[0]
    at = pl.multiple_of(pos[0] * rows, rows)
    out_ref[pl.ds(at, rows), :] = mine_ref[...].astype(out_ref.dtype)
    at = pl.multiple_of((1 - pos[0]) * rows, rows)
    out_ref[pl.ds(at, rows), :] = theirs_ref[...].astype(out_ref.dtype)


def place(line, mine, theirs, dtype):
    rows, width = mine.shape
    return line.run(place_kernel, [shape((2 * rows, width), dtype)], (mine, theirs))[0]


def row_order(bits):
    order = []
    for p in range(BLOCKS):
        r = 0
        for k, bit in enumerate(bits):
            if (p >> (len(bits) - 1 - k)) & 1:
                r |= bit
        order.append(r)
    return order


def store_relative(a, me, scratch, *places):
    scratch[...] = a.T
    for bits, out_ref in places:
        n = out_ref.shape[0] // BLOCKS
        for p, r in enumerate(row_order(bits)):
            at = pl.multiple_of((r ^ me) * n, 16)
            out_ref[p * n : (p + 1) * n, :] = scratch[pl.ds(at, n), :]


def own_rows(pos, ref):
    rows = ref.shape[0] // 2
    return ref[pl.ds(pl.multiple_of(pos[0] * rows, 16), rows), :]


def summed(terms):
    result = terms[0]
    for t in terms[1:]:
        result = result + t
    return result


class Arrival:
    def __init__(self, line, array):
        self.line, self.array, self.waited = line, array, False

    def get(self):
        if not self.waited:
            self.array, self.waited = self.line.here(self.array), True
        return self.array


class Chunk:
    def __init__(self, line, keep, send):
        self.line, self.terms = line, [keep]
        self.n, self.cols = keep.shape[1], keep.shape[2]
        self.heads = keep.shape[0]
        self.sent = send
        self.pending = None

    def start(self):
        sent = across(self.line.here(self.sent), bit_mask(CORE))
        self.pending = (Arrival(self.line, sent), 0)

    def take(self):
        if self.pending:
            arrival, at = self.pending
            self.terms = self.terms + [arrival.get()[:, :, at : at + self.cols]]
            self.pending = None

    def give(self, what):
        self.take()
        if what == HALF:
            half = self.n // 2
            piece = summed([t[: self.heads, half : self.n] for t in self.terms])
            self.n = half
        elif what == OTHER:
            piece = summed([t[1:2, : self.n] for t in self.terms])
            self.heads = 1
        else:
            piece = summed([t[:1, : self.n] for t in self.terms])
        return piece

    def result(self, *more):
        return summed([t[0, : self.n] for t in [*self.terms, *more]])


def exchange(line, move, what, *chunks):
    pieces = [c.give(what) for c in chunks]
    sent = pieces[0] if len(pieces) == 1 else jnp.concatenate(pieces, 2)
    line.after(sent)
    arrival = Arrival(line, move(sent))
    at = 0
    for c in chunks:
        c.pending = (arrival, at)
        at += c.cols
    return arrival


def over(bit):
    return lambda v: across(v, bit_mask(bit))


def groups_of(rest):
    return [[g * rest + k for k in range(rest)] for g in range(BLOCKS)]


def last_rows(v):
    rest = lax.axis_size("batch") // BLOCKS
    if rest == 1:
        return v
    groups = groups_of(rest)
    return lax.psum_scatter(v, "batch", scatter_dimension=0, axis_index_groups=groups, tiled=True)


def norm(v):
    centre = v - jnp.mean(v, -1, keepdims=True)
    inverse = lax.rsqrt(jnp.mean(centre * centre, -1, keepdims=True) + EPS)
    return centre * inverse, inverse


def norm_back(grad, normed, inverse, gain):
    scaled = grad * gain
    return inverse * (
        scaled
        - jnp.mean(scaled, -1, keepdims=True)
        - normed * jnp.mean(scaled * normed, -1, keepdims=True)
    )


def column_sum(v):
    return jnp.sum(v, 0, keepdims=True)


def head_masks():
    lane = lax.broadcasted_iota(jnp.int32, (1, PAIR), 1)
    first = jnp.where(lane < HEAD_DIM, 1.0, 0.0)
    return lane < HEAD_DIM, (first.astype(BF16), (1.0 - first).astype(BF16))


def attend(x, w_ref, b_ref, wo_ref, q_ref, k_ref, v_ref, ctx_ref):
    q_ref[...] = (dot(x, w_ref[0]) + b_ref[0:1, :]).astype(BF16)
    k_ref[...] = dot(x, w_ref[1]).astype(BF16)
    v_ref[...] = (dot(x, w_ref[2]) + b_ref[1:2, :]).astype(BF16)
    is_first, masks = head_masks()
    for s in range(q_ref.shape[0] // SEQ):
        at = slice(s * SEQ, (s + 1) * SEQ)
        for p in range(q_ref.shape[1] // PAIR):
            lanes = slice(p * PAIR, (p + 1) * PAIR)
            q, k, v = q_ref[at, lanes] * SCALE, k_ref[at, lanes], v_ref[at, lanes]
            results = []
            for mask in masks:
                scores = dot_nt(q * mask, k)
                e = jnp.exp(scores - jnp.max(scores, -1, keepdims=True))
                probs = (e * (1.0 / jnp.sum(e, -1, keepdims=True))).astype(BF16)
                results.append(dot(probs, v))
            ctx_ref[at, lanes] = jnp.where(is_first, *results).astype(BF16)
    return dot(ctx_ref[...], wo_ref[...])


def attend_own_kernel(pos, x_ref, w_ref, b_ref, wo_ref, q_ref, k_ref, v_ref, ctx_ref, part_ref, *refs):
    *rel_refs, scratch = refs
    x = own_rows(pos, x_ref)
    store_relative(x, pos[1], scratch, *zip(orders_of("q1", "q2"), rel_refs))
    part_ref[...] = attend(x, w_ref, b_ref, wo_ref, q_ref, k_ref, v_ref, ctx_ref)


def attend_other_kernel(
    pos,
    x_ref,
    w_ref,
    b_ref,
    wo_ref,
    part_ref,
    bias_ref,
    gain_ref,
    shift_ref,
    down_ref,
    q_ref,
    k_ref,
    v_ref,
    ctx_ref,
    mixed_ref,
    base_ref,
    low_ref,
    *refs,
):
    *rel_refs, scratch = refs
    x = own_rows(pos, x_ref)
    part = attend(x, w_ref, b_ref, wo_ref, q_ref, k_ref, v_ref, ctx_ref)
    mixed = x.astype(F32) + (part_ref[...] + part) + bias_ref[...]
    mixed_ref[...] = mixed
    first = norm(mixed)[0] * gain_ref[...] + shift_ref[...]
    base_ref[...] = first + down_ref[...]
    low = first.astype(BF16)
    low_ref[...] = low
    store_relative(low, pos[1], scratch, *zip(orders_of("i1", "i2"), rel_refs))


def lift(low, w_in_ref, b_ref, act_ref, slope_ref, block):
    for i in range(act_ref.shape[1] // block):
        at = slice(i * block, (i + 1) * block)
        inner = dot(low, w_in_ref[:, at]) + b_ref[:, at]
        cdf = 0.5 + 0.5 * lax.erf(inner * 0.5**0.5)
        density = jnp.exp(-0.5 * inner * inner) * 0.3989422804014327
        act_ref[:, at] = (inner * cdf).astype(BF16)
        slope_ref[:, at] = cdf + inner * density


def up_kernel(block, pos, low_ref, w_in_ref, b_ref, w_down_ref, before_ref, act_ref, slope_ref, sum_ref):
    lift(low_ref[...], w_in_ref, b_ref, act_ref, slope_ref, block)
    sum_ref[...] = before_ref[...] + dot(act_ref[...], w_down_ref[...])


def up_in_kernel(block, pos, low_ref, w_in_ref, b_ref, act_ref, slope_ref):
    lift(low_ref[...], w_in_ref, b_ref, act_ref, slope_ref, block)


def up_down_kernel(pos, act_ref, w_down_ref, before_ref, sum_ref):
    sum_ref[...] = before_ref[...] + dot(act_ref[...], w_down_ref[...])


def loss_kernel(
    pos,
    pre_ref,
    answers,
    valid,
    gain_f,
    shift_f,
    span_ref,
    ret_ref,
    query_ref,
    second_ref,
    marks_ref,
    stats_ref,
):
    second = norm(pre_ref[...])[0] * gain_f[...] + shift_f[...]
    second_ref[...] = second
    q_row = query_ref[pl.ds(pos[3], 1), :]
    row = lax.broadcasted_iota(jnp.int32, (SEQ, 1), 0)
    line = lax.broadcasted_iota(jnp.int32, (8, 128), 0)
    lane = lax.broadcasted_iota(jnp.int32, (8, 128), 1)
    stats = jnp.full((8, 128), FLOOR, F32)
    slots = second.shape[0] // SEQ
    for s in range(slots):
        slot = pos[0] * slots + s
        mine = second[s * SEQ : (s + 1) * SEQ, :]
        span = jnp.zeros((1, 1), F32)
        for c in range(2):
            logits = jnp.sum(mine * span_ref[c : c + 1, :], -1, keepdims=True)
            shifted = logits - jnp.max(logits, 0, keepdims=True)
            log_probs = shifted - jnp.log(jnp.sum(jnp.exp(shifted), 0, keepdims=True))
            mark = jnp.where(row == answers[slot, c], 1.0, 0.0)
            span = span + jnp.sum(log_probs * mark, 0, keepdims=True)
            marks_ref[s * SEQ : (s + 1) * SEQ, c : c + 1] = mark - jnp.exp(log_probs)
        embed = dot(mine[:8, :], ret_ref[...], HIGHEST)[0:1, :]
        retrieval = jnp.sum(embed * q_row, -1, keepdims=True)
        live = valid[slot] > 0
        joint = jnp.where(live, retrieval + span, FLOOR)
        prior = jnp.where(live, retrieval, FLOOR)
        stats = jnp.where((line == s) & (lane == 0), joint, stats)
        stats = jnp.where((line == s) & (lane == 1), prior, stats)
    stats_ref[...] = stats


def loss_back_kernel(n_stats, pos, cot_ref, *refs):
    stats_refs = refs[:n_stats]
    (
        second_ref,
        pre_ref,
        marks_ref,
        gain_f,
        span_ref,
        ret_ref,
        query_ref,
        sum_ref,
        low_ref,
        sent_ref,
        ret_out,
        small_ref,
        mll_ref,
        *rel_refs,
        scratch,
        leads,
    ) = refs[n_stats:]
    all_stats = [ref[...] for ref in stats_refs]
    peak = jnp.max(functools.reduce(jnp.maximum, all_stats), 0, keepdims=True)
    total = jnp.sum(summed([jnp.exp(t - peak) for t in all_stats]), 0, keepdims=True)
    lse = peak + jnp.log(total)
    weight = jnp.exp(all_stats[0] - lse)
    q_row = query_ref[pl.ds(pos[3], 1), :]
    lead_grad = dot_nt(jnp.broadcast_to(q_row, (8, q_row.shape[1])), ret_ref[...], HIGHEST)
    top = lax.broadcasted_iota(jnp.int32, (8, 1), 0) == 0
    rows = cot_ref.shape[0] // 2
    slots = rows // SEQ
    small_ref[...] = jnp.zeros(small_ref.shape, F32)
    embeds = []
    for s in range(slots):
        at = slice(s * SEQ, (s + 1) * SEQ)
        post = weight[s : s + 1, 0:1]
        prior = weight[s : s + 1, 1:2]
        second = second_ref[at, :]
        sent_ref[at, :] = second
        start = pl.multiple_of(pos[0] * rows + s * SEQ, 16)
        grad = cot_ref[pl.ds(start, SEQ), :].astype(F32)
        for c in range(2):
            d_logits = -post * marks_ref[at, c : c + 1]
            grad = grad + d_logits * span_ref[c : c + 1, :]
            small_ref[3 + c : 4 + c, :] += column_sum(second * d_logits)
        sum_ref[at, :] = grad
        sum_ref[s * SEQ : s * SEQ + 8, :] += jnp.where(top, (prior - post) * lead_grad, 0.0)
        small_ref[5 + s : 6 + s, :] = second[0:1, :]
        embeds.append((prior - post) * q_row)
    leads[...] = small_ref[...].T
    n = ret_out.shape[0] // BLOCKS
    for p, r in enumerate(row_order(rows_of("d1"))):
        block = leads[pl.ds(pl.multiple_of((r ^ pos[1]) * n, 8), n), :]
        ret_out[p * n : (p + 1) * n, :] = summed(
            [block[:, 5 + s : 6 + s] * embed for s, embed in enumerate(embeds)]
        )
    grad = sum_ref[...]
    normed, inverse = norm(pre_ref[...])
    small_ref[0:1, :] = column_sum(grad * normed)
    small_ref[1:2, :] = column_sum(grad)
    d_sum = norm_back(grad, normed, inverse, gain_f[...])
    small_ref[2:3, :] = column_sum(d_sum)
    sum_ref[...] = d_sum
    low = d_sum.astype(BF16)
    low_ref[...] = low
    store_relative(low, pos[1], scratch, *zip(orders_of("d1", "d2"), rel_refs))
    lane = lax.broadcasted_iota(jnp.int32, mll_ref.shape, 1)
    mll = lse[:, 0:1] - lse[:, 1:2]
    mll_ref[...] = jnp.where(lane == pos[4], mll, 0.0)


def halves(left_ref, right, keep_ref, send_ref, index):
    half = left_ref.shape[0] // 2
    keep_ref[index] = dot(left_ref[:half, :], right)
    send_ref[index] = dot(left_ref[half:, :], right)


def product_kernel(start, block, pos, left_ref, own_ref, other_ref, *refs):
    *more, keep_ref, send_ref = refs
    at = slice(start, start + block)
    half = keep_ref.shape[1]
    for h, ref in enumerate((own_ref, other_ref)):
        halves(left_ref, ref[:, at], keep_ref, send_ref, (h, slice(None), slice(0, block)))
        for extra in more:
            keep_ref[h, :, block:] = extra[:half, :]
            send_ref[h, :, block:] = extra[half:, :]


def product(line, left, own, other, start, block, *more):
    width = left.shape[0]
    outs = [shape((2, width // 2, block + sum(m.shape[1] for m in more)))] * 2
    kernel = functools.partial(product_kernel, start, block)
    return line.run(kernel, outs, (left, own, other, *more))


def down_back_kernel(
    start,
    block,
    pos,
    low_ref,
    rel_ref,
    wd1_ref,
    wd2_ref,
    wi1_ref,
    wi2_ref,
    slope1_ref,
    slope2_ref,
    before_ref,
    keep_ref,
    send_ref,
    sum_ref,
    bias_ref,
    d_ref,
):
    low = low_ref[...]
    total = before_ref[...]
    count = keep_ref.shape[2]
    for h, (wd_ref, wi_ref, slope_ref) in enumerate(
        ((wd1_ref, wi1_ref, slope1_ref), (wd2_ref, wi2_ref, slope2_ref))
    ):
        for i in range(count // block):
            to = slice(i * block, (i + 1) * block)
            at = slice(start + i * block, start + (i + 1) * block)
            d_inner = (dot_nt(low, wd_ref[at, :]) * slope_ref[:, at]).astype(BF16)
            d_ref[:, to] = d_inner
            bias_ref[h : h + 1, to] = column_sum(d_inner.astype(F32))
            halves(rel_ref, d_inner, keep_ref, send_ref, (h, slice(None), to))
        total = total + dot_nt(d_ref[...], wi_ref[:, start : start + count])
    sum_ref[...] = total


def down_back(line, start, count, low, rel, w_down, w_in, slope, before):
    rows, width = low.shape
    block = count // 2
    return line.run(
        functools.partial(down_back_kernel, start, block),
        [
            shape((2, width // 2, count)),
            shape((2, width // 2, count)),
            shape((rows, width)),
            shape((2, count)),
        ],
        (low, rel, *w_down, *w_in, *slope, before),
        scratch=[pltpu.VMEM((rows, count), BF16)],
    )


def mixed_back_kernel(
    pos, part_ref, mixed_ref, gain_ref, mix_ref, low_ref, small_ref, *refs
):
    *rel_refs, scratch = refs
    grad = part_ref[...]
    normed, inverse = norm(mixed_ref[...])
    small_ref[...] = jnp.zeros(small_ref.shape, F32)
    small_ref[1:2, :] = column_sum(grad * normed)
    small_ref[2:3, :] = column_sum(grad)
    d_mixed = norm_back(grad, normed, inverse, gain_ref[...])
    small_ref[0:1, :] = column_sum(d_mixed)
    mix_ref[...] = d_mixed
    low = d_mixed.astype(BF16)
    low_ref[...] = low
    store_relative(low, pos[1], scratch, *zip(orders_of("q1", "q2"), rel_refs))


def head_back(pos, lanes, at, q_ref, k_ref, v_ref, dc, store):
    is_first, masks = head_masks()
    q, k, v = (r[at, lanes] for r in (q_ref, k_ref, v_ref))
    q_low, k_low = q * SCALE, k * SCALE
    d_q, d_k, d_v = [], [], []
    for mask in masks:
        scores = dot_nt(k_low * mask, q)
        e = jnp.exp(scores - jnp.max(scores, 0, keepdims=True))
        probs = e * (1.0 / jnp.sum(e, 0, keepdims=True))
        d_probs = dot_nt(v * mask, dc)
        centre = jnp.sum(d_probs * probs, 0, keepdims=True)
        d_scores = (probs * (d_probs - centre)).astype(BF16)
        d_v.append(dot(probs.astype(BF16), dc))
        d_k.append(dot(d_scores, q_low))
        d_q.append(dot_tn(d_scores, k_low))
    for c, d in enumerate((d_q, d_k, d_v)):
        store(c, jnp.where(is_first, *d).astype(BF16))


def attend_back_kernel(pairs, more, pos, *refs):
    heads = (refs[0:6], refs[6:12])
    low_ref, low_rel_ref, rel_ref, before_ref = refs[12:16]
    keep_ref, send_ref, sum_ref, bias_ref, d_ref, dc_ref = refs[16 + more : 22 + more]
    start, count = pairs[0] * PAIR, len(pairs) * PAIR
    ours = slice(start, start + count)
    total = before_ref[...]
    for h, (q_ref, k_ref, v_ref, ctx_ref, w_ref, wo_ref) in enumerate(heads):
        dc_ref[...] = dot_nt(low_ref[...], wo_ref[ours, :]).astype(BF16)
        for s in range(q_ref.shape[0] // SEQ):
            at = slice(s * SEQ, (s + 1) * SEQ)
            for p in range(len(pairs)):
                lanes = slice(start + p * PAIR, start + (p + 1) * PAIR)

                def store(c, d, at=at, p=p):
                    d_ref[at, c * count + p * PAIR : c * count + (p + 1) * PAIR] = d

                dc = dc_ref[at, p * PAIR : (p + 1) * PAIR]
                head_back(pos, lanes, at, q_ref, k_ref, v_ref, dc, store)
        d = d_ref[...]
        bias_ref[h : h + 1, :count] = column_sum(d[:, :count].astype(F32))
        bias_ref[h : h + 1, count:] = column_sum(d[:, 2 * count :].astype(F32))
        halves(rel_ref, d, keep_ref, send_ref, (h, slice(None), slice(0, 3 * count)))
        context = ctx_ref[:, ours]
        halves(low_rel_ref, context, keep_ref, send_ref, (h, slice(None), slice(3 * count, 4 * count)))
        for c in range(3):
            total = total + dot_nt(d[:, c * count : (c + 1) * count], w_ref[c][:, ours])
    sum_ref[...] = total


def attend_back_last_kernel(bits, pairs, pos, *refs):
    more = 6
    attend_back_kernel(pairs, more, pos, *refs)
    a_ref, f_ref, bin1_ref, bin2_ref, mll_ref, before_ref = refs[16 : 16 + more]
    keep_ref, send_ref, _, bias_ref = refs[16 + more : 20 + more]
    blocks = refs[-1]
    last, count = len(pairs) * PAIR, before_ref.shape[1] // 2
    vectors = jnp.concatenate([a_ref[0:3, :], f_ref[2:3, :], f_ref[0:2, :], f_ref[3:5, :]])
    n = vectors.shape[1] // BLOCKS
    half = keep_ref.shape[1]
    order = row_order(bits)
    blocks[...] = jnp.zeros(blocks.shape, F32)
    for h in range(2):
        b_in = jnp.concatenate([bin1_ref[h : h + 1, :], bin2_ref[h : h + 1, :]], 1)
        b_q = jnp.concatenate([before_ref[h : h + 1, :count], bias_ref[h : h + 1, :last]], 1)
        b_v = jnp.concatenate([before_ref[h : h + 1, count:], bias_ref[h : h + 1, last:]], 1)
        for b in range(BLOCKS):
            blocks[b, 0:8, :n] = vectors[:, b * n : (b + 1) * n]
            blocks[b, 9:10, :] = mll_ref[...]
            for k, v in ((8, b_in), (10, b_q), (11, b_v)):
                few = v.shape[1] // BLOCKS
                blocks[b, k : k + 1, :few] = v[:, b * few : (b + 1) * few]
        for ref, first in ((keep_ref, 0), (send_ref, BLOCKS // 2)):
            ref[h, :, 4 * last :] = jnp.zeros((half, 128), F32)
            for p in range(BLOCKS // 2):
                ref[h, p * n : p * n + 16, 4 * last :] = blocks[order[first + p] ^ pos[1]]


def attend_back(line, kernel, count, extra, heads, shared, small=(), scratch=()):
    rows, width = shared[-1].shape
    sent = shape((2, width // 2, 4 * count + extra))
    scratch = [pltpu.VMEM((rows, 3 * count), BF16), pltpu.VMEM((rows, count), BF16), *scratch]
    outs = [sent, sent, shape((rows, width)), shape((2, 2 * count))]
    return line.run(kernel, outs, (*heads, *shared, *small), scratch=scratch)


def on_device(
    hidden_in,
    cotangent,
    valid,
    answers,
    query_embed,
    w_qkv,
    b_qv,
    w_out,
    b_out,
    gain_attn,
    shift_attn,
    w_in,
    b_in,
    w_down,
    b_down,
    gain_ffn,
    shift_ffn,
    w_ret,
    w_span,
):
    here = lax.axis_index("batch")
    y = lax.axis_index("mp")
    devices = lax.axis_size("batch")
    me = here // (devices // BLOCKS)
    width = hidden_in.shape[1]
    rows = hidden_in.shape[0] // 2
    slots = rows // SEQ
    per_query = SLOTS // (2 * slots)
    n_queries = query_embed.shape[0]
    cols = w_qkv.shape[2]
    hidden = w_in.shape[1]
    query = here // per_query
    told = jnp.where((y == 0) & (here % per_query == 0), query, -1)
    pos = jnp.stack([y, me, me & 7, query, told, here, (me & 7) ^ (X | Z0)]).astype(jnp.int32)
    line = Line(pos)
    block = hidden // 3

    def row(v):
        return v.reshape(1, -1)

    rel = shape((width, rows), BF16)
    low_shape = shape((rows, width), BF16)
    full = shape((rows, width))
    turn = [pltpu.VMEM((width, rows), BF16)]

    qkv_flat = w_qkv.reshape(-1, cols)
    b_in_row = row(b_in)
    heads = [shape((rows, cols), BF16)] * 4
    a0 = over_y(pack_attn(line, qkv_flat, w_out, b_qv, b_in_row, 2))
    ad = over_y(pack_attn(line, qkv_flat, w_out, b_qv, b_in_row, 6))
    q1, k1, v1, ctx1, part, *x_rel = line.run(
        attend_own_kernel, heads + [full] + [rel] * len(orders_of("q1", "q2")), (hidden_in, w_qkv, b_qv, w_out), scratch=turn
    )
    f0 = over_y(pack_in(line, w_in, 2))
    line.post()
    a0 = line.here(a0)
    ax, az = across(a0, bit_mask(X)), across(a0, bit_mask(Z0))
    g0 = over_y(pack_down(line, w_down, 2))
    fd = over_y(pack_in(line, w_in, 6))
    gd = over_y(pack_down(line, w_down, 6))
    a = Pieces(line)
    a.add([a0, ad], [0, X | Z0])
    a.add([ax, az], [X, Z0])
    line.post()
    qkv2, w_out2, b_qv2, b_in2 = line.run(
        functools.partial(unpack_attn_kernel, a.order),
        [shape(qkv_flat.shape, BF16), shape(w_out.shape, BF16), shape(b_qv.shape), shape((1, hidden))],
        a.parts,
    )
    w_qkv2 = qkv2.reshape(w_qkv.shape)
    f0 = line.here(f0)
    fx, fz = across(f0, bit_mask(X)), across(f0, bit_mask(Z0))
    line.after(f0)
    line.post()
    q2, k2, v2, ctx2, mixed, base, first_low, *first_rel = line.run(
        attend_other_kernel,
        heads + [full, full, low_shape] + [rel] * len(orders_of("i1", "i2")),
        (
            hidden_in,
            w_qkv2,
            b_qv2,
            w_out2,
            part,
            row(b_out),
            row(gain_attn),
            row(shift_attn),
            row(b_down),
        ),
        scratch=turn,
    )
    act_shapes = [shape((rows, hidden), BF16), shape((rows, hidden))]
    act1, slope1, pre = line.run(
        functools.partial(up_kernel, block),
        act_shapes + [full],
        (first_low, w_in, b_in_row, w_down, base),
    )
    g0 = line.here(g0)
    line.after(g0)
    gx, gz = across(g0, bit_mask(X)), across(g0, bit_mask(Z0))
    f = Pieces(line)
    f.add([f0, fx, fz], [0, X, Z0])
    f.add([fd], [X | Z0])
    line.post()
    (w_in2,) = line.run(
        functools.partial(unpack_in_kernel, f.order), [shape(w_in.shape, BF16)], f.parts
    )
    act2, slope2 = line.run(
        functools.partial(up_in_kernel, block), act_shapes, (first_low, w_in2, b_in2)
    )
    g = Pieces(line)
    g.add([g0, gx], [0, X])
    g.add([gz, gd], [Z0, X | Z0])
    line.post()
    (w_down2,) = line.run(
        functools.partial(unpack_down_kernel, g.order), [shape(w_down.shape, BF16)], g.parts
    )
    (pre,) = line.run(up_down_kernel, [full], (act2, w_down2, pre))
    span_rows = w_span.T
    second, marks, stats = line.run(
        loss_kernel,
        [full, shape((rows, 2)), shape((8, 128))],
        (pre, answers, valid, row(gain_ffn), row(shift_ffn), span_rows, w_ret, query_embed),
    )

    all_stats = [stats, over_y(stats)]
    mask = 1
    while mask < per_query:
        all_stats = all_stats + [across(t, mask) for t in all_stats]
        mask *= 2
    d_sum, d_ffn, second_sent, ret_rel, small_f, mll_row, *d_ffn_rel = line.run(
        functools.partial(loss_back_kernel, len(all_stats)),
        [
            full,
            low_shape,
            full,
            shape((width, w_ret.shape[1])),
            shape((8, width)),
            shape((1, 128)),
        ]
        + [rel] * len(orders_of("d1", "d2")),
        (cotangent, *all_stats, second, pre, marks, row(gain_ffn), span_rows, w_ret, query_embed),
        scratch=turn + [pltpu.VMEM((width, 8), F32)],
    )
    line.post()

    half = hidden // 2
    both = (w_down, w_down2), (w_in, w_in2), (slope1, slope2)
    two_heads = (q1, k1, v1, ctx1, w_qkv, w_out, q2, k2, v2, ctx2, w_qkv2, w_out2)
    pairs = tuple(range(cols // PAIR))
    x_rel = dict(zip(orders_of("q1", "q2"), x_rel))
    first_rel = dict(zip(orders_of("i1", "i2"), first_rel))
    d_ffn_rel = dict(zip(orders_of("d1", "d2"), d_ffn_rel))
    chunks = {}
    gone = dict.fromkeys(ROUTES, 0)
    for step in PLAN:
        if step == "post":
            line.post()
        elif step == "D1":
            sent = product(line, d_ffn_rel[rows_of("d1")], act1, act2, 0, half, ret_rel)
            chunks["d1"] = Chunk(line, *sent)
        elif step == "D2":
            sent = product(line, d_ffn_rel[rows_of("d2")], act1, act2, half, half)
            chunks["d2"] = Chunk(line, *sent)
        elif step == "I1":
            *sent, part, b_in1 = down_back(line, 0, half, d_ffn, first_rel[rows_of("i1")], *both, d_sum)
            chunks["i1"] = Chunk(line, *sent)
        elif step == "I2":
            *sent, part, b_in2 = down_back(line, half, half, d_ffn, first_rel[rows_of("i2")], *both, part)
            chunks["i2"] = Chunk(line, *sent)
        elif step == "M":
            d_mixed, d_att, small_a, *d_att_rel = line.run(
                mixed_back_kernel,
                [full, low_shape, shape((8, width))] + [rel] * len(x_rel),
                (part, mixed, row(gain_attn)),
                scratch=turn,
            )
            d_att_rel = dict(zip(x_rel, d_att_rel))
        elif step == "Q1":
            rows1 = rows_of("q1")
            *sent, part, bias = attend_back(
                line,
                functools.partial(attend_back_kernel, pairs[:-1], 0),
                cols - PAIR,
                0,
                two_heads,
                (d_att, d_att_rel[rows1], x_rel[rows1], d_mixed),
            )
            chunks["q1"] = Chunk(line, *sent)
        elif step == "Q2":
            rows2 = rows_of("q2")
            *sent, g_in, _ = attend_back(
                line,
                functools.partial(attend_back_last_kernel, rows2, pairs[-1:]),
                PAIR,
                128,
                two_heads,
                (d_att, d_att_rel[rows2], x_rel[rows2], part),
                (small_a, small_f, b_in1, b_in2, mll_row, bias),
                [pltpu.VMEM((BLOCKS, 16, 128), F32)],
            )
            chunks["q2"] = Chunk(line, *sent)
        elif step.startswith("c"):
            chunks[step[1:]].start()
        elif step == "l":
            second_theirs = over_y(second_sent)
        elif step == "L":
            second_theirs = line.here(second_theirs)
            line.after(second_theirs)
        elif step == "place":
            layer_out = place(line, second, second_theirs, BF16)
        elif step == "g":
            grad_theirs = over_y(line.here(g_in))
        elif step == "G":
            grad_in = place(line, g_in, line.here(grad_theirs), F32)
        else:
            axis = ROUTES[step][gone[step]]
            gone[step] += 1
            if axis == Y:
                exchange(line, over_y, OTHER, chunks[step])
            else:
                exchange(line, over(axis), HALF, chunks[step])
    d1, d2, i1, i2, q1, q2 = chunks.values()
    for chunk in (i1, d1, d2, i2):
        chunk.take()
    g_in1 = jnp.concatenate([i1.result(), i2.result()], 1)
    g_down1, g_down2 = d1.result(), d2.result()
    line.last = []
    q2.take()
    q1.take()
    g_q, g_q2 = q1.result(), q2.result()

    rest = devices // BLOCKS
    misc = g_q2[:, 4 * PAIR :]
    if rest > 1:
        misc = lax.psum(misc, "batch", axis_index_groups=groups_of(rest))

    def mine(line_number, total):
        few = total // devices
        values = misc[line_number, : total // BLOCKS]
        return values if rest == 1 else lax.dynamic_slice_in_dim(values, here % rest * few, few, 0)

    vectors = [mine(k, width) for k in range(8)]
    n = cols - PAIR

    def joined(c):
        parts = [g_q[:, c * n : (c + 1) * n], g_q2[:, c * PAIR : (c + 1) * PAIR]]
        return last_rows(jnp.concatenate(parts, 1))

    g_down = jnp.concatenate([last_rows(g_down1[:, :half]).T, last_rows(g_down2).T])
    return (
        misc[9, :n_queries],
        layer_out,
        grad_in,
        jnp.stack([joined(c) for c in range(3)]),
        jnp.stack([mine(10, cols), mine(11, cols)]),
        joined(3).T,
        vectors[0],
        vectors[1],
        vectors[2],
        last_rows(g_in1),
        mine(8, hidden),
        g_down,
        vectors[3],
        vectors[4],
        vectors[5],
        last_rows(g_down1[:, half:]),
        jnp.stack(vectors[6:8], 1),
    )


def solution(mesh):
    return jax.shard_map(
        on_device,
        mesh=mesh,
        in_specs=(
            P("batch", None),
            P("batch", None),
            P("batch"),
            P("batch", None),
            P(),
            P(None, None, "mp"),
            P(None, "mp"),
            P("mp", None),
            P(),
            P(),
            P(),
            P(None, "mp"),
            P("mp"),
            P("mp", None),
            P(),
            P(),
            P(),
            P(),
            P(),
        ),
        out_specs=(
            P(),
            P("batch", None),
            P("batch", None),
            P(None, "batch", "mp"),
            P(None, ("mp", "batch")),
            P("mp", "batch"),
            P("batch"),
            P("batch"),
            P("batch"),
            P("batch", "mp"),
            P(("mp", "batch")),
            P("mp", "batch"),
            P("batch"),
            P("batch"),
            P("batch"),
            P("batch", None),
            P("batch", None),
        ),
        check_vma=False,
    )
```

```python
import functools

import jax
import jax.numpy as jnp
from jax import lax
from jax.experimental import pallas as pl
from jax.experimental.pallas import tpu as pltpu
from jax.sharding import PartitionSpec as P

HEAD_DIM = 64
PAIR = 2 * HEAD_DIM
SEQ = 288
SLOTS = 8
BLOCKS = 16
CORE, X, Z0, Z1 = 1, 2, 4, 8
EPS = 1e-05
FLOOR = -1e30
F32 = jnp.float32
BF16 = jnp.bfloat16
HIGHEST = lax.Precision.HIGHEST
LIMIT = 16
X_FIRST = (CORE, X, Z0, Z1)
Z_FIRST = (CORE, Z0, X, Z1)
Y = 0
ROUTES = {
    "d1": (X, Y, Z0, Z1),
    "d2": (Z0, X, Y, Z1),
    "i1": (Y, Z0, X, Z1),
    "i2": (Z0, Y, X, Z1),
    "q1": (X, Z0, Z1, Y),
    "q2": (Y, X, Z0, Z1),
}
PLAN = (
    "l", "D1", "cd1", "D2", "cd2", "I1", "d1", "d2", "ci1", "I2",
    "post", "ci2", "i1", "M", "i2", "Q1", "cq1", "d2", "d1", "L",
    "Q2", "cq2", "q1", "d2", "post", "q2", "i2", "i1", "d1", "d2",
    "i1", "d1", "q1", "g", "post", "q2", "i1", "place", "i2", "q2",
    "q1", "i2", "q2", "q1", "G",
)


def rows_of(chunk):
    route = ROUTES[chunk]
    return X_FIRST if route.index(X) < route.index(Z0) else Z_FIRST


def orders_of(*chunks):
    return tuple(sorted({rows_of(c) for c in chunks}))

SCALE = HEAD_DIM ** (-0.5)
HALF, OTHER, ALL = 0, 1, 2

VMEM = pl.BlockSpec(memory_space=pltpu.VMEM)
SMEM = pl.BlockSpec(memory_space=pltpu.SMEM)


def across(v, mask):
    n = lax.axis_size("batch")
    return lax.ppermute(v, "batch", [(i, i ^ mask) for i in range(n)])


def over_y(v):
    return lax.ppermute(v, "mp", [(0, 1), (1, 0)])


def bit_mask(bit):
    return bit * (lax.axis_size("batch") // BLOCKS)


def shape(dims, dtype=F32):
    return jax.ShapeDtypeStruct(dims, dtype)


def cost(flops, moved, exps=0):
    return pl.CostEstimate(flops=int(flops), bytes_accessed=int(moved), transcendentals=int(exps))


class Line:
    def __init__(self, pos):
        self.pos = pos
        self.last = []
        self.token = pos

    def after(self, *arrays):
        self.last = self.last + list(arrays)
        self.token = arrays[-1]

    def post(self):
        def kernel(pos, out_ref):
            out_ref[...] = jnp.zeros(out_ref.shape, F32)

        self.run(kernel, [jax.ShapeDtypeStruct((8, 128), F32)], (), flops=1e12)

    def here(self, array):
        return lax.optimization_barrier((array, self.token))[0]

    def run(self, kernel, outs, args, specs=None, scratch=(), flops=0):
        n, extra = len(args), self.last
        params = pltpu.CompilerParams(vmem_limit_bytes=LIMIT * 2**20)

        def body(pos, *refs):
            kernel(pos, *refs[:n], *refs[n + len(extra) :])

        unread = [pl.BlockSpec(memory_space=pl.ANY)] * len(extra)
        if specs is None:
            small = [SMEM if a.dtype == jnp.int32 else VMEM for a in args]
            how = {
                "in_specs": [SMEM] + small + unread,
                "out_specs": (VMEM,) * len(outs),
                "scratch_shapes": list(scratch),
            }
        else:
            how = {
                "grid_spec": pltpu.PrefetchScalarGridSpec(
                    num_scalar_prefetch=1,
                    grid=(1,),
                    in_specs=[whole(a) if spec is None else spec for a, spec in zip(args, specs)]
                    + unread,
                    out_specs=tuple(whole(o) for o in outs),
                    scratch_shapes=list(scratch),
                )
            }
        results = pl.pallas_call(
            body,
            out_shape=tuple(outs),
            compiler_params=params,
            cost_estimate=cost(1e11, 1e8),
            **how,
        )(self.pos, *args, *extra)
        self.last = [min(results, key=lambda r: r.size)]
        self.token = self.last[0]
        return results


def whole(a):
    return pl.BlockSpec(a.shape, lambda *_: (0,) * len(a.shape))


def dot(a, b, precision=None):
    return jnp.dot(a, b, precision=precision, preferred_element_type=F32)


def dot_nt(a, b, precision=None):
    return lax.dot_general(
        a, b, (((1,), (1,)), ((), ())), precision=precision, preferred_element_type=F32
    )


def dot_tn(a, b):
    return lax.dot_general(a, b, (((0,), (0,)), ((), ())), preferred_element_type=F32)


def pack_attn_kernel(pos, qkv_ref, out_ref, bqv_ref, bin_ref, a_ref):
    n, cols = qkv_ref.shape
    m = out_ref.shape[0]
    a_ref[:n, :] = qkv_ref[...].astype(F32)
    a_ref[n : n + m, :] = out_ref[:, :cols].astype(F32)
    a_ref[n + m : n + 2 * m, :] = out_ref[:, cols:].astype(F32)
    at = n + 2 * m
    a_ref[at : at + 8, :] = jnp.zeros((8, cols), F32)
    a_ref[at : at + 2, :] = bqv_ref[...]
    for k in range(bin_ref.shape[1] // cols):
        a_ref[at + 2 + k : at + 3 + k, :] = bin_ref[:, k * cols : (k + 1) * cols]


def eighth_of(w, place):
    return pl.BlockSpec((w.shape[0] // 8, w.shape[1]), lambda i, pos: (pos[place], 0))


def pack_attn(line, qkv, w_out, b_qv, b_in, place):
    rows = qkv.shape[0] // 8 + w_out.shape[0] // 4 + 8
    specs = [eighth_of(qkv, place), eighth_of(w_out, place), None, None]
    outs = [shape((rows, qkv.shape[1]))]
    return line.run(pack_attn_kernel, outs, (qkv, w_out, b_qv, b_in), specs)[0]


def pack_in_kernel(pos, in_ref, b_ref):
    r, wide = in_ref.shape[0], b_ref.shape[1]
    b_ref[:r, :] = in_ref[:, :wide].astype(F32)
    b_ref[r:, :] = in_ref[:, wide:].astype(F32)


def pack_in(line, w, place):
    outs = [shape((w.shape[0] // 4, w.shape[1] // 2))]
    return line.run(pack_in_kernel, outs, (w,), [eighth_of(w, place)])[0]


def pack_down_kernel(pos, down_ref, c_ref):
    c_ref[...] = down_ref[...].astype(F32)


def pack_down(line, w, place):
    outs = [shape((w.shape[0] // 8, w.shape[1]))]
    return line.run(pack_down_kernel, outs, (w,), [eighth_of(w, place)])[0]


def unpack_attn_kernel(order, pos, *refs):
    qkv_ref, out_ref, bqv_ref, bin_ref = refs[-4:]
    n, m = qkv_ref.shape[0] // 8, out_ref.shape[0] // 8
    cols = qkv_ref.shape[1]
    for r, ref, at in pieces(order, refs[:-4], n + 2 * m + 8):
        place = r ^ pos[2]
        to = pl.ds(pl.multiple_of(place * n, 16), n)
        qkv_ref[to, :] = ref[at : at + n, :].astype(BF16)
        to = pl.ds(pl.multiple_of(place * m, 16), m)
        out_ref[to, :cols] = ref[at + n : at + n + m, :].astype(BF16)
        out_ref[to, cols:] = ref[at + n + m : at + n + 2 * m, :].astype(BF16)
    first = refs[0]
    at = n + 2 * m
    bqv_ref[...] = first[at : at + 2, :]
    for k in range(bin_ref.shape[1] // cols):
        bin_ref[:, k * cols : (k + 1) * cols] = first[at + 2 + k : at + 3 + k, :]


def unpack_in_kernel(order, pos, *refs):
    in_ref = refs[-1]
    n = in_ref.shape[0] // 8
    wide = in_ref.shape[1] // 2
    for r, ref, at in pieces(order, refs[:-1], 2 * n):
        to = pl.ds(pl.multiple_of((r ^ pos[2]) * n, 16), n)
        in_ref[to, :wide] = ref[at : at + n, :].astype(BF16)
        in_ref[to, wide:] = ref[at + n : at + 2 * n, :].astype(BF16)


def unpack_down_kernel(order, pos, *refs):
    down_ref = refs[-1]
    m = down_ref.shape[0] // 8
    for r, ref, at in pieces(order, refs[:-1], m):
        to = pl.ds(pl.multiple_of((r ^ pos[2]) * m, 16), m)
        down_ref[to, :] = ref[at : at + m, :].astype(BF16)


class Pieces:
    def __init__(self, line):
        self.line = line
        self.parts, self.order = [], []

    def add(self, arrays, order):
        arrays = [self.line.here(a) for a in arrays]
        both = arrays[0] if len(arrays) == 1 else jnp.concatenate(arrays)
        self.line.after(both)
        self.parts = self.parts + [both, across(both, bit_mask(CORE))]
        self.order = self.order + order + [r | CORE for r in order]


def pieces(order, refs, rows):
    at = 0
    for ref in refs:
        for k in range(ref.shape[0] // rows):
            yield order[at], ref, k * rows
            at += 1


def place_kernel(pos, mine_ref, theirs_ref, out_ref):
    rows = mine_ref.shape[0]
    at = pl.multiple_of(pos[0] * rows, rows)
    out_ref[pl.ds(at, rows), :] = mine_ref[...].astype(out_ref.dtype)
    at = pl.multiple_of((1 - pos[0]) * rows, rows)
    out_ref[pl.ds(at, rows), :] = theirs_ref[...].astype(out_ref.dtype)


def place(line, mine, theirs, dtype):
    rows, width = mine.shape
    return line.run(place_kernel, [shape((2 * rows, width), dtype)], (mine, theirs))[0]


def row_order(bits):
    order = []
    for p in range(BLOCKS):
        r = 0
        for k, bit in enumerate(bits):
            if (p >> (len(bits) - 1 - k)) & 1:
                r |= bit
        order.append(r)
    return order


def store_relative(a, me, scratch, *places):
    scratch[...] = a.T
    for bits, out_ref in places:
        n = out_ref.shape[0] // BLOCKS
        for p, r in enumerate(row_order(bits)):
            at = pl.multiple_of((r ^ me) * n, 16)
            out_ref[p * n : (p + 1) * n, :] = scratch[pl.ds(at, n), :]


def own_rows(pos, ref):
    rows = ref.shape[0] // 2
    return ref[pl.ds(pl.multiple_of(pos[0] * rows, 16), rows), :]


def summed(terms):
    result = terms[0]
    for t in terms[1:]:
        result = result + t
    return result


class Arrival:
    def __init__(self, line, array):
        self.line, self.array, self.waited = line, array, False

    def get(self):
        if not self.waited:
            self.array, self.waited = self.line.here(self.array), True
        return self.array


class Chunk:
    def __init__(self, line, keep, send):
        self.line, self.terms = line, [keep]
        self.n, self.cols = keep.shape[1], keep.shape[2]
        self.heads = keep.shape[0]
        self.sent = send
        self.pending = None

    def start(self):
        sent = across(self.line.here(self.sent), bit_mask(CORE))
        self.pending = (Arrival(self.line, sent), 0)

    def take(self):
        if self.pending:
            arrival, at = self.pending
            self.terms = self.terms + [arrival.get()[:, :, at : at + self.cols]]
            self.pending = None

    def give(self, what):
        self.take()
        if what == HALF:
            half = self.n // 2
            piece = summed([t[: self.heads, half : self.n] for t in self.terms])
            self.n = half
        elif what == OTHER:
            piece = summed([t[1:2, : self.n] for t in self.terms])
            self.heads = 1
        else:
            piece = summed([t[:1, : self.n] for t in self.terms])
        return piece

    def result(self, *more):
        return summed([t[0, : self.n] for t in [*self.terms, *more]])


def exchange(line, move, what, *chunks):
    pieces = [c.give(what) for c in chunks]
    sent = pieces[0] if len(pieces) == 1 else jnp.concatenate(pieces, 2)
    line.after(sent)
    arrival = Arrival(line, move(sent))
    at = 0
    for c in chunks:
        c.pending = (arrival, at)
        at += c.cols
    return arrival


def over(bit):
    return lambda v: across(v, bit_mask(bit))


def groups_of(rest):
    return [[g * rest + k for k in range(rest)] for g in range(BLOCKS)]


def last_rows(v):
    rest = lax.axis_size("batch") // BLOCKS
    if rest == 1:
        return v
    groups = groups_of(rest)
    return lax.psum_scatter(v, "batch", scatter_dimension=0, axis_index_groups=groups, tiled=True)


def norm(v):
    centre = v - jnp.mean(v, -1, keepdims=True)
    inverse = lax.rsqrt(jnp.mean(centre * centre, -1, keepdims=True) + EPS)
    return centre * inverse, inverse


def norm_back(grad, normed, inverse, gain):
    scaled = grad * gain
    return inverse * (
        scaled
        - jnp.mean(scaled, -1, keepdims=True)
        - normed * jnp.mean(scaled * normed, -1, keepdims=True)
    )


def column_sum(v):
    return jnp.sum(v, 0, keepdims=True)


def head_masks():
    lane = lax.broadcasted_iota(jnp.int32, (1, PAIR), 1)
    first = jnp.where(lane < HEAD_DIM, 1.0, 0.0)
    return lane < HEAD_DIM, (first.astype(BF16), (1.0 - first).astype(BF16))


def both_heads(a, masks):
    return jnp.concatenate([a * mask for mask in masks])


def attend(x, w_ref, b_ref, wo_ref, q_ref, k_ref, v_ref, ctx_ref):
    q_ref[...] = (dot(x, w_ref[0]) + b_ref[0:1, :]).astype(BF16)
    k_ref[...] = dot(x, w_ref[1]).astype(BF16)
    v_ref[...] = (dot(x, w_ref[2]) + b_ref[1:2, :]).astype(BF16)
    is_first, masks = head_masks()
    for s in range(q_ref.shape[0] // SEQ):
        at = slice(s * SEQ, (s + 1) * SEQ)
        for p in range(q_ref.shape[1] // PAIR):
            lanes = slice(p * PAIR, (p + 1) * PAIR)
            q, k, v = q_ref[at, lanes] * SCALE, k_ref[at, lanes], v_ref[at, lanes]
            scores = dot_nt(both_heads(q, masks), k)
            e = jnp.exp(scores - jnp.max(scores, -1, keepdims=True))
            probs = (e * (1.0 / jnp.sum(e, -1, keepdims=True))).astype(BF16)
            context = dot(probs, v)
            ctx_ref[at, lanes] = jnp.where(is_first, context[:SEQ], context[SEQ:]).astype(BF16)
    return dot(ctx_ref[...], wo_ref[...])


def attend_own_kernel(pos, x_ref, w_ref, b_ref, wo_ref, q_ref, k_ref, v_ref, ctx_ref, part_ref, *refs):
    *rel_refs, scratch = refs
    x = own_rows(pos, x_ref)
    store_relative(x, pos[1], scratch, *zip(orders_of("q1", "q2"), rel_refs))
    part_ref[...] = attend(x, w_ref, b_ref, wo_ref, q_ref, k_ref, v_ref, ctx_ref)


def attend_other_kernel(
    pos,
    x_ref,
    w_ref,
    b_ref,
    wo_ref,
    part_ref,
    bias_ref,
    gain_ref,
    shift_ref,
    down_ref,
    q_ref,
    k_ref,
    v_ref,
    ctx_ref,
    mixed_ref,
    base_ref,
    low_ref,
    *refs,
):
    *rel_refs, scratch = refs
    x = own_rows(pos, x_ref)
    part = attend(x, w_ref, b_ref, wo_ref, q_ref, k_ref, v_ref, ctx_ref)
    mixed = x.astype(F32) + (part_ref[...] + part) + bias_ref[...]
    mixed_ref[...] = mixed
    first = norm(mixed)[0] * gain_ref[...] + shift_ref[...]
    base_ref[...] = first + down_ref[...]
    low = first.astype(BF16)
    low_ref[...] = low
    store_relative(low, pos[1], scratch, *zip(orders_of("i1", "i2"), rel_refs))


def lift(low, w_in_ref, b_ref, act_ref, slope_ref, block):
    for i in range(act_ref.shape[1] // block):
        at = slice(i * block, (i + 1) * block)
        inner = dot(low, w_in_ref[:, at]) + b_ref[:, at]
        cdf = 0.5 + 0.5 * lax.erf(inner * 0.5**0.5)
        density = jnp.exp(-0.5 * inner * inner) * 0.3989422804014327
        act_ref[:, at] = (inner * cdf).astype(BF16)
        slope_ref[:, at] = cdf + inner * density


def up_kernel(block, pos, low_ref, w_in_ref, b_ref, w_down_ref, before_ref, act_ref, slope_ref, sum_ref):
    lift(low_ref[...], w_in_ref, b_ref, act_ref, slope_ref, block)
    sum_ref[...] = before_ref[...] + dot(act_ref[...], w_down_ref[...])


def up_in_kernel(block, pos, low_ref, w_in_ref, b_ref, act_ref, slope_ref):
    lift(low_ref[...], w_in_ref, b_ref, act_ref, slope_ref, block)


def up_down_kernel(pos, act_ref, w_down_ref, before_ref, sum_ref):
    sum_ref[...] = before_ref[...] + dot(act_ref[...], w_down_ref[...])


def loss_kernel(
    pos,
    pre_ref,
    answers,
    valid,
    gain_f,
    shift_f,
    span_ref,
    ret_ref,
    query_ref,
    second_ref,
    marks_ref,
    stats_ref,
):
    second = norm(pre_ref[...])[0] * gain_f[...] + shift_f[...]
    second_ref[...] = second
    q_row = query_ref[pl.ds(pos[3], 1), :]
    row = lax.broadcasted_iota(jnp.int32, (SEQ, 1), 0)
    line = lax.broadcasted_iota(jnp.int32, (8, 128), 0)
    lane = lax.broadcasted_iota(jnp.int32, (8, 128), 1)
    stats = jnp.full((8, 128), FLOOR, F32)
    slots = second.shape[0] // SEQ
    for s in range(slots):
        slot = pos[0] * slots + s
        mine = second[s * SEQ : (s + 1) * SEQ, :]
        span = jnp.zeros((1, 1), F32)
        for c in range(2):
            logits = jnp.sum(mine * span_ref[c : c + 1, :], -1, keepdims=True)
            shifted = logits - jnp.max(logits, 0, keepdims=True)
            log_probs = shifted - jnp.log(jnp.sum(jnp.exp(shifted), 0, keepdims=True))
            mark = jnp.where(row == answers[slot, c], 1.0, 0.0)
            span = span + jnp.sum(log_probs * mark, 0, keepdims=True)
            marks_ref[s * SEQ : (s + 1) * SEQ, c : c + 1] = mark - jnp.exp(log_probs)
        embed = dot(mine[:8, :], ret_ref[...], HIGHEST)[0:1, :]
        retrieval = jnp.sum(embed * q_row, -1, keepdims=True)
        live = valid[slot] > 0
        joint = jnp.where(live, retrieval + span, FLOOR)
        prior = jnp.where(live, retrieval, FLOOR)
        stats = jnp.where((line == s) & (lane == 0), joint, stats)
        stats = jnp.where((line == s) & (lane == 1), prior, stats)
    stats_ref[...] = stats


def loss_back_kernel(n_stats, pos, cot_ref, *refs):
    stats_refs = refs[:n_stats]
    (
        second_ref,
        pre_ref,
        marks_ref,
        gain_f,
        span_ref,
        ret_ref,
        query_ref,
        sum_ref,
        low_ref,
        sent_ref,
        ret_out,
        small_ref,
        mll_ref,
        *rel_refs,
        scratch,
        leads,
    ) = refs[n_stats:]
    all_stats = [ref[...] for ref in stats_refs]
    peak = jnp.max(functools.reduce(jnp.maximum, all_stats), 0, keepdims=True)
    total = jnp.sum(summed([jnp.exp(t - peak) for t in all_stats]), 0, keepdims=True)
    lse = peak + jnp.log(total)
    weight = jnp.exp(all_stats[0] - lse)
    q_row = query_ref[pl.ds(pos[3], 1), :]
    lead_grad = dot_nt(jnp.broadcast_to(q_row, (8, q_row.shape[1])), ret_ref[...], HIGHEST)
    top = lax.broadcasted_iota(jnp.int32, (8, 1), 0) == 0
    rows = cot_ref.shape[0] // 2
    slots = rows // SEQ
    small_ref[...] = jnp.zeros(small_ref.shape, F32)
    embeds = []
    for s in range(slots):
        at = slice(s * SEQ, (s + 1) * SEQ)
        post = weight[s : s + 1, 0:1]
        prior = weight[s : s + 1, 1:2]
        second = second_ref[at, :]
        sent_ref[at, :] = second
        start = pl.multiple_of(pos[0] * rows + s * SEQ, 16)
        grad = cot_ref[pl.ds(start, SEQ), :].astype(F32)
        for c in range(2):
            d_logits = -post * marks_ref[at, c : c + 1]
            grad = grad + d_logits * span_ref[c : c + 1, :]
            small_ref[3 + c : 4 + c, :] += column_sum(second * d_logits)
        sum_ref[at, :] = grad
        sum_ref[s * SEQ : s * SEQ + 8, :] += jnp.where(top, (prior - post) * lead_grad, 0.0)
        small_ref[5 + s : 6 + s, :] = second[0:1, :]
        embeds.append((prior - post) * q_row)
    leads[...] = small_ref[...].T
    n = ret_out.shape[0] // BLOCKS
    for p, r in enumerate(row_order(rows_of("d1"))):
        block = leads[pl.ds(pl.multiple_of((r ^ pos[1]) * n, 8), n), :]
        ret_out[p * n : (p + 1) * n, :] = summed(
            [block[:, 5 + s : 6 + s] * embed for s, embed in enumerate(embeds)]
        )
    grad = sum_ref[...]
    normed, inverse = norm(pre_ref[...])
    small_ref[0:1, :] = column_sum(grad * normed)
    small_ref[1:2, :] = column_sum(grad)
    d_sum = norm_back(grad, normed, inverse, gain_f[...])
    small_ref[2:3, :] = column_sum(d_sum)
    sum_ref[...] = d_sum
    low = d_sum.astype(BF16)
    low_ref[...] = low
    store_relative(low, pos[1], scratch, *zip(orders_of("d1", "d2"), rel_refs))
    lane = lax.broadcasted_iota(jnp.int32, mll_ref.shape, 1)
    mll = lse[:, 0:1] - lse[:, 1:2]
    mll_ref[...] = jnp.where(lane == pos[4], mll, 0.0)


def halves(left_ref, right, keep_ref, send_ref, index):
    half = left_ref.shape[0] // 2
    keep_ref[index] = dot(left_ref[:half, :], right)
    send_ref[index] = dot(left_ref[half:, :], right)


def product_kernel(start, block, pos, left_ref, own_ref, other_ref, *refs):
    *more, keep_ref, send_ref = refs
    at = slice(start, start + block)
    half = keep_ref.shape[1]
    for h, ref in enumerate((own_ref, other_ref)):
        halves(left_ref, ref[:, at], keep_ref, send_ref, (h, slice(None), slice(0, block)))
        for extra in more:
            keep_ref[h, :, block:] = extra[:half, :]
            send_ref[h, :, block:] = extra[half:, :]


def product(line, left, own, other, start, block, *more):
    width = left.shape[0]
    outs = [shape((2, width // 2, block + sum(m.shape[1] for m in more)))] * 2
    kernel = functools.partial(product_kernel, start, block)
    return line.run(kernel, outs, (left, own, other, *more))


def down_back_kernel(
    start,
    block,
    pos,
    low_ref,
    rel_ref,
    wd1_ref,
    wd2_ref,
    wi1_ref,
    wi2_ref,
    slope1_ref,
    slope2_ref,
    before_ref,
    keep_ref,
    send_ref,
    sum_ref,
    bias_ref,
    d_ref,
):
    low = low_ref[...]
    total = before_ref[...]
    count = keep_ref.shape[2]
    for h, (wd_ref, wi_ref, slope_ref) in enumerate(
        ((wd1_ref, wi1_ref, slope1_ref), (wd2_ref, wi2_ref, slope2_ref))
    ):
        for i in range(count // block):
            to = slice(i * block, (i + 1) * block)
            at = slice(start + i * block, start + (i + 1) * block)
            d_inner = (dot_nt(low, wd_ref[at, :]) * slope_ref[:, at]).astype(BF16)
            d_ref[:, to] = d_inner
            bias_ref[h : h + 1, to] = column_sum(d_inner.astype(F32))
            halves(rel_ref, d_inner, keep_ref, send_ref, (h, slice(None), to))
        total = total + dot_nt(d_ref[...], wi_ref[:, start : start + count])
    sum_ref[...] = total


def down_back(line, start, count, low, rel, w_down, w_in, slope, before):
    rows, width = low.shape
    block = count // 3
    return line.run(
        functools.partial(down_back_kernel, start, block),
        [
            shape((2, width // 2, count)),
            shape((2, width // 2, count)),
            shape((rows, width)),
            shape((2, count)),
        ],
        (low, rel, *w_down, *w_in, *slope, before),
        scratch=[pltpu.VMEM((rows, count), BF16)],
    )


def mixed_back_kernel(
    pos, part_ref, mixed_ref, gain_ref, mix_ref, low_ref, small_ref, *refs
):
    *rel_refs, scratch = refs
    grad = part_ref[...]
    normed, inverse = norm(mixed_ref[...])
    small_ref[...] = jnp.zeros(small_ref.shape, F32)
    small_ref[1:2, :] = column_sum(grad * normed)
    small_ref[2:3, :] = column_sum(grad)
    d_mixed = norm_back(grad, normed, inverse, gain_ref[...])
    small_ref[0:1, :] = column_sum(d_mixed)
    mix_ref[...] = d_mixed
    low = d_mixed.astype(BF16)
    low_ref[...] = low
    store_relative(low, pos[1], scratch, *zip(orders_of("q1", "q2"), rel_refs))


def head_back(pos, lanes, at, q_ref, k_ref, v_ref, dc, store):
    is_first, masks = head_masks()
    q, k, v = (r[at, lanes] for r in (q_ref, k_ref, v_ref))
    q_low, k_low = q * SCALE, k * SCALE
    k_two = both_heads(k_low, masks)
    scores = dot_nt(k_two, q)
    d_probs = dot_nt(both_heads(v, masks), dc)
    probs_two, d_scores_two = [], []
    for h in range(2):
        rows = slice(h * SEQ, (h + 1) * SEQ)
        e = jnp.exp(scores[rows] - jnp.max(scores[rows], 0, keepdims=True))
        probs = e * (1.0 / jnp.sum(e, 0, keepdims=True))
        centre = jnp.sum(d_probs[rows] * probs, 0, keepdims=True)
        d_scores_two.append((probs * (d_probs[rows] - centre)).astype(BF16))
        probs_two.append(probs.astype(BF16))
    d_scores = jnp.concatenate(d_scores_two)
    d_v = dot(jnp.concatenate(probs_two), dc)
    d_k = dot(d_scores, q_low)
    store(0, dot_tn(d_scores, k_two).astype(BF16))
    store(1, jnp.where(is_first, d_k[:SEQ], d_k[SEQ:]).astype(BF16))
    store(2, jnp.where(is_first, d_v[:SEQ], d_v[SEQ:]).astype(BF16))


def attend_back_kernel(pairs, more, pos, *refs):
    heads = (refs[0:6], refs[6:12])
    low_ref, low_rel_ref, rel_ref, before_ref = refs[12:16]
    keep_ref, send_ref, sum_ref, bias_ref, d_ref, dc_ref = refs[16 + more : 22 + more]
    start, count = pairs[0] * PAIR, len(pairs) * PAIR
    ours = slice(start, start + count)
    total = before_ref[...]
    for h, (q_ref, k_ref, v_ref, ctx_ref, w_ref, wo_ref) in enumerate(heads):
        dc_ref[...] = dot_nt(low_ref[...], wo_ref[ours, :]).astype(BF16)
        for s in range(q_ref.shape[0] // SEQ):
            at = slice(s * SEQ, (s + 1) * SEQ)
            for p in range(len(pairs)):
                lanes = slice(start + p * PAIR, start + (p + 1) * PAIR)

                def store(c, d, at=at, p=p):
                    d_ref[at, c * count + p * PAIR : c * count + (p + 1) * PAIR] = d

                dc = dc_ref[at, p * PAIR : (p + 1) * PAIR]
                head_back(pos, lanes, at, q_ref, k_ref, v_ref, dc, store)
        d = d_ref[...]
        bias_ref[h : h + 1, :count] = column_sum(d[:, :count].astype(F32))
        bias_ref[h : h + 1, count:] = column_sum(d[:, 2 * count :].astype(F32))
        halves(rel_ref, d, keep_ref, send_ref, (h, slice(None), slice(0, 3 * count)))
        context = ctx_ref[:, ours]
        halves(low_rel_ref, context, keep_ref, send_ref, (h, slice(None), slice(3 * count, 4 * count)))
        for c in range(3):
            total = total + dot_nt(d[:, c * count : (c + 1) * count], w_ref[c][:, ours])
    sum_ref[...] = total


def attend_back_last_kernel(bits, pairs, pos, *refs):
    more = 6
    attend_back_kernel(pairs, more, pos, *refs)
    a_ref, f_ref, bin1_ref, bin2_ref, mll_ref, before_ref = refs[16 : 16 + more]
    keep_ref, send_ref, _, bias_ref = refs[16 + more : 20 + more]
    blocks = refs[-1]
    last, count = len(pairs) * PAIR, before_ref.shape[1] // 2
    vectors = jnp.concatenate([a_ref[0:3, :], f_ref[2:3, :], f_ref[0:2, :], f_ref[3:5, :]])
    n = vectors.shape[1] // BLOCKS
    half = keep_ref.shape[1]
    order = row_order(bits)
    blocks[...] = jnp.zeros(blocks.shape, F32)
    for h in range(2):
        b_in = jnp.concatenate([bin1_ref[h : h + 1, :], bin2_ref[h : h + 1, :]], 1)
        b_q = jnp.concatenate([before_ref[h : h + 1, :count], bias_ref[h : h + 1, :last]], 1)
        b_v = jnp.concatenate([before_ref[h : h + 1, count:], bias_ref[h : h + 1, last:]], 1)
        for b in range(BLOCKS):
            blocks[b, 0:8, :n] = vectors[:, b * n : (b + 1) * n]
            blocks[b, 9:10, :] = mll_ref[...]
            for k, v in ((8, b_in), (10, b_q), (11, b_v)):
                few = v.shape[1] // BLOCKS
                blocks[b, k : k + 1, :few] = v[:, b * few : (b + 1) * few]
        for ref, first in ((keep_ref, 0), (send_ref, BLOCKS // 2)):
            ref[h, :, 4 * last :] = jnp.zeros((half, 128), F32)
            for p in range(BLOCKS // 2):
                ref[h, p * n : p * n + 16, 4 * last :] = blocks[order[first + p] ^ pos[1]]


def attend_back(line, kernel, count, extra, heads, shared, small=(), scratch=()):
    rows, width = shared[-1].shape
    sent = shape((2, width // 2, 4 * count + extra))
    scratch = [pltpu.VMEM((rows, 3 * count), BF16), pltpu.VMEM((rows, count), BF16), *scratch]
    outs = [sent, sent, shape((rows, width)), shape((2, 2 * count))]
    return line.run(kernel, outs, (*heads, *shared, *small), scratch=scratch)


def on_device(
    hidden_in,
    cotangent,
    valid,
    answers,
    query_embed,
    w_qkv,
    b_qv,
    w_out,
    b_out,
    gain_attn,
    shift_attn,
    w_in,
    b_in,
    w_down,
    b_down,
    gain_ffn,
    shift_ffn,
    w_ret,
    w_span,
):
    here = lax.axis_index("batch")
    y = lax.axis_index("mp")
    devices = lax.axis_size("batch")
    me = here // (devices // BLOCKS)
    width = hidden_in.shape[1]
    rows = hidden_in.shape[0] // 2
    slots = rows // SEQ
    per_query = SLOTS // (2 * slots)
    n_queries = query_embed.shape[0]
    cols = w_qkv.shape[2]
    hidden = w_in.shape[1]
    query = here // per_query
    told = jnp.where((y == 0) & (here % per_query == 0), query, -1)
    pos = jnp.stack([y, me, me & 7, query, told, here, (me & 7) ^ (X | Z0)]).astype(jnp.int32)
    line = Line(pos)
    block = hidden // 3

    def row(v):
        return v.reshape(1, -1)

    rel = shape((width, rows), BF16)
    low_shape = shape((rows, width), BF16)
    full = shape((rows, width))
    turn = [pltpu.VMEM((width, rows), BF16)]

    qkv_flat = w_qkv.reshape(-1, cols)
    b_in_row = row(b_in)
    heads = [shape((rows, cols), BF16)] * 4
    a0 = over_y(pack_attn(line, qkv_flat, w_out, b_qv, b_in_row, 2))
    ad = over_y(pack_attn(line, qkv_flat, w_out, b_qv, b_in_row, 6))
    q1, k1, v1, ctx1, part, *x_rel = line.run(
        attend_own_kernel, heads + [full] + [rel] * len(orders_of("q1", "q2")), (hidden_in, w_qkv, b_qv, w_out), scratch=turn
    )
    f0 = over_y(pack_in(line, w_in, 2))
    line.post()
    a0 = line.here(a0)
    ax, az = across(a0, bit_mask(X)), across(a0, bit_mask(Z0))
    g0 = over_y(pack_down(line, w_down, 2))
    fd = over_y(pack_in(line, w_in, 6))
    gd = over_y(pack_down(line, w_down, 6))
    a = Pieces(line)
    a.add([a0, ad], [0, X | Z0])
    a.add([ax, az], [X, Z0])
    line.post()
    qkv2, w_out2, b_qv2, b_in2 = line.run(
        functools.partial(unpack_attn_kernel, a.order),
        [shape(qkv_flat.shape, BF16), shape(w_out.shape, BF16), shape(b_qv.shape), shape((1, hidden))],
        a.parts,
    )
    w_qkv2 = qkv2.reshape(w_qkv.shape)
    f0 = line.here(f0)
    fx, fz = across(f0, bit_mask(X)), across(f0, bit_mask(Z0))
    line.after(f0)
    line.post()
    q2, k2, v2, ctx2, mixed, base, first_low, *first_rel = line.run(
        attend_other_kernel,
        heads + [full, full, low_shape] + [rel] * len(orders_of("i1", "i2")),
        (
            hidden_in,
            w_qkv2,
            b_qv2,
            w_out2,
            part,
            row(b_out),
            row(gain_attn),
            row(shift_attn),
            row(b_down),
        ),
        scratch=turn,
    )
    act_shapes = [shape((rows, hidden), BF16), shape((rows, hidden))]
    act1, slope1, pre = line.run(
        functools.partial(up_kernel, block),
        act_shapes + [full],
        (first_low, w_in, b_in_row, w_down, base),
    )
    g0 = line.here(g0)
    line.after(g0)
    gx, gz = across(g0, bit_mask(X)), across(g0, bit_mask(Z0))
    f = Pieces(line)
    f.add([f0, fx, fz], [0, X, Z0])
    f.add([fd], [X | Z0])
    line.post()
    (w_in2,) = line.run(
        functools.partial(unpack_in_kernel, f.order), [shape(w_in.shape, BF16)], f.parts
    )
    act2, slope2 = line.run(
        functools.partial(up_in_kernel, block), act_shapes, (first_low, w_in2, b_in2)
    )
    g = Pieces(line)
    g.add([g0, gx], [0, X])
    g.add([gz, gd], [Z0, X | Z0])
    line.post()
    (w_down2,) = line.run(
        functools.partial(unpack_down_kernel, g.order), [shape(w_down.shape, BF16)], g.parts
    )
    (pre,) = line.run(up_down_kernel, [full], (act2, w_down2, pre))
    span_rows = w_span.T
    second, marks, stats = line.run(
        loss_kernel,
        [full, shape((rows, 2)), shape((8, 128))],
        (pre, answers, valid, row(gain_ffn), row(shift_ffn), span_rows, w_ret, query_embed),
    )

    all_stats = [stats, over_y(stats)]
    mask = 1
    while mask < per_query:
        all_stats = all_stats + [across(t, mask) for t in all_stats]
        mask *= 2
    d_sum, d_ffn, second_sent, ret_rel, small_f, mll_row, *d_ffn_rel = line.run(
        functools.partial(loss_back_kernel, len(all_stats)),
        [
            full,
            low_shape,
            full,
            shape((width, w_ret.shape[1])),
            shape((8, width)),
            shape((1, 128)),
        ]
        + [rel] * len(orders_of("d1", "d2")),
        (cotangent, *all_stats, second, pre, marks, row(gain_ffn), span_rows, w_ret, query_embed),
        scratch=turn + [pltpu.VMEM((width, 8), F32)],
    )
    line.post()

    half = hidden // 2
    both = (w_down, w_down2), (w_in, w_in2), (slope1, slope2)
    two_heads = (q1, k1, v1, ctx1, w_qkv, w_out, q2, k2, v2, ctx2, w_qkv2, w_out2)
    pairs = tuple(range(cols // PAIR))
    x_rel = dict(zip(orders_of("q1", "q2"), x_rel))
    first_rel = dict(zip(orders_of("i1", "i2"), first_rel))
    d_ffn_rel = dict(zip(orders_of("d1", "d2"), d_ffn_rel))
    chunks = {}
    gone = dict.fromkeys(ROUTES, 0)
    for step in PLAN:
        if step == "post":
            line.post()
        elif step == "D1":
            sent = product(line, d_ffn_rel[rows_of("d1")], act1, act2, 0, half, ret_rel)
            chunks["d1"] = Chunk(line, *sent)
        elif step == "D2":
            sent = product(line, d_ffn_rel[rows_of("d2")], act1, act2, half, half)
            chunks["d2"] = Chunk(line, *sent)
        elif step == "I1":
            *sent, part, b_in1 = down_back(line, 0, half, d_ffn, first_rel[rows_of("i1")], *both, d_sum)
            chunks["i1"] = Chunk(line, *sent)
        elif step == "I2":
            *sent, part, b_in2 = down_back(line, half, half, d_ffn, first_rel[rows_of("i2")], *both, part)
            chunks["i2"] = Chunk(line, *sent)
        elif step == "M":
            d_mixed, d_att, small_a, *d_att_rel = line.run(
                mixed_back_kernel,
                [full, low_shape, shape((8, width))] + [rel] * len(x_rel),
                (part, mixed, row(gain_attn)),
                scratch=turn,
            )
            d_att_rel = dict(zip(x_rel, d_att_rel))
        elif step == "Q1":
            rows1 = rows_of("q1")
            *sent, part, bias = attend_back(
                line,
                functools.partial(attend_back_kernel, pairs[:-1], 0),
                cols - PAIR,
                0,
                two_heads,
                (d_att, d_att_rel[rows1], x_rel[rows1], d_mixed),
            )
            chunks["q1"] = Chunk(line, *sent)
        elif step == "Q2":
            rows2 = rows_of("q2")
            *sent, g_in, _ = attend_back(
                line,
                functools.partial(attend_back_last_kernel, rows2, pairs[-1:]),
                PAIR,
                128,
                two_heads,
                (d_att, d_att_rel[rows2], x_rel[rows2], part),
                (small_a, small_f, b_in1, b_in2, mll_row, bias),
                [pltpu.VMEM((BLOCKS, 16, 128), F32)],
            )
            chunks["q2"] = Chunk(line, *sent)
        elif step.startswith("t"):
            chunks[step[1:]].take()
            line.after(chunks[step[1:]].terms[-1])
        elif step.startswith("c"):
            chunks[step[1:]].start()
        elif step == "l":
            second_theirs = over_y(second_sent)
        elif step == "L":
            second_theirs = line.here(second_theirs)
            line.after(second_theirs)
        elif step == "place":
            layer_out = place(line, second, second_theirs, BF16)
        elif step == "g":
            grad_theirs = over_y(line.here(g_in))
        elif step == "G":
            grad_in = place(line, g_in, line.here(grad_theirs), F32)
        else:
            axis = ROUTES[step][gone[step]]
            gone[step] += 1
            if axis == Y:
                exchange(line, over_y, OTHER, chunks[step])
            else:
                exchange(line, over(axis), HALF, chunks[step])
    d1, d2, i1, i2, q1, q2 = chunks.values()
    for chunk in (i1, d1, d2, i2):
        chunk.take()
    g_in1 = jnp.concatenate([i1.result(), i2.result()], 1)
    g_down1, g_down2 = d1.result(), d2.result()
    line.last = []
    q2.take()
    q1.take()
    g_q, g_q2 = q1.result(), q2.result()

    rest = devices // BLOCKS
    misc = g_q2[:, 4 * PAIR :]
    if rest > 1:
        misc = lax.psum(misc, "batch", axis_index_groups=groups_of(rest))

    def mine(line_number, total):
        few = total // devices
        values = misc[line_number, : total // BLOCKS]
        return values if rest == 1 else lax.dynamic_slice_in_dim(values, here % rest * few, few, 0)

    vectors = [mine(k, width) for k in range(8)]
    n = cols - PAIR

    def joined(c):
        parts = [g_q[:, c * n : (c + 1) * n], g_q2[:, c * PAIR : (c + 1) * PAIR]]
        return last_rows(jnp.concatenate(parts, 1))

    g_down = jnp.concatenate([last_rows(g_down1[:, :half]).T, last_rows(g_down2).T])
    return (
        misc[9, :n_queries],
        layer_out,
        grad_in,
        jnp.stack([joined(c) for c in range(3)]),
        jnp.stack([mine(10, cols), mine(11, cols)]),
        joined(3).T,
        vectors[0],
        vectors[1],
        vectors[2],
        last_rows(g_in1),
        mine(8, hidden),
        g_down,
        vectors[3],
        vectors[4],
        vectors[5],
        last_rows(g_down1[:, half:]),
        jnp.stack(vectors[6:8], 1),
    )


def solution(mesh):
    return jax.shard_map(
        on_device,
        mesh=mesh,
        in_specs=(
            P("batch", None),
            P("batch", None),
            P("batch"),
            P("batch", None),
            P(),
            P(None, None, "mp"),
            P(None, "mp"),
            P("mp", None),
            P(),
            P(),
            P(),
            P(None, "mp"),
            P("mp"),
            P("mp", None),
            P(),
            P(),
            P(),
            P(),
            P(),
        ),
        out_specs=(
            P(),
            P("batch", None),
            P("batch", None),
            P(None, "batch", "mp"),
            P(None, ("mp", "batch")),
            P("mp", "batch"),
            P("batch"),
            P("batch"),
            P("batch"),
            P("batch", "mp"),
            P(("mp", "batch")),
            P("mp", "batch"),
            P("batch"),
            P("batch"),
            P("batch"),
            P("batch", None),
            P("batch", None),
        ),
        check_vma=False,
    )
```

```python
import functools

import jax
import jax.numpy as jnp
from jax import lax
from jax.experimental import pallas as pl
from jax.experimental.pallas import tpu as pltpu
from jax.sharding import PartitionSpec as P

HEAD_DIM = 64
PAIR = 2 * HEAD_DIM
SEQ = 288
SLOTS = 8
BLOCKS = 16
CORE, X, Z0, Z1 = 1, 2, 4, 8
EPS = 1e-05
FLOOR = -1e30
F32 = jnp.float32
BF16 = jnp.bfloat16
HIGHEST = lax.Precision.HIGHEST
LIMIT = 11
X_FIRST = (CORE, X, Z0, Z1)
Z_FIRST = (CORE, Z0, X, Z1)
Y = 0
ROUTES = {
    "d1": (X, Y, Z0, Z1),
    "d2": (Z0, X, Y, Z1),
    "i1": (Y, Z0, X, Z1),
    "i2": (Z0, Y, X, Z1),
    "q1": (X, Z0, Z1, Y),
    "q2": (Y, X, Z0, Z1),
}
PLAN = (
    "l", "D1", "cd1", "D2", "cd2", "I1", "d1", "d2", "ci1", "I2",
    "post", "ci2", "i1", "M", "i2", "Q1", "cq1", "d2", "d1", "L",
    "Q2", "cq2", "q1", "d2", "post", "q2", "i2", "i1", "d1", "d2",
    "i1", "d1", "q1", "g", "post", "q2", "i1", "place", "i2", "q2",
    "q1", "i2", "q2", "q1", "G",
)


def rows_of(chunk):
    route = ROUTES[chunk]
    return X_FIRST if route.index(X) < route.index(Z0) else Z_FIRST


def orders_of(*chunks):
    return tuple(sorted({rows_of(c) for c in chunks}))

SCALE = HEAD_DIM ** (-0.5)
HALF, OTHER, ALL = 0, 1, 2

VMEM = pl.BlockSpec(memory_space=pltpu.VMEM)
SMEM = pl.BlockSpec(memory_space=pltpu.SMEM)


def across(v, mask):
    n = lax.axis_size("batch")
    return lax.ppermute(v, "batch", [(i, i ^ mask) for i in range(n)])


def over_y(v):
    return lax.ppermute(v, "mp", [(0, 1), (1, 0)])


def bit_mask(bit):
    return bit * (lax.axis_size("batch") // BLOCKS)


def shape(dims, dtype=F32):
    return jax.ShapeDtypeStruct(dims, dtype)


def cost(flops, moved, exps=0):
    return pl.CostEstimate(flops=int(flops), bytes_accessed=int(moved), transcendentals=int(exps))


class Line:
    def __init__(self, pos):
        self.pos = pos
        self.last = []
        self.token = pos

    def after(self, *arrays):
        self.last = self.last + list(arrays)
        self.token = arrays[-1]

    def post(self):
        def kernel(pos, out_ref):
            out_ref[...] = jnp.zeros(out_ref.shape, F32)

        self.run(kernel, [jax.ShapeDtypeStruct((8, 128), F32)], (), flops=1e12)

    def here(self, array):
        return lax.optimization_barrier((array, self.token))[0]

    def run(self, kernel, outs, args, specs=None, scratch=(), flops=0):
        n, extra = len(args), self.last
        params = pltpu.CompilerParams(vmem_limit_bytes=LIMIT * 2**20)

        def body(pos, *refs):
            kernel(pos, *refs[:n], *refs[n + len(extra) :])

        unread = [pl.BlockSpec(memory_space=pl.ANY)] * len(extra)
        if specs is None:
            small = [SMEM if a.dtype == jnp.int32 else VMEM for a in args]
            how = {
                "in_specs": [SMEM] + small + unread,
                "out_specs": (VMEM,) * len(outs),
                "scratch_shapes": list(scratch),
            }
        else:
            how = {
                "grid_spec": pltpu.PrefetchScalarGridSpec(
                    num_scalar_prefetch=1,
                    grid=(1,),
                    in_specs=[whole(a) if spec is None else spec for a, spec in zip(args, specs)]
                    + unread,
                    out_specs=tuple(whole(o) for o in outs),
                    scratch_shapes=list(scratch),
                )
            }
        results = pl.pallas_call(
            body,
            out_shape=tuple(outs),
            compiler_params=params,
            cost_estimate=cost(1e11, 1e8),
            **how,
        )(self.pos, *args, *extra)
        self.last = [min(results, key=lambda r: r.size)]
        self.token = self.last[0]
        return results


def whole(a):
    return pl.BlockSpec(a.shape, lambda *_: (0,) * len(a.shape))


def dot(a, b, precision=None):
    return jnp.dot(a, b, precision=precision, preferred_element_type=F32)


def dot_nt(a, b, precision=None):
    return lax.dot_general(
        a, b, (((1,), (1,)), ((), ())), precision=precision, preferred_element_type=F32
    )


def dot_tn(a, b):
    return lax.dot_general(a, b, (((0,), (0,)), ((), ())), preferred_element_type=F32)


def pack_attn_kernel(pos, qkv_ref, out_ref, bqv_ref, bin_ref, a_ref):
    n, cols = qkv_ref.shape
    m = out_ref.shape[0]
    a_ref[:n, :] = qkv_ref[...].astype(F32)
    a_ref[n : n + m, :] = out_ref[:, :cols].astype(F32)
    a_ref[n + m : n + 2 * m, :] = out_ref[:, cols:].astype(F32)
    at = n + 2 * m
    a_ref[at : at + 8, :] = jnp.zeros((8, cols), F32)
    a_ref[at : at + 2, :] = bqv_ref[...]
    for k in range(bin_ref.shape[1] // cols):
        a_ref[at + 2 + k : at + 3 + k, :] = bin_ref[:, k * cols : (k + 1) * cols]


def eighth_of(w, place):
    return pl.BlockSpec((w.shape[0] // 8, w.shape[1]), lambda i, pos: (pos[place], 0))


def pack_attn(line, qkv, w_out, b_qv, b_in, place):
    rows = qkv.shape[0] // 8 + w_out.shape[0] // 4 + 8
    specs = [eighth_of(qkv, place), eighth_of(w_out, place), None, None]
    outs = [shape((rows, qkv.shape[1]))]
    return line.run(pack_attn_kernel, outs, (qkv, w_out, b_qv, b_in), specs)[0]


def pack_in_kernel(pos, in_ref, b_ref):
    r, wide = in_ref.shape[0], b_ref.shape[1]
    b_ref[:r, :] = in_ref[:, :wide].astype(F32)
    b_ref[r:, :] = in_ref[:, wide:].astype(F32)


def pack_in(line, w, place):
    outs = [shape((w.shape[0] // 4, w.shape[1] // 2))]
    return line.run(pack_in_kernel, outs, (w,), [eighth_of(w, place)])[0]


def pack_down_kernel(pos, down_ref, c_ref):
    c_ref[...] = down_ref[...].astype(F32)


def pack_down(line, w, place):
    outs = [shape((w.shape[0] // 8, w.shape[1]))]
    return line.run(pack_down_kernel, outs, (w,), [eighth_of(w, place)])[0]


def unpack_attn_kernel(order, pos, *refs):
    qkv_ref, out_ref, bqv_ref, bin_ref = refs[-4:]
    n, m = qkv_ref.shape[0] // 8, out_ref.shape[0] // 8
    cols = qkv_ref.shape[1]
    for r, ref, at in pieces(order, refs[:-4], n + 2 * m + 8):
        place = r ^ pos[2]
        to = pl.ds(pl.multiple_of(place * n, 16), n)
        qkv_ref[to, :] = ref[at : at + n, :].astype(BF16)
        to = pl.ds(pl.multiple_of(place * m, 16), m)
        out_ref[to, :cols] = ref[at + n : at + n + m, :].astype(BF16)
        out_ref[to, cols:] = ref[at + n + m : at + n + 2 * m, :].astype(BF16)
    first = refs[0]
    at = n + 2 * m
    bqv_ref[...] = first[at : at + 2, :]
    for k in range(bin_ref.shape[1] // cols):
        bin_ref[:, k * cols : (k + 1) * cols] = first[at + 2 + k : at + 3 + k, :]


def unpack_in_kernel(order, pos, *refs):
    in_ref = refs[-1]
    n = in_ref.shape[0] // 8
    wide = in_ref.shape[1] // 2
    for r, ref, at in pieces(order, refs[:-1], 2 * n):
        to = pl.ds(pl.multiple_of((r ^ pos[2]) * n, 16), n)
        in_ref[to, :wide] = ref[at : at + n, :].astype(BF16)
        in_ref[to, wide:] = ref[at + n : at + 2 * n, :].astype(BF16)


def unpack_down_kernel(order, pos, *refs):
    down_ref = refs[-1]
    m = down_ref.shape[0] // 8
    for r, ref, at in pieces(order, refs[:-1], m):
        to = pl.ds(pl.multiple_of((r ^ pos[2]) * m, 16), m)
        down_ref[to, :] = ref[at : at + m, :].astype(BF16)


class Pieces:
    def __init__(self, line):
        self.line = line
        self.parts, self.order = [], []

    def add(self, arrays, order):
        arrays = [self.line.here(a) for a in arrays]
        both = arrays[0] if len(arrays) == 1 else jnp.concatenate(arrays)
        self.line.after(both)
        self.parts = self.parts + [both, across(both, bit_mask(CORE))]
        self.order = self.order + order + [r | CORE for r in order]


def pieces(order, refs, rows):
    at = 0
    for ref in refs:
        for k in range(ref.shape[0] // rows):
            yield order[at], ref, k * rows
            at += 1


def place_kernel(pos, mine_ref, theirs_ref, out_ref):
    rows = mine_ref.shape[0]
    at = pl.multiple_of(pos[0] * rows, rows)
    out_ref[pl.ds(at, rows), :] = mine_ref[...].astype(out_ref.dtype)
    at = pl.multiple_of((1 - pos[0]) * rows, rows)
    out_ref[pl.ds(at, rows), :] = theirs_ref[...].astype(out_ref.dtype)


def place(line, mine, theirs, dtype):
    rows, width = mine.shape
    return line.run(place_kernel, [shape((2 * rows, width), dtype)], (mine, theirs))[0]


def row_order(bits):
    order = []
    for p in range(BLOCKS):
        r = 0
        for k, bit in enumerate(bits):
            if (p >> (len(bits) - 1 - k)) & 1:
                r |= bit
        order.append(r)
    return order


def store_relative(a, me, scratch, *places):
    scratch[...] = a.T
    for bits, out_ref in places:
        n = out_ref.shape[0] // BLOCKS
        for p, r in enumerate(row_order(bits)):
            at = pl.multiple_of((r ^ me) * n, 16)
            out_ref[p * n : (p + 1) * n, :] = scratch[pl.ds(at, n), :]


def own_rows(pos, ref):
    rows = ref.shape[0] // 2
    return ref[pl.ds(pl.multiple_of(pos[0] * rows, 16), rows), :]


def summed(terms):
    result = terms[0]
    for t in terms[1:]:
        result = result + t
    return result


class Arrival:
    def __init__(self, line, array):
        self.line, self.array, self.waited = line, array, False

    def get(self):
        if not self.waited:
            self.array, self.waited = self.line.here(self.array), True
        return self.array


class Chunk:
    def __init__(self, line, keep, send):
        self.line, self.terms = line, [keep]
        self.n, self.cols = keep.shape[1], keep.shape[2]
        self.heads = keep.shape[0]
        self.sent = send
        self.pending = None

    def start(self):
        sent = across(self.line.here(self.sent), bit_mask(CORE))
        self.pending = (Arrival(self.line, sent), 0)

    def take(self):
        if self.pending:
            arrival, at = self.pending
            self.terms = self.terms + [arrival.get()[:, :, at : at + self.cols]]
            self.pending = None

    def give(self, what):
        self.take()
        if what == HALF:
            half = self.n // 2
            piece = summed([t[: self.heads, half : self.n] for t in self.terms])
            self.n = half
        elif what == OTHER:
            piece = summed([t[1:2, : self.n] for t in self.terms])
            self.heads = 1
        else:
            piece = summed([t[:1, : self.n] for t in self.terms])
        return piece

    def result(self, *more):
        return summed([t[0, : self.n] for t in [*self.terms, *more]])


def exchange(line, move, what, *chunks):
    pieces = [c.give(what) for c in chunks]
    sent = pieces[0] if len(pieces) == 1 else jnp.concatenate(pieces, 2)
    line.after(sent)
    arrival = Arrival(line, move(sent))
    at = 0
    for c in chunks:
        c.pending = (arrival, at)
        at += c.cols
    return arrival


def over(bit):
    return lambda v: across(v, bit_mask(bit))


def groups_of(rest):
    return [[g * rest + k for k in range(rest)] for g in range(BLOCKS)]


def last_rows(v):
    rest = lax.axis_size("batch") // BLOCKS
    if rest == 1:
        return v
    groups = groups_of(rest)
    return lax.psum_scatter(v, "batch", scatter_dimension=0, axis_index_groups=groups, tiled=True)


def norm(v):
    centre = v - jnp.mean(v, -1, keepdims=True)
    inverse = lax.rsqrt(jnp.mean(centre * centre, -1, keepdims=True) + EPS)
    return centre * inverse, inverse


def norm_back(grad, normed, inverse, gain):
    scaled = grad * gain
    return inverse * (
        scaled
        - jnp.mean(scaled, -1, keepdims=True)
        - normed * jnp.mean(scaled * normed, -1, keepdims=True)
    )


def column_sum(v):
    return jnp.sum(v, 0, keepdims=True)


def head_masks():
    lane = lax.broadcasted_iota(jnp.int32, (1, PAIR), 1)
    first = jnp.where(lane < HEAD_DIM, 1.0, 0.0)
    return lane < HEAD_DIM, (first.astype(BF16), (1.0 - first).astype(BF16))


def both_heads(a, masks):
    return jnp.concatenate([a * mask for mask in masks])


def attend(x, w_ref, b_ref, wo_ref, q_ref, k_ref, v_ref, ctx_ref):
    q_ref[...] = (dot(x, w_ref[0]) + b_ref[0:1, :]).astype(BF16)
    k_ref[...] = dot(x, w_ref[1]).astype(BF16)
    v_ref[...] = (dot(x, w_ref[2]) + b_ref[1:2, :]).astype(BF16)
    is_first, masks = head_masks()
    for s in range(q_ref.shape[0] // SEQ):
        at = slice(s * SEQ, (s + 1) * SEQ)
        for p in range(q_ref.shape[1] // PAIR):
            lanes = slice(p * PAIR, (p + 1) * PAIR)
            q, k, v = q_ref[at, lanes] * SCALE, k_ref[at, lanes], v_ref[at, lanes]
            scores = dot_nt(both_heads(q, masks), k)
            e = jnp.exp(scores - jnp.max(scores, -1, keepdims=True))
            probs = (e * (1.0 / jnp.sum(e, -1, keepdims=True))).astype(BF16)
            context = dot(probs, v)
            ctx_ref[at, lanes] = jnp.where(is_first, context[:SEQ], context[SEQ:]).astype(BF16)
    return dot(ctx_ref[...], wo_ref[...])


def attend_own_kernel(pos, x_ref, w_ref, b_ref, wo_ref, q_ref, k_ref, v_ref, ctx_ref, part_ref, *refs):
    *rel_refs, scratch = refs
    x = own_rows(pos, x_ref)
    store_relative(x, pos[1], scratch, *zip(orders_of("q1", "q2"), rel_refs))
    part_ref[...] = attend(x, w_ref, b_ref, wo_ref, q_ref, k_ref, v_ref, ctx_ref)


def attend_other_kernel(
    pos,
    x_ref,
    w_ref,
    b_ref,
    wo_ref,
    part_ref,
    bias_ref,
    gain_ref,
    shift_ref,
    down_ref,
    q_ref,
    k_ref,
    v_ref,
    ctx_ref,
    mixed_ref,
    base_ref,
    low_ref,
    *refs,
):
    *rel_refs, scratch = refs
    x = own_rows(pos, x_ref)
    part = attend(x, w_ref, b_ref, wo_ref, q_ref, k_ref, v_ref, ctx_ref)
    mixed = x.astype(F32) + (part_ref[...] + part) + bias_ref[...]
    mixed_ref[...] = mixed
    first = norm(mixed)[0] * gain_ref[...] + shift_ref[...]
    base_ref[...] = first + down_ref[...]
    low = first.astype(BF16)
    low_ref[...] = low
    store_relative(low, pos[1], scratch, *zip(orders_of("i1", "i2"), rel_refs))


def lift(low, w_in_ref, b_ref, act_ref, slope_ref, block):
    for i in range(act_ref.shape[1] // block):
        at = slice(i * block, (i + 1) * block)
        inner = dot(low, w_in_ref[:, at]) + b_ref[:, at]
        cdf = 0.5 + 0.5 * lax.erf(inner * 0.5**0.5)
        density = jnp.exp(-0.5 * inner * inner) * 0.3989422804014327
        act_ref[:, at] = (inner * cdf).astype(BF16)
        slope_ref[:, at] = cdf + inner * density


def up_kernel(block, pos, low_ref, w_in_ref, b_ref, w_down_ref, before_ref, act_ref, slope_ref, sum_ref):
    lift(low_ref[...], w_in_ref, b_ref, act_ref, slope_ref, block)
    sum_ref[...] = before_ref[...] + dot(act_ref[...], w_down_ref[...])


def up_in_kernel(block, pos, low_ref, w_in_ref, b_ref, act_ref, slope_ref):
    lift(low_ref[...], w_in_ref, b_ref, act_ref, slope_ref, block)


def up_down_kernel(pos, act_ref, w_down_ref, before_ref, sum_ref):
    sum_ref[...] = before_ref[...] + dot(act_ref[...], w_down_ref[...])


def loss_kernel(
    pos,
    pre_ref,
    answers,
    valid,
    gain_f,
    shift_f,
    span_ref,
    ret_ref,
    query_ref,
    second_ref,
    marks_ref,
    stats_ref,
):
    second = norm(pre_ref[...])[0] * gain_f[...] + shift_f[...]
    second_ref[...] = second
    q_row = query_ref[pl.ds(pos[3], 1), :]
    row = lax.broadcasted_iota(jnp.int32, (SEQ, 1), 0)
    line = lax.broadcasted_iota(jnp.int32, (8, 128), 0)
    lane = lax.broadcasted_iota(jnp.int32, (8, 128), 1)
    stats = jnp.full((8, 128), FLOOR, F32)
    slots = second.shape[0] // SEQ
    for s in range(slots):
        slot = pos[0] * slots + s
        mine = second[s * SEQ : (s + 1) * SEQ, :]
        span = jnp.zeros((1, 1), F32)
        for c in range(2):
            logits = jnp.sum(mine * span_ref[c : c + 1, :], -1, keepdims=True)
            shifted = logits - jnp.max(logits, 0, keepdims=True)
            log_probs = shifted - jnp.log(jnp.sum(jnp.exp(shifted), 0, keepdims=True))
            mark = jnp.where(row == answers[slot, c], 1.0, 0.0)
            span = span + jnp.sum(log_probs * mark, 0, keepdims=True)
            marks_ref[s * SEQ : (s + 1) * SEQ, c : c + 1] = mark - jnp.exp(log_probs)
        embed = dot(mine[:8, :], ret_ref[...], HIGHEST)[0:1, :]
        retrieval = jnp.sum(embed * q_row, -1, keepdims=True)
        live = valid[slot] > 0
        joint = jnp.where(live, retrieval + span, FLOOR)
        prior = jnp.where(live, retrieval, FLOOR)
        stats = jnp.where((line == s) & (lane == 0), joint, stats)
        stats = jnp.where((line == s) & (lane == 1), prior, stats)
    stats_ref[...] = stats


def loss_back_kernel(n_stats, pos, cot_ref, *refs):
    stats_refs = refs[:n_stats]
    (
        second_ref,
        pre_ref,
        marks_ref,
        gain_f,
        span_ref,
        ret_ref,
        query_ref,
        sum_ref,
        low_ref,
        sent_ref,
        ret_out,
        small_ref,
        mll_ref,
        *rel_refs,
        scratch,
        leads,
    ) = refs[n_stats:]
    all_stats = [ref[...] for ref in stats_refs]
    peak = jnp.max(functools.reduce(jnp.maximum, all_stats), 0, keepdims=True)
    total = jnp.sum(summed([jnp.exp(t - peak) for t in all_stats]), 0, keepdims=True)
    lse = peak + jnp.log(total)
    weight = jnp.exp(all_stats[0] - lse)
    q_row = query_ref[pl.ds(pos[3], 1), :]
    lead_grad = dot_nt(jnp.broadcast_to(q_row, (8, q_row.shape[1])), ret_ref[...], HIGHEST)
    top = lax.broadcasted_iota(jnp.int32, (8, 1), 0) == 0
    rows = cot_ref.shape[0] // 2
    slots = rows // SEQ
    small_ref[...] = jnp.zeros(small_ref.shape, F32)
    embeds = []
    for s in range(slots):
        at = slice(s * SEQ, (s + 1) * SEQ)
        post = weight[s : s + 1, 0:1]
        prior = weight[s : s + 1, 1:2]
        second = second_ref[at, :]
        sent_ref[at, :] = second
        start = pl.multiple_of(pos[0] * rows + s * SEQ, 16)
        grad = cot_ref[pl.ds(start, SEQ), :].astype(F32)
        for c in range(2):
            d_logits = -post * marks_ref[at, c : c + 1]
            grad = grad + d_logits * span_ref[c : c + 1, :]
            small_ref[3 + c : 4 + c, :] += column_sum(second * d_logits)
        sum_ref[at, :] = grad
        sum_ref[s * SEQ : s * SEQ + 8, :] += jnp.where(top, (prior - post) * lead_grad, 0.0)
        small_ref[5 + s : 6 + s, :] = second[0:1, :]
        embeds.append((prior - post) * q_row)
    leads[...] = small_ref[...].T
    n = ret_out.shape[0] // BLOCKS
    for p, r in enumerate(row_order(rows_of("d1"))):
        block = leads[pl.ds(pl.multiple_of((r ^ pos[1]) * n, 8), n), :]
        ret_out[p * n : (p + 1) * n, :] = summed(
            [block[:, 5 + s : 6 + s] * embed for s, embed in enumerate(embeds)]
        )
    grad = sum_ref[...]
    normed, inverse = norm(pre_ref[...])
    small_ref[0:1, :] = column_sum(grad * normed)
    small_ref[1:2, :] = column_sum(grad)
    d_sum = norm_back(grad, normed, inverse, gain_f[...])
    small_ref[2:3, :] = column_sum(d_sum)
    sum_ref[...] = d_sum
    low = d_sum.astype(BF16)
    low_ref[...] = low
    store_relative(low, pos[1], scratch, *zip(orders_of("d1", "d2"), rel_refs))
    lane = lax.broadcasted_iota(jnp.int32, mll_ref.shape, 1)
    mll = lse[:, 0:1] - lse[:, 1:2]
    mll_ref[...] = jnp.where(lane == pos[4], mll, 0.0)


def halves(left_ref, right, keep_ref, send_ref, index):
    half = left_ref.shape[0] // 2
    keep_ref[index] = dot(left_ref[:half, :], right)
    send_ref[index] = dot(left_ref[half:, :], right)


def product_kernel(start, block, pos, left_ref, own_ref, other_ref, *refs):
    *more, keep_ref, send_ref = refs
    at = slice(start, start + block)
    half = keep_ref.shape[1]
    for h, ref in enumerate((own_ref, other_ref)):
        halves(left_ref, ref[:, at], keep_ref, send_ref, (h, slice(None), slice(0, block)))
        for extra in more:
            keep_ref[h, :, block:] = extra[:half, :]
            send_ref[h, :, block:] = extra[half:, :]


def product(line, left, own, other, start, block, *more):
    width = left.shape[0]
    outs = [shape((2, width // 2, block + sum(m.shape[1] for m in more)))] * 2
    kernel = functools.partial(product_kernel, start, block)
    return line.run(kernel, outs, (left, own, other, *more))


def down_back_kernel(
    start,
    block,
    pos,
    low_ref,
    rel_ref,
    wd1_ref,
    wd2_ref,
    wi1_ref,
    wi2_ref,
    slope1_ref,
    slope2_ref,
    before_ref,
    keep_ref,
    send_ref,
    sum_ref,
    bias_ref,
    d_ref,
):
    low = low_ref[...]
    total = before_ref[...]
    count = keep_ref.shape[2]
    for h, (wd_ref, wi_ref, slope_ref) in enumerate(
        ((wd1_ref, wi1_ref, slope1_ref), (wd2_ref, wi2_ref, slope2_ref))
    ):
        for i in range(count // block):
            to = slice(i * block, (i + 1) * block)
            at = slice(start + i * block, start + (i + 1) * block)
            d_inner = (dot_nt(low, wd_ref[at, :]) * slope_ref[:, at]).astype(BF16)
            d_ref[:, to] = d_inner
            bias_ref[h : h + 1, to] = column_sum(d_inner.astype(F32))
            halves(rel_ref, d_inner, keep_ref, send_ref, (h, slice(None), to))
        total = total + dot_nt(d_ref[...], wi_ref[:, start : start + count])
    sum_ref[...] = total


def down_back(line, start, count, low, rel, w_down, w_in, slope, before):
    rows, width = low.shape
    block = count // 3
    return line.run(
        functools.partial(down_back_kernel, start, block),
        [
            shape((2, width // 2, count)),
            shape((2, width // 2, count)),
            shape((rows, width)),
            shape((2, count)),
        ],
        (low, rel, *w_down, *w_in, *slope, before),
        scratch=[pltpu.VMEM((rows, count), BF16)],
    )


def mixed_back_kernel(
    pos, part_ref, mixed_ref, gain_ref, mix_ref, low_ref, small_ref, *refs
):
    *rel_refs, scratch = refs
    grad = part_ref[...]
    normed, inverse = norm(mixed_ref[...])
    small_ref[...] = jnp.zeros(small_ref.shape, F32)
    small_ref[1:2, :] = column_sum(grad * normed)
    small_ref[2:3, :] = column_sum(grad)
    d_mixed = norm_back(grad, normed, inverse, gain_ref[...])
    small_ref[0:1, :] = column_sum(d_mixed)
    mix_ref[...] = d_mixed
    low = d_mixed.astype(BF16)
    low_ref[...] = low
    store_relative(low, pos[1], scratch, *zip(orders_of("q1", "q2"), rel_refs))


def head_back(pos, lanes, at, q_ref, k_ref, v_ref, dc, store):
    is_first, masks = head_masks()
    q, k, v = (r[at, lanes] for r in (q_ref, k_ref, v_ref))
    q_low, k_low = q * SCALE, k * SCALE
    k_two = both_heads(k_low, masks)
    scores = dot_nt(k_two, q)
    d_probs = dot_nt(both_heads(v, masks), dc)
    probs_two, d_scores_two = [], []
    for h in range(2):
        rows = slice(h * SEQ, (h + 1) * SEQ)
        e = jnp.exp(scores[rows] - jnp.max(scores[rows], 0, keepdims=True))
        probs = e * (1.0 / jnp.sum(e, 0, keepdims=True))
        centre = jnp.sum(d_probs[rows] * probs, 0, keepdims=True)
        d_scores_two.append((probs * (d_probs[rows] - centre)).astype(BF16))
        probs_two.append(probs.astype(BF16))
    d_scores = jnp.concatenate(d_scores_two)
    d_v = dot(jnp.concatenate(probs_two), dc)
    d_k = dot(d_scores, q_low)
    store(0, dot_tn(d_scores, k_two).astype(BF16))
    store(1, jnp.where(is_first, d_k[:SEQ], d_k[SEQ:]).astype(BF16))
    store(2, jnp.where(is_first, d_v[:SEQ], d_v[SEQ:]).astype(BF16))


def attend_back_kernel(pairs, more, pos, *refs):
    heads = (refs[0:6], refs[6:12])
    low_ref, low_rel_ref, rel_ref, before_ref = refs[12:16]
    keep_ref, send_ref, sum_ref, bias_ref, d_ref, dc_ref = refs[16 + more : 22 + more]
    start, count = pairs[0] * PAIR, len(pairs) * PAIR
    ours = slice(start, start + count)
    total = before_ref[...]
    for h, (q_ref, k_ref, v_ref, ctx_ref, w_ref, wo_ref) in enumerate(heads):
        dc_ref[...] = dot_nt(low_ref[...], wo_ref[ours, :]).astype(BF16)
        for s in range(q_ref.shape[0] // SEQ):
            at = slice(s * SEQ, (s + 1) * SEQ)
            for p in range(len(pairs)):
                lanes = slice(start + p * PAIR, start + (p + 1) * PAIR)

                def store(c, d, at=at, p=p):
                    d_ref[at, c * count + p * PAIR : c * count + (p + 1) * PAIR] = d

                dc = dc_ref[at, p * PAIR : (p + 1) * PAIR]
                head_back(pos, lanes, at, q_ref, k_ref, v_ref, dc, store)
        d = d_ref[...]
        bias_ref[h : h + 1, :count] = column_sum(d[:, :count].astype(F32))
        bias_ref[h : h + 1, count:] = column_sum(d[:, 2 * count :].astype(F32))
        halves(rel_ref, d, keep_ref, send_ref, (h, slice(None), slice(0, 3 * count)))
        context = ctx_ref[:, ours]
        halves(low_rel_ref, context, keep_ref, send_ref, (h, slice(None), slice(3 * count, 4 * count)))
        for c in range(3):
            total = total + dot_nt(d[:, c * count : (c + 1) * count], w_ref[c][:, ours])
    sum_ref[...] = total


def attend_back_last_kernel(bits, pairs, pos, *refs):
    more = 6
    attend_back_kernel(pairs, more, pos, *refs)
    a_ref, f_ref, bin1_ref, bin2_ref, mll_ref, before_ref = refs[16 : 16 + more]
    keep_ref, send_ref, _, bias_ref = refs[16 + more : 20 + more]
    blocks = refs[-1]
    last, count = len(pairs) * PAIR, before_ref.shape[1] // 2
    vectors = jnp.concatenate([a_ref[0:3, :], f_ref[2:3, :], f_ref[0:2, :], f_ref[3:5, :]])
    n = vectors.shape[1] // BLOCKS
    half = keep_ref.shape[1]
    order = row_order(bits)
    blocks[...] = jnp.zeros(blocks.shape, F32)
    for h in range(2):
        b_in = jnp.concatenate([bin1_ref[h : h + 1, :], bin2_ref[h : h + 1, :]], 1)
        b_q = jnp.concatenate([before_ref[h : h + 1, :count], bias_ref[h : h + 1, :last]], 1)
        b_v = jnp.concatenate([before_ref[h : h + 1, count:], bias_ref[h : h + 1, last:]], 1)
        for b in range(BLOCKS):
            blocks[b, 0:8, :n] = vectors[:, b * n : (b + 1) * n]
            blocks[b, 9:10, :] = mll_ref[...]
            for k, v in ((8, b_in), (10, b_q), (11, b_v)):
                few = v.shape[1] // BLOCKS
                blocks[b, k : k + 1, :few] = v[:, b * few : (b + 1) * few]
        for ref, first in ((keep_ref, 0), (send_ref, BLOCKS // 2)):
            ref[h, :, 4 * last :] = jnp.zeros((half, 128), F32)
            for p in range(BLOCKS // 2):
                ref[h, p * n : p * n + 16, 4 * last :] = blocks[order[first + p] ^ pos[1]]


def attend_back(line, kernel, count, extra, heads, shared, small=(), scratch=()):
    rows, width = shared[-1].shape
    sent = shape((2, width // 2, 4 * count + extra))
    scratch = [pltpu.VMEM((rows, 3 * count), BF16), pltpu.VMEM((rows, count), BF16), *scratch]
    outs = [sent, sent, shape((rows, width)), shape((2, 2 * count))]
    return line.run(kernel, outs, (*heads, *shared, *small), scratch=scratch)


def on_device(
    hidden_in,
    cotangent,
    valid,
    answers,
    query_embed,
    w_qkv,
    b_qv,
    w_out,
    b_out,
    gain_attn,
    shift_attn,
    w_in,
    b_in,
    w_down,
    b_down,
    gain_ffn,
    shift_ffn,
    w_ret,
    w_span,
):
    here = lax.axis_index("batch")
    y = lax.axis_index("mp")
    devices = lax.axis_size("batch")
    me = here // (devices // BLOCKS)
    width = hidden_in.shape[1]
    rows = hidden_in.shape[0] // 2
    slots = rows // SEQ
    per_query = SLOTS // (2 * slots)
    n_queries = query_embed.shape[0]
    cols = w_qkv.shape[2]
    hidden = w_in.shape[1]
    query = here // per_query
    told = jnp.where((y == 0) & (here % per_query == 0), query, -1)
    pos = jnp.stack([y, me, me & 7, query, told, here, (me & 7) ^ (X | Z0)]).astype(jnp.int32)
    line = Line(pos)
    block = hidden // 3

    def row(v):
        return v.reshape(1, -1)

    rel = shape((width, rows), BF16)
    low_shape = shape((rows, width), BF16)
    full = shape((rows, width))
    turn = [pltpu.VMEM((width, rows), BF16)]

    qkv_flat = w_qkv.reshape(-1, cols)
    b_in_row = row(b_in)
    heads = [shape((rows, cols), BF16)] * 4
    a0 = over_y(pack_attn(line, qkv_flat, w_out, b_qv, b_in_row, 2))
    ad = over_y(pack_attn(line, qkv_flat, w_out, b_qv, b_in_row, 6))
    q1, k1, v1, ctx1, part, *x_rel = line.run(
        attend_own_kernel, heads + [full] + [rel] * len(orders_of("q1", "q2")), (hidden_in, w_qkv, b_qv, w_out), scratch=turn
    )
    f0 = over_y(pack_in(line, w_in, 2))
    line.post()
    a0 = line.here(a0)
    ax, az = across(a0, bit_mask(X)), across(a0, bit_mask(Z0))
    g0 = over_y(pack_down(line, w_down, 2))
    fd = over_y(pack_in(line, w_in, 6))
    gd = over_y(pack_down(line, w_down, 6))
    a = Pieces(line)
    a.add([a0, ad], [0, X | Z0])
    a.add([ax, az], [X, Z0])
    line.post()
    qkv2, w_out2, b_qv2, b_in2 = line.run(
        functools.partial(unpack_attn_kernel, a.order),
        [shape(qkv_flat.shape, BF16), shape(w_out.shape, BF16), shape(b_qv.shape), shape((1, hidden))],
        a.parts,
    )
    w_qkv2 = qkv2.reshape(w_qkv.shape)
    f0 = line.here(f0)
    fx, fz = across(f0, bit_mask(X)), across(f0, bit_mask(Z0))
    line.after(f0)
    line.post()
    q2, k2, v2, ctx2, mixed, base, first_low, *first_rel = line.run(
        attend_other_kernel,
        heads + [full, full, low_shape] + [rel] * len(orders_of("i1", "i2")),
        (
            hidden_in,
            w_qkv2,
            b_qv2,
            w_out2,
            part,
            row(b_out),
            row(gain_attn),
            row(shift_attn),
            row(b_down),
        ),
        scratch=turn,
    )
    act_shapes = [shape((rows, hidden), BF16), shape((rows, hidden))]
    act1, slope1, pre = line.run(
        functools.partial(up_kernel, block),
        act_shapes + [full],
        (first_low, w_in, b_in_row, w_down, base),
    )
    g0 = line.here(g0)
    line.after(g0)
    gx, gz = across(g0, bit_mask(X)), across(g0, bit_mask(Z0))
    f = Pieces(line)
    f.add([f0, fx, fz], [0, X, Z0])
    f.add([fd], [X | Z0])
    line.post()
    (w_in2,) = line.run(
        functools.partial(unpack_in_kernel, f.order), [shape(w_in.shape, BF16)], f.parts
    )
    act2, slope2 = line.run(
        functools.partial(up_in_kernel, block), act_shapes, (first_low, w_in2, b_in2)
    )
    g = Pieces(line)
    g.add([g0, gx], [0, X])
    g.add([gz, gd], [Z0, X | Z0])
    line.post()
    (w_down2,) = line.run(
        functools.partial(unpack_down_kernel, g.order), [shape(w_down.shape, BF16)], g.parts
    )
    (pre,) = line.run(up_down_kernel, [full], (act2, w_down2, pre))
    span_rows = w_span.T
    second, marks, stats = line.run(
        loss_kernel,
        [full, shape((rows, 2)), shape((8, 128))],
        (pre, answers, valid, row(gain_ffn), row(shift_ffn), span_rows, w_ret, query_embed),
    )

    all_stats = [stats, over_y(stats)]
    mask = 1
    while mask < per_query:
        all_stats = all_stats + [across(t, mask) for t in all_stats]
        mask *= 2
    d_sum, d_ffn, second_sent, ret_rel, small_f, mll_row, *d_ffn_rel = line.run(
        functools.partial(loss_back_kernel, len(all_stats)),
        [
            full,
            low_shape,
            full,
            shape((width, w_ret.shape[1])),
            shape((8, width)),
            shape((1, 128)),
        ]
        + [rel] * len(orders_of("d1", "d2")),
        (cotangent, *all_stats, second, pre, marks, row(gain_ffn), span_rows, w_ret, query_embed),
        scratch=turn + [pltpu.VMEM((width, 8), F32)],
    )
    line.post()

    half = hidden // 2
    both = (w_down, w_down2), (w_in, w_in2), (slope1, slope2)
    two_heads = (q1, k1, v1, ctx1, w_qkv, w_out, q2, k2, v2, ctx2, w_qkv2, w_out2)
    pairs = tuple(range(cols // PAIR))
    x_rel = dict(zip(orders_of("q1", "q2"), x_rel))
    first_rel = dict(zip(orders_of("i1", "i2"), first_rel))
    d_ffn_rel = dict(zip(orders_of("d1", "d2"), d_ffn_rel))
    chunks = {}
    gone = dict.fromkeys(ROUTES, 0)
    for step in PLAN:
        if step == "post":
            line.post()
        elif step == "D1":
            sent = product(line, d_ffn_rel[rows_of("d1")], act1, act2, 0, half, ret_rel)
            chunks["d1"] = Chunk(line, *sent)
        elif step == "D2":
            sent = product(line, d_ffn_rel[rows_of("d2")], act1, act2, half, half)
            chunks["d2"] = Chunk(line, *sent)
        elif step == "I1":
            *sent, part, b_in1 = down_back(line, 0, half, d_ffn, first_rel[rows_of("i1")], *both, d_sum)
            chunks["i1"] = Chunk(line, *sent)
        elif step == "I2":
            *sent, part, b_in2 = down_back(line, half, half, d_ffn, first_rel[rows_of("i2")], *both, part)
            chunks["i2"] = Chunk(line, *sent)
        elif step == "M":
            d_mixed, d_att, small_a, *d_att_rel = line.run(
                mixed_back_kernel,
                [full, low_shape, shape((8, width))] + [rel] * len(x_rel),
                (part, mixed, row(gain_attn)),
                scratch=turn,
            )
            d_att_rel = dict(zip(x_rel, d_att_rel))
        elif step == "Q1":
            rows1 = rows_of("q1")
            *sent, part, bias = attend_back(
                line,
                functools.partial(attend_back_kernel, pairs[:-1], 0),
                cols - PAIR,
                0,
                two_heads,
                (d_att, d_att_rel[rows1], x_rel[rows1], d_mixed),
            )
            chunks["q1"] = Chunk(line, *sent)
        elif step == "Q2":
            rows2 = rows_of("q2")
            *sent, g_in, _ = attend_back(
                line,
                functools.partial(attend_back_last_kernel, rows2, pairs[-1:]),
                PAIR,
                128,
                two_heads,
                (d_att, d_att_rel[rows2], x_rel[rows2], part),
                (small_a, small_f, b_in1, b_in2, mll_row, bias),
                [pltpu.VMEM((BLOCKS, 16, 128), F32)],
            )
            chunks["q2"] = Chunk(line, *sent)
        elif step.startswith("t"):
            chunks[step[1:]].take()
            line.after(chunks[step[1:]].terms[-1])
        elif step.startswith("c"):
            chunks[step[1:]].start()
        elif step == "l":
            second_theirs = over_y(second_sent)
        elif step == "L":
            second_theirs = line.here(second_theirs)
            line.after(second_theirs)
        elif step == "place":
            layer_out = place(line, second, second_theirs, BF16)
        elif step == "g":
            grad_theirs = over_y(line.here(g_in))
        elif step == "G":
            grad_in = place(line, g_in, line.here(grad_theirs), F32)
        else:
            axis = ROUTES[step][gone[step]]
            gone[step] += 1
            if axis == Y:
                exchange(line, over_y, OTHER, chunks[step])
            else:
                exchange(line, over(axis), HALF, chunks[step])
    d1, d2, i1, i2, q1, q2 = chunks.values()
    for chunk in (i1, d1, d2, i2):
        chunk.take()
    g_in1 = jnp.concatenate([i1.result(), i2.result()], 1)
    g_down1, g_down2 = d1.result(), d2.result()
    line.last = []
    q2.take()
    q1.take()
    g_q, g_q2 = q1.result(), q2.result()

    rest = devices // BLOCKS
    misc = g_q2[:, 4 * PAIR :]
    if rest > 1:
        misc = lax.psum(misc, "batch", axis_index_groups=groups_of(rest))

    def mine(line_number, total):
        few = total // devices
        values = misc[line_number, : total // BLOCKS]
        return values if rest == 1 else lax.dynamic_slice_in_dim(values, here % rest * few, few, 0)

    vectors = [mine(k, width) for k in range(8)]
    n = cols - PAIR

    def joined(c):
        parts = [g_q[:, c * n : (c + 1) * n], g_q2[:, c * PAIR : (c + 1) * PAIR]]
        return last_rows(jnp.concatenate(parts, 1))

    g_down = jnp.concatenate([last_rows(g_down1[:, :half]).T, last_rows(g_down2).T])
    return (
        misc[9, :n_queries],
        layer_out,
        grad_in,
        jnp.stack([joined(c) for c in range(3)]),
        jnp.stack([mine(10, cols), mine(11, cols)]),
        joined(3).T,
        vectors[0],
        vectors[1],
        vectors[2],
        last_rows(g_in1),
        mine(8, hidden),
        g_down,
        vectors[3],
        vectors[4],
        vectors[5],
        last_rows(g_down1[:, half:]),
        jnp.stack(vectors[6:8], 1),
    )


def solution(mesh):
    return jax.shard_map(
        on_device,
        mesh=mesh,
        in_specs=(
            P("batch", None),
            P("batch", None),
            P("batch"),
            P("batch", None),
            P(),
            P(None, None, "mp"),
            P(None, "mp"),
            P("mp", None),
            P(),
            P(),
            P(),
            P(None, "mp"),
            P("mp"),
            P("mp", None),
            P(),
            P(),
            P(),
            P(),
            P(),
        ),
        out_specs=(
            P(),
            P("batch", None),
            P("batch", None),
            P(None, "batch", "mp"),
            P(None, ("mp", "batch")),
            P("mp", "batch"),
            P("batch"),
            P("batch"),
            P("batch"),
            P("batch", "mp"),
            P(("mp", "batch")),
            P("mp", "batch"),
            P("batch"),
            P("batch"),
            P("batch"),
            P("batch", None),
            P("batch", None),
        ),
        check_vma=False,
    )
```
